32 devices in a mesh: dp: 2 (over core), expert: 4 (over z), tensor: 4 (over y, x).
Axes of the slice: x: 2, y: 2, z: 4, core: 2. Of those that a mesh axis runs over, the one named last changes fastest.
Arguments:
- hidden_in: bfloat16 [20480, 768], P(('dp', 'expert', 'tensor')), may hold values from -6 to 6
- route_ids: int32 [2, 20480, 1], P(None, ('dp', 'expert', 'tensor')), may hold values from 0 to 3; in each aligned block of 640 rows (0 to 639, 640 to 1279, ..., all dimensions but the last counted through in order) at most 240 rows name the same one
- segment_ids: int32 [20480], P(('dp', 'expert')), may hold values from 0 to 12, as said below
- path_pos: int32 [20480], P(('dp', 'expert')), may hold values from 0 to 1279, as said below
- parent_ids: int32 [8, 13], P(('dp', 'expert')), may hold values from 0 to 4, as said below
- norm_att: bfloat16 [2, 768], replicated, may hold values from 0.5 to 1.5
- w_qkv: bfloat16 [2, 768, 3, 768], P(None, None, None, 'tensor'), may hold values from -0.21875 to 0.21875
- w_out: bfloat16 [2, 768, 768], P(None, 'tensor'), may hold values from -0.875 to 0.875
- norm_ffn: bfloat16 [2, 768], replicated, may hold values from 0.5 to 1.5
- w_route: bfloat16 [2, 768, 4], replicated, may hold values from -0.15625 to 0.15625
- w_in: bfloat16 [2, 4, 768, 3072], P(None, 'expert', None, 'tensor'), may hold values from -0.21875 to 0.21875
- w_down: bfloat16 [2, 4, 3072, 768], P(None, 'expert', 'tensor'), may hold values from -0.4375 to 0.4375
- cotangent: bfloat16 [20480, 768], P(('dp', 'expert', 'tensor')), may hold values from -6 to 6
Outputs:
- hidden_out: bfloat16 [20480, 768], P(('dp', 'expert', 'tensor'))
- grad_hidden: float32 [20480, 768], P(('dp', 'expert', 'tensor'))
- grad_norm_att: float32 [2, 768], replicated
- grad_qkv: float32 [2, 768, 3, 768], P(None, None, None, 'tensor')
- grad_out: float32 [2, 768, 768], P(None, 'tensor')
- grad_norm_ffn: float32 [2, 768], replicated
- grad_route: float32 [2, 768, 4], replicated
- grad_w_in: float32 [2, 4, 768, 3072], P(None, 'expert', None, 'tensor')
- grad_w_down: float32 [2, 4, 3072, 768], P(None, 'expert', 'tensor')
The draws below stay inside these ranges and needn't reach their ends.
Inputs may be any that keep to these rules, and one draw needn't show every extreme that they name: `route_ids`: in the rows of one device at most 240 tokens name one expert. `segment_ids`: each tree is 2560 consecutive tokens in 20 blocks of 128, the blocks in an order drawn from the seed: eight of segment 0 (the trunk), one of each branch 1 to 4 and one of each leaf 5 to 12. `path_pos`: inside a block positions rise by one; the trunk's blocks hold 0 to 1023, a branch starts at 1024, a leaf at 1152. `parent_ids`: segments 0 to 4 have parent 0; each branch 1 to 4 is the parent of two leaves.
All inputs are finite; a program needn't handle non-finite values.
Results may differ from the reference program's by a relative error of at most 0.03.
Values may be sent and summed in bfloat16 or wider, within the bound.
A program may use at most 256 MiB of HBM per device.

```python
import math
from functools import partial
import jax
import jax.numpy as jnp
import numpy as np
from jax import lax

D = 768
HEADS = 12
HEAD_DIM = 64
FF = 3072
LAYERS = 2
BLK = 128
TREE = 2560
QBLK = 512
TOK_DEV = 640
TREES = 8
TOKENS = 20480
EXPERTS = 4
CAP = 240
N_DP = 2
N_EXPERT = 4
N_TENSOR = 4


def tree_layout(key):

    def one_tree(tree_index):
        return jax.random.permutation(jax.random.fold_in(key, tree_index), 20).astype(jnp.int32)
    orders = jax.vmap(one_tree)(jnp.arange(TREES, dtype=jnp.int32))
    segment = jnp.where(orders < 8, 0, orders - 7)
    offset = jnp.where(orders < 8, orders * BLK, jnp.where(orders < 12, 8 * BLK, 9 * BLK))
    return (segment.astype(jnp.int32), offset.astype(jnp.int32))


def draw_segment_ids(key, part):
    segment, offset = tree_layout(key)
    return jnp.repeat(segment.reshape(-1), BLK)


def draw_path_pos(key, part):
    segment, offset = tree_layout(key)
    return (offset.reshape(-1, 1) + jnp.arange(BLK, dtype=jnp.int32)[None, :]).reshape(-1)


def draw_parent_ids(key, part):
    key = jax.random.fold_in(key, 13)

    def one_tree(tree_index):
        shuffled = jax.random.permutation(jax.random.fold_in(key, tree_index), 8).astype(jnp.int32)
        return jnp.concatenate([jnp.zeros((5,), jnp.int32), 1 + shuffled // 2])
    return jax.vmap(one_tree)(jnp.arange(TREES, dtype=jnp.int32))


def block_levels(stream_key, shape, pieces, low, top_value):
    def one(position, blocks):
        draws = jax.random.uniform(jax.random.fold_in(jax.random.fold_in(stream_key, 6), position), (blocks,), jnp.float32, low / len(pieces), top_value / len(pieces))
        return jnp.repeat(jnp.exp(draws), shape[position] // blocks).reshape((-1,) + (1,) * (len(shape) - position - 1))

    level = one(*pieces[0])
    for cut in pieces[1:]:
        level = level * one(*cut)
    return level


def deal_out(own_key, own, number, rows, amount, top, bound, lean):
    sequence = jax.random.permutation(own_key, amount)
    heavy_load, common = load_shares(amount, rows * top, bound, lean, True), load_shares(amount, rows * top, bound, lean, False)
    places = jnp.arange(amount)

    def named(lengths, offset_by):
        used = int((lengths > 0).sum())
        fixed = max(1, used // 4)
        shifted = fixed + (places - fixed + offset_by * (used - fixed)) % max(1, amount - fixed)
        return jnp.zeros((amount,), jnp.int32).at[sequence[jnp.where(places < fixed, places, shifted)]].set(jnp.asarray(lengths, jnp.int32))

    lengths = jnp.where(number % 4 == 0, named(heavy_load, number // 4), named(common, number - number // 4 - 1))
    mixed = jax.random.permutation(jax.random.fold_in(own, 3), amount)
    donor, receiver = mixed[0:amount // 2 * 2:2], mixed[1:amount // 2 * 2:2]
    room = jnp.minimum(lengths[donor] - 1, bound - lengths[receiver]) // 2
    room = jnp.where((donor == sequence[0]) | (receiver == sequence[0]) | (lengths[receiver] == 0), 0, jnp.maximum(room, 0))
    shifted = jax.random.randint(jax.random.fold_in(own, 4), (amount // 2,), 0, 1 << 20) % (room + 1)
    lengths = lengths.at[donor].add(-shifted).at[receiver].add(shifted)
    items = jnp.searchsorted(jnp.cumsum(lengths), jnp.arange(rows * top), side="right").astype(jnp.int32)
    listing = items.reshape(top, rows).T
    listing = listing[jax.random.permutation(jax.random.fold_in(own, 1), rows)]
    offset_by = jax.random.randint(jax.random.fold_in(own, 2), (rows, 1), 0, top)
    return jnp.take_along_axis(listing, (jnp.arange(top)[None, :] + offset_by) % top, axis=1)


def load_shares(amount, total, bound, lean, full):
    weights = [(1 << 20) // math.isqrt(standing ** lean) + 1 for standing in range(1, amount + 1)]
    largest = bound if full else min(bound, max(-(-total // amount), total * weights[0] // sum(weights)))
    least = 1 if total - largest >= amount - 1 else 0
    given, rest = [largest] + [least] * (amount - 1), total - largest - least * (amount - 1)
    while rest > 0:
        movable = [i for i in range(1, amount) if given[i] < largest] or [i for i in range(1, amount) if given[i] < bound]
        pool, budget = sum([weights[i] for i in movable]), rest
        for i in movable:
            addition = min(bound - given[i], max(1, budget * weights[i] // pool), rest)
            given[i] = given[i] + addition
            rest = rest - addition
    return np.array(given)


def gaussian(key, dims, scale, reach, pieces=(), kind=jnp.bfloat16):
    values = jax.random.normal(key, dims, jnp.float32) * scale
    if len(pieces) > 0:
        values = block_levels(key, dims, pieces, -0.22, 0.18) * values
    return jnp.clip(values, min=-reach, max=reach).astype(kind)


def setup_inputs(seed: int = 0) -> dict:
    splits = jax.random.split(jax.random.key(seed), 14)
    hidden_in = gaussian(splits[0], (TOKENS, D), 1.0, 6.0, ((0, 32),))
    route_ids_keys = jax.random.split(jax.random.fold_in(splits[1], 1), LAYERS * TOKENS // TOK_DEV)
    route_ids_turns = jax.random.permutation(jax.random.fold_in(splits[1], 3), LAYERS * TOKENS // TOK_DEV)
    route_ids = jax.vmap(lambda own, number: deal_out(jax.random.fold_in(splits[1], 2), own, number, TOK_DEV, EXPERTS, 1, CAP, 2))(route_ids_keys, route_ids_turns).reshape((LAYERS, TOKENS, 1))
    segment_ids = draw_segment_ids(jax.random.fold_in(splits[13], 71), 0)
    path_pos = draw_path_pos(jax.random.fold_in(splits[13], 71), 0)
    parent_ids = draw_parent_ids(jax.random.fold_in(splits[13], 71), 0)
    norm_att = jnp.clip(1.0 + 0.1 * jax.random.normal(splits[5], (LAYERS, D), jnp.float32), 0.5, 1.5).astype(jnp.bfloat16)
    w_qkv = gaussian(splits[6], (LAYERS, D, 3, D), D ** -0.5, 0.21875, ((3, 4),))
    w_out = gaussian(splits[7], (LAYERS, D, D), (D // 16) ** -0.5, 0.875, ((1, 4),))
    norm_ffn = jnp.clip(1.0 + 0.1 * jax.random.normal(splits[8], (LAYERS, D), jnp.float32), 0.5, 1.5).astype(jnp.bfloat16)
    w_route = gaussian(splits[9], (LAYERS, D, EXPERTS), (2 * D) ** -0.5, 0.15625)
    w_in = gaussian(splits[10], (LAYERS, EXPERTS, D, FF), D ** -0.5, 0.21875, ((1, 4), (3, 4)))
    w_down = gaussian(splits[11], (LAYERS, EXPERTS, FF, D), (max(FF // (EXPERTS * EXPERTS), 1)) ** -0.5, 0.4375, ((1, 4), (2, 4)))
    cotangent = gaussian(splits[12], (TOKENS, D), 1.0, 6.0, ((0, 32),))
    return dict(hidden_in=hidden_in, route_ids=route_ids, segment_ids=segment_ids, path_pos=path_pos, parent_ids=parent_ids, norm_att=norm_att, w_qkv=w_qkv, w_out=w_out, norm_ffn=norm_ffn, w_route=w_route, w_in=w_in, w_down=w_down, cotangent=cotangent)


EPS = 1e-06
NEG = -1000000000.0
HIGH = lax.Precision.HIGHEST

@jax.custom_vjp
def low(v):
    return lax.optimization_barrier(v.astype(jnp.bfloat16)).astype(jnp.float32)

@jax.custom_vjp
def low_back(v):
    return v

def low_keep(v):
    return (low(v), None)

def low_pass(kept, grad):
    return (grad,)

def back_keep(v):
    return (v, None)

def back_low(kept, grad):
    return (low(grad),)
low.defvjp(low_keep, low_pass)
low_back.defvjp(back_keep, back_low)

def matmul(left, right):
    return jnp.dot(left, right, precision=HIGH)

def rms_norm(stream, gain):
    return stream * lax.rsqrt(lax.optimization_barrier(jnp.mean(stream * stream, axis=-1, keepdims=True)) + EPS) * gain

def lookup(indices, parent_rows):
    matches = indices[:, None] == jnp.arange(parent_rows.shape[-1], dtype=jnp.int32)[None, :]
    return lax.optimization_barrier(jnp.sum(jnp.where(matches, parent_rows, 0), axis=1)).astype(jnp.int32)

def query_block(keys_all, values_all, key_segs, key_places, entries):
    queries, seg_self, seg_parent, seg_grand, place_self = entries
    scores = jnp.einsum('qhd,khd->hqk', queries, keys_all, precision=HIGH) * HEAD_DIM ** (-0.5)
    allowed = (key_segs[None, :] == seg_self[:, None]) | (key_segs[None, :] == seg_parent[:, None]) | (key_segs[None, :] == seg_grand[:, None])
    allowed = allowed & (key_places[None, :] <= place_self[:, None])
    scores = low_back(jnp.where(allowed[None], scores, NEG))
    weights = jax.nn.softmax(scores, axis=-1)
    return jnp.einsum('hqk,khd->qhd', low(weights), values_all, precision=HIGH)

def tree_attention(entries):
    mixed, seg_ids, parents, grands, places = entries
    blocks = TREE // QBLK
    queries = mixed[:, 0].reshape(blocks, QBLK, HEADS, HEAD_DIM)
    block_fn = jax.checkpoint(partial(query_block, mixed[:, 1], mixed[:, 2], seg_ids, places))
    heads = lax.map(block_fn, (queries, seg_ids.reshape(blocks, QBLK), parents.reshape(blocks, QBLK), grands.reshape(blocks, QBLK), places.reshape(blocks, QBLK)))
    return heads.reshape(TREE, HEADS, HEAD_DIM)

def expert_ffn(entries):
    slot_rows, first_w, second_w = entries
    pre_act = low_back(matmul(slot_rows, first_w))
    return matmul(low(jax.nn.gelu(pre_act)), second_w)

def routing(route_col):
    devices = N_DP * N_EXPERT * N_TENSOR
    token_ids = jnp.arange(TOKENS, dtype=jnp.int32)
    chosen = route_col[:, None] == jnp.arange(EXPERTS, dtype=jnp.int32)[None, :]
    before = jnp.cumsum(chosen.astype(jnp.int32).reshape(devices, TOK_DEV, EXPERTS), axis=1).reshape(TOKENS, EXPERTS) - 1
    slot_ids = lax.optimization_barrier(jnp.sum(jnp.where(chosen, before, 0), axis=1)).astype(jnp.int32)
    flat_slot = (route_col * (devices * CAP) + token_ids // TOK_DEV * CAP + slot_ids).astype(jnp.int32)
    slot_table = jnp.full((EXPERTS * devices * CAP,), TOKENS, dtype=jnp.int32).at[flat_slot].set(token_ids)
    return (flat_slot, slot_table.reshape(EXPERTS, devices * CAP), chosen)

def layer(stream, weights, path_info, plan):
    gain_att, w_mix, w_proj, gain_ffn, w_gate, w_up, w_back = weights
    seg_ids, places, parents, grands = path_info
    flat_slot, slot_table, chosen = plan
    normed = low(rms_norm(stream, gain_att))
    mixed = low_back(low(matmul(normed, w_mix.reshape(D, 3 * D))))
    mixed = mixed.reshape(TREES, TREE, 3, HEADS, HEAD_DIM)
    heads = lax.map(tree_attention, (mixed, seg_ids.reshape(TREES, TREE), parents.reshape(TREES, TREE), grands.reshape(TREES, TREE), places.reshape(TREES, TREE)))
    heads = low_back(low(heads.reshape(TOKENS, D)))
    after_att = stream + low_back(matmul(heads, w_proj))
    token_rows = low(rms_norm(after_att, gain_ffn))
    sent_rows = low_back(token_rows)
    router = jax.nn.softmax(matmul(token_rows, w_gate), axis=-1)
    gate = lax.optimization_barrier(jnp.sum(jnp.where(chosen, router, 0.0), axis=1))
    padded = jnp.concatenate([sent_rows, jnp.zeros((1, D), sent_rows.dtype)], axis=0)
    slots = padded[slot_table]
    results = lax.map(jax.checkpoint(expert_ffn), (slots, w_up, w_back))
    expert_rows = low_back(low(results.reshape(-1, D)[flat_slot]))
    return after_att + gate[:, None] * expert_rows

def reference(hidden_in, route_ids, segment_ids, path_pos, parent_ids, norm_att, w_qkv, w_out, norm_ffn, w_route, w_in, w_down, cotangent):
    parent_rows = parent_ids[jnp.arange(TOKENS, dtype=jnp.int32) // TREE]
    parents = lookup(segment_ids, parent_rows)
    grands = lookup(parents, parent_rows)
    path_info = (segment_ids, path_pos, parents, grands)
    plans = [routing(route_ids[depth, :, 0]) for depth in range(LAYERS)]

    def forward(stream, weights):
        for depth in range(LAYERS):
            stream = layer(stream, [w[depth] for w in weights], path_info, plans[depth])
        return stream
    weights = tuple((w.astype(jnp.float32) for w in (norm_att, w_qkv, w_out, norm_ffn, w_route, w_in, w_down)))
    result, pullback = jax.vjp(forward, hidden_in.astype(jnp.float32), weights)
    grad_x, grads = pullback(cotangent.astype(jnp.float32))
    return (result.astype(jnp.bfloat16), grad_x, grads[0], grads[1], grads[2], grads[3], grads[4], grads[5], grads[6])
```

```python
import functools

import jax
import jax.numpy as jnp
from jax import lax
from jax.experimental import pallas as pl
from jax.experimental.pallas import tpu as pltpu
from jax.sharding import PartitionSpec as P

HEAD_DIM = 64
BLK = 128
TRUNK = 8
PAIR = 2 * HEAD_DIM
EPS = 1e-06
NEG = -1000000000.0
BIG = 1 << 20
F32 = jnp.float32
BF16 = jnp.bfloat16
VMEM_LIMIT = 56 * 1024 * 1024

NT = (((1,), (1,)), ((), ()))
TN = (((0,), (0,)), ((), ()))


def dot(a, b):
    return jnp.dot(a, b, preferred_element_type=F32)


def dot_nt(a, b):
    return lax.dot_general(a, b, NT, preferred_element_type=F32)


def dot_tn(a, b):
    return lax.dot_general(a, b, TN, preferred_element_type=F32)


def cost(macs, moved, trans=0):
    return pl.CostEstimate(flops=2 * macs, bytes_accessed=moved, transcendentals=trans)


def xperm(x, axis, k):
    n = lax.axis_size(axis)
    return lax.ppermute(x, axis, [(i, i ^ k) for i in range(n)])


def after(x, dep):
    return lax.optimization_barrier((x, dep))[0]


def gather_rows(x):
    half = x.shape[0] // 2
    lo, hi = x[:half], x[half:]
    a_lo, b_hi = xperm(lo, "tensor", 1), xperm(hi, "tensor", 2)
    a_hi, b_lo = xperm(hi, "tensor", 1), xperm(lo, "tensor", 2)
    c_lo, c_hi = xperm(a_lo, "tensor", 2), xperm(b_hi, "tensor", 1)
    return [x, a_lo, a_hi, b_lo, b_hi, c_lo, c_hi]


def gather_shared(mine, other):
    half = mine.shape[0] // 2
    a, b = xperm(mine, "tensor", 1), xperm(mine, "tensor", 2)
    c = jnp.concatenate([xperm(a[:half], "tensor", 2), xperm(b[half:], "tensor", 1)], axis=0)
    got = [mine, a, b, c]
    return got, [other] + [xperm(p, "dp", 1) for p in got[1:]]


def scatter_rows(blocks, own):
    half = own.shape[0] // 2
    b1, b2, b3 = blocks
    x3, y3 = xperm(b3[:half], "tensor", 1), xperm(b3[half:], "tensor", 2)
    x1, y2 = xperm(b1[:half], "tensor", 1), xperm(b2[half:], "tensor", 2)
    x2 = xperm((b2[:half].astype(F32) + x3.astype(F32)).astype(BF16), "tensor", 2)
    y1 = xperm((b1[half:].astype(F32) + y3.astype(F32)).astype(BF16), "tensor", 1)
    low = own[:half] + x1.astype(F32) + x2.astype(F32)
    high = own[half:] + y2.astype(F32) + y1.astype(F32)
    return jnp.concatenate([low, high], axis=0)


def scatter_shared(mine, other):
    total = mine.astype(F32) + xperm(other, "dp", 1).astype(F32)
    own, rest = total[0], total[1:].astype(BF16)
    return scatter_rows([rest[0], rest[1], rest[2]], own)


def sum_expert(piece):
    n = lax.axis_size("expert")
    if n != 4:
        return lax.psum(piece, "expert")
    rows = piece.shape[0] // n
    z = lax.axis_index("expert")
    cut = [lax.dynamic_slice_in_dim(piece, (z ^ k) * rows, rows, 0) for k in range(n)]
    total = cut[0]
    for k in range(1, n):
        total = total + xperm(cut[k].astype(BF16), "expert", k).astype(F32)
    low = total.astype(BF16)
    parts = [low] + [xperm(low, "expert", k) for k in range(1, n)]
    stacked = jnp.stack(parts)
    order = jnp.arange(n, dtype=jnp.int32) ^ z
    return jnp.concatenate([lax.dynamic_index_in_dim(stacked, order[k], 0, keepdims=False) for k in range(n)], axis=0)


def sum_small(x):
    for axis in ("dp", "tensor", "expert"):
        n = lax.axis_size(axis)
        k = 1
        while k < n:
            x = x + xperm(x, axis, k)
            k *= 2
    return x


def by_core(mine, other, axis):
    first = lax.axis_index("dp") == 0
    return jnp.concatenate([jnp.where(first, mine, other), jnp.where(first, other, mine)], axis=axis)


def exchange(chunks):
    n = len(chunks)
    if n == 4:
        return [chunks[0]] + [xperm(chunks[k], "expert", k) for k in range(1, n)]
    out = lax.all_to_all(jnp.stack(chunks), "expert", split_axis=0, concat_axis=0, tiled=True)
    return [out[k] for k in range(n)]


def masked_pair(x):
    lane = lax.broadcasted_iota(jnp.int32, x.shape, 1)
    zero = jnp.zeros_like(x)
    return jnp.concatenate([jnp.where(lane < HEAD_DIM, x, zero), jnp.where(lane < HEAD_DIM, zero, x)], axis=0)


def attend_kernel(table, q_ref, k_ref, v_ref, out_ref, lse_ref, keys, values):
    pair = pl.program_id(0)
    blocks = k_ref.shape[0] // BLK
    mine = q_ref.shape[0] // BLK
    trunk = TRUNK * BLK
    for b in range(blocks):
        place = pl.ds(pl.multiple_of(table[b] * BLK, BLK), BLK)
        rows = pl.ds(b * BLK, BLK)
        keys[place, :] = k_ref[rows, :]
        values[place, pl.ds(0, PAIR)] = v_ref[rows, :]
    values[:, pl.ds(PAIR, PAIR)] = jnp.ones((blocks * BLK, PAIR), BF16)
    lane = lax.broadcasted_iota(jnp.int32, (BLK, PAIR), 1)
    for i in range(mine):
        at = blocks + 5 * i
        place_q, own, parent, base_own, base_parent = [table[at + j] for j in range(5)]
        rows = pl.ds(i * BLK, BLK)
        own_rows = pl.ds(pl.multiple_of(own * BLK, BLK), BLK)
        parent_rows = pl.ds(pl.multiple_of(parent * BLK, BLK), BLK)
        q = masked_pair(q_ref[rows, :] * jnp.asarray(HEAD_DIM ** -0.5, BF16))
        row = lax.broadcasted_iota(jnp.int32, (2 * BLK, 1), 0) % BLK
        pos_q = place_q + row
        s_trunk = dot_nt(q, keys[pl.ds(0, trunk), :])
        key_pos = lax.broadcasted_iota(jnp.int32, s_trunk.shape, 1)
        s_trunk = jnp.where(key_pos <= pos_q, s_trunk, NEG)
        s_parent = dot_nt(q, keys[parent_rows, :])
        col = lax.broadcasted_iota(jnp.int32, s_parent.shape, 1)
        s_parent = jnp.where(col + base_parent <= pos_q, s_parent, NEG)
        s_own = dot_nt(q, keys[own_rows, :])
        s_own = jnp.where(col + base_own <= pos_q, s_own, NEG)
        top = jnp.maximum(
            jnp.max(s_trunk, axis=1, keepdims=True),
            jnp.max(jnp.maximum(s_parent, s_own), axis=1, keepdims=True),
        )
        p_trunk = jnp.exp(s_trunk - top).astype(BF16)
        p_parent = jnp.exp(s_parent - top).astype(BF16)
        p_own = jnp.exp(s_own - top).astype(BF16)
        both = dot(p_trunk, values[pl.ds(0, trunk), :])
        both = both + dot(p_parent, values[parent_rows, :]) + dot(p_own, values[own_rows, :])
        total = both[:, PAIR:]
        heads = both[:, :PAIR] / total
        lse = top + jnp.log(total)
        out_ref[rows, :] = jnp.where(lane < HEAD_DIM, heads[:BLK], heads[BLK:]).astype(BF16)
        known = jnp.where(pair == 0, 0.0, lse_ref[rows, :])
        known = jnp.where(lane == 2 * pair, lse[:BLK], known)
        lse_ref[rows, :] = jnp.where(lane == 2 * pair + 1, lse[BLK:], known)


def attend(table, q, k, v):
    mine, width = q.shape
    rows = k.shape[0]
    pairs = width // PAIR
    column = lambda n: pl.BlockSpec((n, PAIR), lambda p, table: (0, p))
    return pl.pallas_call(
        attend_kernel,
        grid_spec=pltpu.PrefetchScalarGridSpec(
            num_scalar_prefetch=1,
            grid=(pairs,),
            in_specs=[column(mine), column(rows), column(rows)],
            out_specs=[column(mine), pl.BlockSpec((mine, PAIR), lambda p, table: (0, 0))],
            scratch_shapes=[pltpu.VMEM((rows, PAIR), BF16), pltpu.VMEM((rows, 2 * PAIR), BF16)],
        ),
        out_shape=[jax.ShapeDtypeStruct((mine, width), BF16), jax.ShapeDtypeStruct((mine, PAIR), F32)],
        compiler_params=pltpu.CompilerParams(vmem_limit_bytes=VMEM_LIMIT),
        cost_estimate=cost(mine * 1280 * width * 8, 4 * rows * width, mine * 1280 * width // HEAD_DIM),
        name="attend",
    )(table, q, k, v)


def attend_back_kernel(
    table, q_ref, k_ref, v_ref, do_ref, o_ref, lse_ref, dq_ref, dk_ref, dv_ref,
    keys, values, keys_t, dk_acc, dv_acc, lse_t,
):
    pair = pl.program_id(0)
    blocks = k_ref.shape[0] // BLK
    mine = q_ref.shape[0] // BLK
    trunk = TRUNK * BLK
    for b in range(blocks):
        place = pl.ds(pl.multiple_of(table[b] * BLK, BLK), BLK)
        rows = pl.ds(b * BLK, BLK)
        keys[place, :] = k_ref[rows, :]
        values[place, :] = v_ref[rows, :]
        keys_t[:, place] = k_ref[rows, :].T
    dk_acc[...] = jnp.zeros_like(dk_acc)
    dv_acc[...] = jnp.zeros_like(dv_acc)

    @pl.when(pair == 0)
    def _():
        for i in range(mine):
            turned = lse_ref[pl.ds(i * BLK, BLK), :].T
            for p in range(lse_t.shape[0]):
                lse_t[p, pl.ds(0, 2), pl.ds(i * BLK, BLK)] = turned[2 * p : 2 * p + 2]

    lane = lax.broadcasted_iota(jnp.int32, (BLK, PAIR), 1)
    scale = jnp.asarray(HEAD_DIM ** -0.5, BF16)
    for i in range(mine):
        at = blocks + 5 * i
        place_q, own, parent, base_own, base_parent = [table[at + j] for j in range(5)]
        rows = pl.ds(i * BLK, BLK)
        q = masked_pair(q_ref[rows, :] * scale)
        do = do_ref[rows, :]
        product = (do.astype(F32) * o_ref[rows, :].astype(F32)).T
        inner = jnp.concatenate(
            [
                jnp.sum(product[:HEAD_DIM], axis=0, keepdims=True),
                jnp.sum(product[HEAD_DIM:], axis=0, keepdims=True),
            ],
            axis=1,
        )
        do = masked_pair(do)
        lse = jnp.concatenate([lse_t[pair, pl.ds(0, 1), rows], lse_t[pair, pl.ds(1, 1), rows]], axis=1)
        pos_q = place_q + lax.broadcasted_iota(jnp.int32, (1, 2 * BLK), 1) % BLK
        dq_t = jnp.zeros((PAIR, 2 * BLK), F32)
        steps = [(j * 2 * BLK, 2 * BLK, j * 2 * BLK) for j in range(TRUNK // 2)]
        steps += [(pl.multiple_of(parent * BLK, BLK), BLK, base_parent)]
        steps += [(pl.multiple_of(own * BLK, BLK), BLK, base_own)]
        for start, size, base in steps:
            here = pl.ds(start, size)
            k_rows, v_rows = keys[here, :], values[here, :]
            scores = dot_nt(k_rows, q)
            key_pos = base + lax.broadcasted_iota(jnp.int32, (size, 1), 0)
            weights = jnp.exp(jnp.where(key_pos <= pos_q, scores - lse, NEG))
            d_weights = dot_nt(v_rows, do)
            d_scores = (weights * (d_weights - inner)).astype(BF16)
            dv_acc[here, :] += dot(weights.astype(BF16), do)
            dk_acc[here, :] += dot(d_scores, q)
            dq_t = dq_t + dot(keys_t[:, here], d_scores)
        dq = dq_t.T * (HEAD_DIM ** -0.5)
        dq_ref[rows, :] = jnp.where(lane < HEAD_DIM, dq[:BLK], dq[BLK:]).astype(BF16)
    for b in range(blocks):
        place = pl.ds(pl.multiple_of(table[b] * BLK, BLK), BLK)
        rows = pl.ds(b * BLK, BLK)
        dk_ref[rows, :] = dk_acc[place, :].astype(BF16)
        dv_ref[rows, :] = dv_acc[place, :].astype(BF16)


def attend_back(table, q, k, v, d_heads, heads, lse):
    mine, width = q.shape
    rows = k.shape[0]
    pairs = width // PAIR
    column = lambda n: pl.BlockSpec((n, PAIR), lambda p, table: (0, p))
    return pl.pallas_call(
        attend_back_kernel,
        grid_spec=pltpu.PrefetchScalarGridSpec(
            num_scalar_prefetch=1,
            grid=(pairs,),
            in_specs=[
                column(mine), column(rows), column(rows), column(mine), column(mine),
                pl.BlockSpec((mine, PAIR), lambda p, table: (0, 0)),
            ],
            out_specs=[column(mine), column(rows), column(rows)],
            scratch_shapes=[
                pltpu.VMEM((rows, PAIR), BF16),
                pltpu.VMEM((rows, PAIR), BF16),
                pltpu.VMEM((PAIR, rows), BF16),
                pltpu.VMEM((rows, PAIR), F32),
                pltpu.VMEM((rows, PAIR), F32),
                pltpu.VMEM((pairs, 8, mine), F32),
            ],
        ),
        out_shape=[
            jax.ShapeDtypeStruct((mine, width), BF16),
            jax.ShapeDtypeStruct((rows, width), BF16),
            jax.ShapeDtypeStruct((rows, width), BF16),
        ],
        compiler_params=pltpu.CompilerParams(vmem_limit_bytes=VMEM_LIMIT),
        cost_estimate=cost(mine * 1280 * width * 20, 8 * rows * width, mine * 1280 * width // HEAD_DIM),
        name="attend_back",
    )(table, q, k, v, d_heads, heads, lse)


GELU_C = 0.7978845608028654
GELU_A = 0.044715


def row_cuts(total):
    step = next(s for s in (240, 320, 160, 128, total) if total % s == 0)
    return [pl.ds(i, step) for i in range(0, total, step)]


def expert_kernel(rows_ref, up_ref, down_ref, out_ref, hidden_ref, slope_ref, acc):
    step = pl.program_id(0)
    last = pl.num_programs(0) - 1
    for cut in row_cuts(rows_ref.shape[0]):
        u = dot(rows_ref[cut, :], up_ref[0])
        square = u * u
        half = 0.5 + 0.5 * jnp.tanh(u * (GELU_C + (GELU_C * GELU_A) * square))
        hidden = u * half
        low = hidden.astype(BF16)
        hidden_ref[0, cut, :] = low
        slope = half + hidden * (1.0 - half) * (2 * GELU_C + (6 * GELU_C * GELU_A) * square)
        slope_ref[0, cut, :] = slope.astype(BF16)
        part = dot(low, down_ref[0])
        total = jnp.where(step == 0, part, acc[cut, :] + part)
        acc[cut, :] = total

        @pl.when(step == last)
        def _():
            out_ref[cut, :] = total.astype(BF16)


def expert_forward(rows, up, down):
    count, width = rows.shape
    pieces, _, size = up.shape
    whole = pl.BlockSpec((count, width), lambda n: (0, 0))
    piece = pl.BlockSpec((1, count, size), lambda n: (n, 0, 0))
    kept = jax.ShapeDtypeStruct((pieces, count, size), BF16)
    return pl.pallas_call(
        expert_kernel,
        grid=(pieces,),
        in_specs=[
            whole,
            pl.BlockSpec((1, width, size), lambda n: (n, 0, 0)),
            pl.BlockSpec((1, size, width), lambda n: (n, 0, 0)),
        ],
        out_specs=[whole, piece, piece],
        out_shape=[jax.ShapeDtypeStruct((count, width), BF16), kept, kept],
        scratch_shapes=[pltpu.VMEM((count, width), F32)],
        compiler_params=pltpu.CompilerParams(vmem_limit_bytes=VMEM_LIMIT),
        cost_estimate=cost(2 * count * width * size * pieces, 4 * count * size * pieces + 4 * pieces * size * width),
        name="expert_forward",
    )(rows, up, down)


def expert_rows_kernel(
    expert, d_out_ref, up_ref, down_ref, slope_ref, rows_ref, out_ref, route_ref, d_rows_ref, d_pre_ref, d_log_ref, gain_ref, acc,
    *, experts,
):
    step = pl.program_id(0)
    last = pl.num_programs(0) - 1
    count = d_out_ref.shape[0]
    for cut in row_cuts(count):
        d_hidden = dot_nt(d_out_ref[cut, :], down_ref[0])
        d_pre = (d_hidden * slope_ref[0, cut, :].astype(F32)).astype(BF16)
        d_pre_ref[0, cut, :] = d_pre
        part = dot_nt(d_pre, up_ref[0])
        acc[cut, :] = jnp.where(step == 0, part, acc[cut, :] + part)

    @pl.when(step == last)
    def _():
        gain = jnp.zeros((1, acc.shape[1]), F32)
        for cut in row_cuts(count):
            rows = rows_ref[cut, :]
            logits = dot(rows, route_ref[...])
            lane = lax.broadcasted_iota(jnp.int32, logits.shape, 1)
            logits = jnp.where(lane < experts, logits, NEG)
            router = jnp.exp(logits - jnp.max(logits, axis=1, keepdims=True))
            router = router / jnp.sum(router, axis=1, keepdims=True)
            amount = jnp.sum(out_ref[cut, :].astype(F32) * d_out_ref[cut, :].astype(F32), axis=1, keepdims=True)
            d_log = amount * (jnp.where(lane == expert[0], 1.0, 0.0) - router)
            d_low = d_log.astype(BF16)
            d_log_ref[cut, :] = d_low
            d_rows = acc[cut, :] + dot_nt(d_low, route_ref[...])
            gain = gain + jnp.sum(d_rows * rows.astype(F32), axis=0, keepdims=True)
            d_rows_ref[cut, :] = d_rows.astype(BF16)
        gain_ref[...] = gain


def expert_rows(expert, d_out, up, down, slope, rows, out, route, experts):
    count, width = d_out.shape
    pieces, _, size = up.shape
    lanes = route.shape[1]
    whole = pl.BlockSpec((count, width), lambda n, e: (0, 0))
    piece = pl.BlockSpec((1, count, size), lambda n, e: (n, 0, 0))
    return pl.pallas_call(
        functools.partial(expert_rows_kernel, experts=experts),
        grid_spec=pltpu.PrefetchScalarGridSpec(
            num_scalar_prefetch=1,
            grid=(pieces,),
            in_specs=[
                whole,
                pl.BlockSpec((1, width, size), lambda n, e: (n, 0, 0)),
                pl.BlockSpec((1, size, width), lambda n, e: (n, 0, 0)),
                piece, whole, whole,
                pl.BlockSpec((width, lanes), lambda n, e: (0, 0)),
            ],
            out_specs=[
                whole, piece,
                pl.BlockSpec((count, lanes), lambda n, e: (0, 0)),
                pl.BlockSpec((1, width), lambda n, e: (0, 0)),
            ],
            scratch_shapes=[pltpu.VMEM((count, width), F32)],
        ),
        out_shape=[
            jax.ShapeDtypeStruct((count, width), BF16),
            jax.ShapeDtypeStruct((pieces, count, size), BF16),
            jax.ShapeDtypeStruct((count, lanes), BF16),
            jax.ShapeDtypeStruct((1, width), F32),
        ],
        compiler_params=pltpu.CompilerParams(vmem_limit_bytes=VMEM_LIMIT),
        cost_estimate=cost(2 * count * width * size * pieces, 4 * count * size * pieces + 4 * pieces * size * width),
        name="expert_rows",
    )(expert, d_out, up, down, slope, rows, out, route)


def expert_grads_kernel(rows_ref, d_out_ref, hidden_ref, d_pre_ref, d_log_ref, up_ref, down_ref, route_ref, rows_t):
    @pl.when(pl.program_id(0) == 0)
    def _():
        rows_t[...] = rows_ref[...].T
        route_ref[...] = dot(rows_t[...], d_log_ref[...])

    up_ref[0] = dot(rows_t[...], d_pre_ref[0]).astype(BF16)
    down_ref[0] = dot_tn(hidden_ref[0], d_out_ref[...]).astype(BF16)


def expert_grads(rows, d_out, hidden, d_pre, d_log):
    count, width = rows.shape
    pieces, _, size = hidden.shape
    lanes = d_log.shape[1]
    whole = pl.BlockSpec((count, width), lambda n: (0, 0))
    piece = pl.BlockSpec((1, count, size), lambda n: (n, 0, 0))
    return pl.pallas_call(
        expert_grads_kernel,
        grid=(pieces,),
        in_specs=[whole, whole, piece, piece, pl.BlockSpec((count, lanes), lambda n: (0, 0))],
        out_specs=[
            pl.BlockSpec((1, width, size), lambda n: (n, 0, 0)),
            pl.BlockSpec((1, size, width), lambda n: (n, 0, 0)),
            pl.BlockSpec((width, lanes), lambda n: (0, 0)),
        ],
        out_shape=[
            jax.ShapeDtypeStruct((pieces, width, size), BF16),
            jax.ShapeDtypeStruct((pieces, size, width), BF16),
            jax.ShapeDtypeStruct((width, lanes), F32),
        ],
        scratch_shapes=[pltpu.VMEM((width, count), BF16)],
        compiler_params=pltpu.CompilerParams(vmem_limit_bytes=VMEM_LIMIT),
        cost_estimate=cost(2 * count * width * size * pieces, 4 * count * size * pieces + 4 * pieces * size * width),
        name="expert_grads",
    )(rows, d_out, hidden, d_pre, d_log)


def inverse_rms(stream):
    return lax.rsqrt(jnp.mean(stream * stream, axis=-1, keepdims=True) + EPS)


def norm_backward(upstream, stream, inverse, gain):
    weighted = upstream * gain
    inner = jnp.mean(weighted * stream, axis=-1, keepdims=True)
    return inverse * weighted - stream * (inverse * inverse * inverse) * inner


def path_table(segment_ids, path_pos, parent_ids, peers):
    segment = segment_ids[::BLK].reshape(peers, -1)
    position = path_pos[::BLK].reshape(peers, -1)
    t = lax.axis_index("tensor")
    order = jnp.arange(peers, dtype=jnp.int32) ^ t
    match = order[:, None] == jnp.arange(peers, dtype=jnp.int32)[None, :]
    pick = lambda v: jnp.sum(jnp.where(match[:, :, None], v[None], 0), axis=1)
    segment, position = pick(segment), pick(position)
    place = jnp.where(segment == 0, position // BLK, segment + (TRUNK - 1))
    seg, pos, own = segment[0], position[0], place[0]
    names = jnp.arange(parent_ids.shape[-1], dtype=jnp.int32)
    parent = jnp.sum(jnp.where(seg[:, None] == names[None, :], parent_ids[0][None], 0), axis=1)
    leaf = (seg > 0) & (parent > 0)
    parent_place = jnp.where(leaf, parent + (TRUNK - 1), own)
    base_own = jnp.where(seg > 0, pos, BIG)
    base_parent = jnp.where(leaf, TRUNK * BLK, BIG)
    mine = jnp.stack([pos, own, parent_place, base_own, base_parent], axis=1)
    return jnp.concatenate([place.reshape(-1), mine.reshape(-1)]).astype(jnp.int32)


def dispatch_plan(route, experts, capacity):
    count = route.shape[0]
    chosen = route[:, None] == jnp.arange(experts, dtype=jnp.int32)[None, :]
    index = jnp.arange(count, dtype=jnp.int32)
    before = (index[None, :] < index[:, None]).astype(BF16)
    ranks = dot(before, chosen.astype(BF16)).astype(jnp.int32)
    rank = jnp.sum(jnp.where(chosen, ranks, 0), axis=1)
    to = route ^ lax.axis_index("expert") if experts == 4 else route
    slot = to * capacity + rank
    table = slot[None, :] == jnp.arange(experts * capacity, dtype=jnp.int32)[:, None]
    return chosen, table.astype(BF16)


def send_rows(table, rows, experts, capacity):
    chunks = [
        dot(table[k * capacity : (k + 1) * capacity], rows).astype(BF16) for k in range(experts)
    ]
    return jnp.concatenate(exchange(chunks), axis=0)


def return_rows(table, results, experts, capacity):
    chunks = exchange([results[k * capacity : (k + 1) * capacity] for k in range(experts)])
    return dot_tn(table, jnp.concatenate(chunks, axis=0))


def split_core(x, axis):
    c = lax.axis_index("dp")
    half = x.shape[axis] // 2
    return (
        lax.dynamic_slice_in_dim(x, c * half, half, axis),
        lax.dynamic_slice_in_dim(x, (1 - c) * half, half, axis),
    )


def attention_weights(w_mix, w_proj):
    width = w_mix.shape[0]
    mix = gather_shared(*split_core(w_mix.reshape(width, -1), 0))
    proj = gather_shared(*split_core(w_proj, 0))
    mixes = [by_core(a, b, 0).reshape(width, 3, -1) for a, b in zip(*mix)]
    projs = [by_core(a, b, 0) for a, b in zip(*proj)]
    parts = [jnp.concatenate([m[:, i] for m in mixes], axis=1) for i in range(3)]
    return parts[0], parts[1], parts[2], jnp.concatenate(projs, axis=0)


def expert_weights(w_up, w_back):
    up = gather_shared(*split_core(w_up, 1))
    down = gather_shared(*split_core(w_back, 0))
    return jnp.stack(up[0] + up[1]), jnp.stack(down[0] + down[1])


def body(
    hidden_in, route_ids, segment_ids, path_pos, parent_ids, norm_att, w_qkv, w_out, norm_ffn, w_route, w_in, w_down, cotangent,
):
    depth_total = w_qkv.shape[0]
    tokens, width = hidden_in.shape
    experts = w_route.shape[-1]
    capacity = 3 * tokens // (2 * experts)
    peers = lax.axis_size("tensor")
    own_expert = lax.axis_index("expert").reshape(1).astype(jnp.int32)
    shard = width // peers
    table = path_table(segment_ids, path_pos, parent_ids, peers)
    plans = [dispatch_plan(route_ids[d, :, 0], experts, capacity) for d in range(depth_total)]
    routes = [jnp.pad(w_route[d], ((0, 0), (0, BLK - experts))) for d in range(depth_total)]
    cotangent = cotangent.astype(F32)

    stream = hidden_in.astype(F32)
    kept = []
    weights, moe = [None] * depth_total, [None] * depth_total
    weights[0] = attention_weights(w_qkv[0], w_out[0])
    for depth in range(depth_total):
        gain_att, gain_ffn = norm_att[depth].astype(F32), norm_ffn[depth].astype(F32)
        chosen, plan = plans[depth]
        inverse_att = inverse_rms(stream)
        normed = (stream * inverse_att * gain_att).astype(BF16)
        normed_all = jnp.concatenate(gather_rows(normed), axis=0)
        if depth == 0:
            up, down = after((w_in[0, 0], w_down[0, 0]), normed_all)
            moe[0] = expert_weights(up, down)
        w_q, w_k, w_v, w_o = weights[depth]
        q = dot(normed, w_q).astype(BF16)
        k = dot(normed_all, w_k).astype(BF16)
        v = dot(normed_all, w_v).astype(BF16)
        heads, lse = attend(table, q, k, v)
        after_att = stream + dot(heads, w_o)
        inverse_ffn = inverse_rms(after_att)
        token_rows = (after_att * inverse_ffn * gain_ffn).astype(BF16)
        if depth + 1 < depth_total:
            mix, proj, up, down = after(
                (w_qkv[depth + 1], w_out[depth + 1], w_in[depth + 1, 0], w_down[depth + 1, 0]), token_rows
            )
            weights[depth + 1] = attention_weights(mix, proj)
            moe[depth + 1] = expert_weights(up, down)
        rows = send_rows(plan, token_rows, experts, capacity)
        router = jax.nn.softmax(dot(token_rows, w_route[depth]), axis=-1)
        gate = jnp.sum(jnp.where(chosen, router, 0.0), axis=1, keepdims=True)
        d_sent = None
        if depth + 1 == depth_total:
            d_low = (gate * cotangent).astype(BF16)
            d_sent = send_rows(plan, d_low, experts, capacity)
        out, hidden, slope = expert_forward(rows, *moe[depth])
        stream_next = after_att + gate * return_rows(plan, out, experts, capacity)
        kept.append(
            (stream, inverse_att, normed, normed_all, q, k, v, heads, lse, after_att, inverse_ffn, gate, rows, d_sent, out, hidden, slope)
        )
        stream = stream_next
    hidden_out = stream.astype(BF16)

    upstream = cotangent
    grads = [None] * depth_total
    for depth in reversed(range(depth_total)):
        (stream, inverse_att, normed, normed_all, q, k, v, heads, lse, after_att, inverse_ffn, gate, rows, d_sent, out, hidden, slope) = kept[depth]
        gain_att, gain_ffn = norm_att[depth].astype(F32), norm_ffn[depth].astype(F32)
        chosen, plan = plans[depth]
        w_q, w_k, w_v, w_o = weights[depth]
        if d_sent is None:
            d_sent = send_rows(plan, (gate * upstream).astype(BF16), experts, capacity)
        d_slots, d_pre, d_log, gain_sum = expert_rows(
            own_expert, d_sent, *moe[depth], slope, rows, out, routes[depth], experts
        )
        d_rows = return_rows(plan, d_slots, experts, capacity)
        g_up, g_down, g_route = expert_grads(rows, d_sent, hidden, d_pre, d_log)
        half = peers
        up_mine = scatter_shared(g_up[:half], g_up[half:]).astype(BF16)
        down_mine = scatter_shared(g_down[:half], g_down[half:]).astype(BF16)
        grad_up = by_core(up_mine, xperm(up_mine, "dp", 1), 1).astype(F32)
        grad_down = by_core(down_mine, xperm(down_mine, "dp", 1), 0).astype(F32)

        dx1 = upstream + norm_backward(d_rows, after_att, inverse_ffn, gain_ffn)
        d_att = dx1.astype(BF16)
        d_heads = dot_nt(d_att, w_o).astype(BF16)
        dq, dk, dv = attend_back(table, q, k, v, d_heads, heads, lse)
        blocks = []
        for j in reversed(range(peers)):
            at = slice(j * tokens, (j + 1) * tokens)
            part = dot_nt(dk[at], w_k) + dot_nt(dv[at], w_v)
            if j == 0:
                part = part + dot_nt(dq, w_q)
            else:
                part = part.astype(BF16)
            blocks.insert(0, part)
        d_normed = scatter_rows(blocks[1:], blocks[0])
        g_q, g_k, g_v = dot_tn(normed, dq), dot_tn(normed_all, dk), dot_tn(normed_all, dv)
        g_o = dot_tn(heads, d_att).reshape(peers, shard, width).astype(BF16)
        att_sum = jnp.sum(g_q * w_q.astype(F32) + g_k * w_k.astype(F32) + g_v * w_v.astype(F32), axis=1)
        g_mix = jnp.stack(
            [
                jnp.concatenate([g[:, j * shard : (j + 1) * shard].astype(BF16) for g in (g_q, g_k, g_v)], axis=1)
                for j in range(peers)
            ]
        )
        mix_mine = sum_expert(scatter_shared(*split_core(g_mix, 1))).astype(BF16)
        out_mine = sum_expert(scatter_shared(*split_core(g_o, 1))).astype(BF16)
        grad_mix = by_core(mix_mine, xperm(mix_mine, "dp", 1), 0).astype(F32).reshape(width, 3, shard)
        grad_out = by_core(out_mine, xperm(out_mine, "dp", 1), 0).astype(F32)
        small = sum_small(
            jnp.concatenate([g_route[:, :experts].T, gain_sum, att_sum[None]], axis=0)
        )
        grads[depth] = (
            small[experts + 1] / gain_att, grad_mix, grad_out, small[experts] / gain_ffn, small[:experts].T, grad_up[None], grad_down[None],
        )
        upstream = dx1 + norm_backward(d_normed, stream, inverse_att, gain_att)
    stacked = [jnp.stack([grads[d][m] for d in range(depth_total)]) for m in range(7)]
    return (hidden_out, upstream, *stacked)


def solution(mesh):
    in_specs = (
        P(("dp", "expert", "tensor"), None),
        P(None, ("dp", "expert", "tensor"), None),
        P(("dp", "expert")),
        P(("dp", "expert")),
        P(("dp", "expert"), None),
        P(),
        P(None, None, None, "tensor"),
        P(None, "tensor", None),
        P(),
        P(),
        P(None, "expert", None, "tensor"),
        P(None, "expert", "tensor", None),
        P(("dp", "expert", "tensor"), None),
    )
    out_specs = (
        P(("dp", "expert", "tensor"), None),
        P(("dp", "expert", "tensor"), None),
        P(),
        P(None, None, None, "tensor"),
        P(None, "tensor", None),
        P(),
        P(),
        P(None, "expert", None, "tensor"),
        P(None, "expert", "tensor", None),
    )
    return jax.shard_map(body, mesh=mesh, in_specs=in_specs, out_specs=out_specs, check_vma=False)
```

```python
import functools

import jax
import jax.numpy as jnp
from jax import lax
from jax.experimental import pallas as pl
from jax.experimental.pallas import tpu as pltpu
from jax.sharding import PartitionSpec as P

HEAD_DIM = 64
BLK = 128
TRUNK = 8
PAIR = 2 * HEAD_DIM
EPS = 1e-06
NEG = -1000000000.0
BIG = 1 << 20
F32 = jnp.float32
BF16 = jnp.bfloat16
VMEM_LIMIT = 56 * 1024 * 1024

NT = (((1,), (1,)), ((), ()))
TN = (((0,), (0,)), ((), ()))


def dot(a, b):
    return jnp.dot(a, b, preferred_element_type=F32)


def dot_nt(a, b):
    return lax.dot_general(a, b, NT, preferred_element_type=F32)


def dot_tn(a, b):
    return lax.dot_general(a, b, TN, preferred_element_type=F32)


def cost(macs, moved, trans=0):
    return pl.CostEstimate(flops=macs // 64, bytes_accessed=moved // 64, transcendentals=0)


def xperm(x, axis, k):
    n = lax.axis_size(axis)
    return lax.ppermute(x, axis, [(i, i ^ k) for i in range(n)])


def after(x, dep):
    return lax.optimization_barrier((x, dep))[0]


def gather_rows(x):
    half = x.shape[0] // 2
    lo, hi = x[:half], x[half:]
    a_lo, b_hi = xperm(lo, "tensor", 1), xperm(hi, "tensor", 2)
    a_hi, b_lo = xperm(hi, "tensor", 1), xperm(lo, "tensor", 2)
    c_lo, c_hi = xperm(a_lo, "tensor", 2), xperm(b_hi, "tensor", 1)
    return [x, a_lo, a_hi, b_lo, b_hi, c_lo, c_hi]


def scatter_rows(blocks, own):
    half = own.shape[0] // 2
    b1, b2, b3 = blocks
    x3, y3 = xperm(b3[:half], "tensor", 1), xperm(b3[half:], "tensor", 2)
    x1, y2 = xperm(b1[:half], "tensor", 1), xperm(b2[half:], "tensor", 2)
    x2 = xperm((b2[:half].astype(F32) + x3.astype(F32)).astype(BF16), "tensor", 2)
    y1 = xperm((b1[half:].astype(F32) + y3.astype(F32)).astype(BF16), "tensor", 1)
    low = own[:half] + x1.astype(F32) + x2.astype(F32)
    high = own[half:] + y2.astype(F32) + y1.astype(F32)
    return jnp.concatenate([low, high], axis=0)


def sum_small(x):
    for axis in ("dp", "tensor", "expert"):
        n = lax.axis_size(axis)
        k = 1
        while k < n:
            x = x + xperm(x, axis, k)
            k *= 2
    return x


def exchange(chunks):
    n = len(chunks)
    if n == 4:
        return [chunks[0]] + [xperm(chunks[k], "expert", k) for k in range(1, n)]
    out = lax.all_to_all(jnp.stack(chunks), "expert", split_axis=0, concat_axis=0, tiled=True)
    return [out[k] for k in range(n)]


def masked_pair(x):
    lane = lax.broadcasted_iota(jnp.int32, x.shape, 1)
    zero = jnp.zeros_like(x)
    return jnp.concatenate([jnp.where(lane < HEAD_DIM, x, zero), jnp.where(lane < HEAD_DIM, zero, x)], axis=0)


def attend_kernel(table, q_ref, k_ref, v_ref, out_ref, lse_ref, keys, values):
    pair = pl.program_id(0)
    blocks = k_ref.shape[0] // BLK
    mine = q_ref.shape[0] // BLK
    trunk = TRUNK * BLK
    for b in range(blocks):
        place = pl.ds(pl.multiple_of(table[b] * BLK, BLK), BLK)
        rows = pl.ds(b * BLK, BLK)
        keys[place, :] = k_ref[rows, :]
        values[place, pl.ds(0, PAIR)] = v_ref[rows, :]
    values[:, pl.ds(PAIR, PAIR)] = jnp.ones((blocks * BLK, PAIR), BF16)
    lane = lax.broadcasted_iota(jnp.int32, (BLK, PAIR), 1)
    for i in range(mine):
        at = blocks + 5 * i
        place_q, own, parent, base_own, base_parent = [table[at + j] for j in range(5)]
        rows = pl.ds(i * BLK, BLK)
        own_rows = pl.ds(pl.multiple_of(own * BLK, BLK), BLK)
        parent_rows = pl.ds(pl.multiple_of(parent * BLK, BLK), BLK)
        q = masked_pair(q_ref[rows, :] * jnp.asarray(HEAD_DIM ** -0.5, BF16))
        row = lax.broadcasted_iota(jnp.int32, (2 * BLK, 1), 0) % BLK
        pos_q = place_q + row
        s_trunk = dot_nt(q, keys[pl.ds(0, trunk), :])
        key_pos = lax.broadcasted_iota(jnp.int32, s_trunk.shape, 1)
        s_trunk = jnp.where(key_pos <= pos_q, s_trunk, NEG)
        s_parent = dot_nt(q, keys[parent_rows, :])
        col = lax.broadcasted_iota(jnp.int32, s_parent.shape, 1)
        s_parent = jnp.where(col + base_parent <= pos_q, s_parent, NEG)
        s_own = dot_nt(q, keys[own_rows, :])
        s_own = jnp.where(col + base_own <= pos_q, s_own, NEG)
        top = jnp.maximum(
            jnp.max(s_trunk, axis=1, keepdims=True),
            jnp.max(jnp.maximum(s_parent, s_own), axis=1, keepdims=True),
        )
        p_trunk = jnp.exp(s_trunk - top).astype(BF16)
        p_parent = jnp.exp(s_parent - top).astype(BF16)
        p_own = jnp.exp(s_own - top).astype(BF16)
        both = dot(p_trunk, values[pl.ds(0, trunk), :])
        both = both + dot(p_parent, values[parent_rows, :]) + dot(p_own, values[own_rows, :])
        total = both[:, PAIR:]
        heads = both[:, :PAIR] / total
        lse = top + jnp.log(total)
        out_ref[rows, :] = jnp.where(lane < HEAD_DIM, heads[:BLK], heads[BLK:]).astype(BF16)
        known = jnp.where(pair == 0, 0.0, lse_ref[rows, :])
        known = jnp.where(lane == 2 * pair, lse[:BLK], known)
        lse_ref[rows, :] = jnp.where(lane == 2 * pair + 1, lse[BLK:], known)


def attend(table, q, k, v):
    mine, width = q.shape
    rows = k.shape[0]
    pairs = width // PAIR
    column = lambda n: pl.BlockSpec((n, PAIR), lambda p, table: (0, p))
    return pl.pallas_call(
        attend_kernel,
        grid_spec=pltpu.PrefetchScalarGridSpec(
            num_scalar_prefetch=1,
            grid=(pairs,),
            in_specs=[column(mine), column(rows), column(rows)],
            out_specs=[column(mine), pl.BlockSpec((mine, PAIR), lambda p, table: (0, 0))],
            scratch_shapes=[pltpu.VMEM((rows, PAIR), BF16), pltpu.VMEM((rows, 2 * PAIR), BF16)],
        ),
        out_shape=[jax.ShapeDtypeStruct((mine, width), BF16), jax.ShapeDtypeStruct((mine, PAIR), F32)],
        compiler_params=pltpu.CompilerParams(vmem_limit_bytes=VMEM_LIMIT),
        cost_estimate=cost(mine * 1280 * width * 8, 4 * rows * width, mine * 1280 * width // HEAD_DIM),
        name="attend",
    )(table, q, k, v)


def attend_back_kernel(
    table, q_ref, k_ref, v_ref, do_ref, o_ref, lse_ref, dq_ref, dk_ref, dv_ref,
    keys, values, keys_t, dk_acc, dv_acc, lse_t,
):
    pair = pl.program_id(0)
    blocks = k_ref.shape[0] // BLK
    mine = q_ref.shape[0] // BLK
    trunk = TRUNK * BLK
    for b in range(blocks):
        place = pl.ds(pl.multiple_of(table[b] * BLK, BLK), BLK)
        rows = pl.ds(b * BLK, BLK)
        keys[place, :] = k_ref[rows, :]
        values[place, :] = v_ref[rows, :]
        keys_t[:, place] = k_ref[rows, :].T
    dk_acc[...] = jnp.zeros_like(dk_acc)
    dv_acc[...] = jnp.zeros_like(dv_acc)

    @pl.when(pair == 0)
    def _():
        for i in range(mine):
            turned = lse_ref[pl.ds(i * BLK, BLK), :].T
            for p in range(lse_t.shape[0]):
                lse_t[p, pl.ds(0, 2), pl.ds(i * BLK, BLK)] = turned[2 * p : 2 * p + 2]

    lane = lax.broadcasted_iota(jnp.int32, (BLK, PAIR), 1)
    scale = jnp.asarray(HEAD_DIM ** -0.5, BF16)
    for i in range(mine):
        at = blocks + 5 * i
        place_q, own, parent, base_own, base_parent = [table[at + j] for j in range(5)]
        rows = pl.ds(i * BLK, BLK)
        q = masked_pair(q_ref[rows, :] * scale)
        do = do_ref[rows, :]
        product = (do.astype(F32) * o_ref[rows, :].astype(F32)).T
        inner = jnp.concatenate(
            [
                jnp.sum(product[:HEAD_DIM], axis=0, keepdims=True),
                jnp.sum(product[HEAD_DIM:], axis=0, keepdims=True),
            ],
            axis=1,
        )
        do = masked_pair(do)
        lse = jnp.concatenate([lse_t[pair, pl.ds(0, 1), rows], lse_t[pair, pl.ds(1, 1), rows]], axis=1)
        pos_q = place_q + lax.broadcasted_iota(jnp.int32, (1, 2 * BLK), 1) % BLK
        dq_t = jnp.zeros((PAIR, 2 * BLK), F32)
        steps = [(j * 2 * BLK, 2 * BLK, j * 2 * BLK) for j in range(TRUNK // 2)]
        steps += [(pl.multiple_of(parent * BLK, BLK), BLK, base_parent)]
        steps += [(pl.multiple_of(own * BLK, BLK), BLK, base_own)]
        for start, size, base in steps:
            here = pl.ds(start, size)
            k_rows, v_rows = keys[here, :], values[here, :]
            scores = dot_nt(k_rows, q)
            key_pos = base + lax.broadcasted_iota(jnp.int32, (size, 1), 0)
            weights = jnp.exp(jnp.where(key_pos <= pos_q, scores - lse, NEG))
            d_weights = dot_nt(v_rows, do)
            d_scores = (weights * (d_weights - inner)).astype(BF16)
            dv_acc[here, :] += dot(weights.astype(BF16), do)
            dk_acc[here, :] += dot(d_scores, q)
            dq_t = dq_t + dot(keys_t[:, here], d_scores)
        dq = dq_t.T * (HEAD_DIM ** -0.5)
        dq_ref[rows, :] = jnp.where(lane < HEAD_DIM, dq[:BLK], dq[BLK:]).astype(BF16)
    for b in range(blocks):
        place = pl.ds(pl.multiple_of(table[b] * BLK, BLK), BLK)
        rows = pl.ds(b * BLK, BLK)
        dk_ref[rows, :] = dk_acc[place, :].astype(BF16)
        dv_ref[rows, :] = dv_acc[place, :].astype(BF16)


def attend_back(table, q, k, v, d_heads, heads, lse):
    mine, width = q.shape
    rows = k.shape[0]
    pairs = width // PAIR
    column = lambda n: pl.BlockSpec((n, PAIR), lambda p, table: (0, p))
    return pl.pallas_call(
        attend_back_kernel,
        grid_spec=pltpu.PrefetchScalarGridSpec(
            num_scalar_prefetch=1,
            grid=(pairs,),
            in_specs=[
                column(mine), column(rows), column(rows), column(mine), column(mine),
                pl.BlockSpec((mine, PAIR), lambda p, table: (0, 0)),
            ],
            out_specs=[column(mine), column(rows), column(rows)],
            scratch_shapes=[
                pltpu.VMEM((rows, PAIR), BF16),
                pltpu.VMEM((rows, PAIR), BF16),
                pltpu.VMEM((PAIR, rows), BF16),
                pltpu.VMEM((rows, PAIR), F32),
                pltpu.VMEM((rows, PAIR), F32),
                pltpu.VMEM((pairs, 8, mine), F32),
            ],
        ),
        out_shape=[
            jax.ShapeDtypeStruct((mine, width), BF16),
            jax.ShapeDtypeStruct((rows, width), BF16),
            jax.ShapeDtypeStruct((rows, width), BF16),
        ],
        compiler_params=pltpu.CompilerParams(vmem_limit_bytes=VMEM_LIMIT),
        cost_estimate=cost(mine * 1280 * width * 20, 8 * rows * width, mine * 1280 * width // HEAD_DIM),
        name="attend_back",
    )(table, q, k, v, d_heads, heads, lse)


GELU_C = 0.7978845608028654
GELU_A = 0.044715
CUTS = 4
MESH = pl.DeviceIdType.MESH


def xor_peer(index, k):
    if k == 1:
        return index + 1 - 2 * lax.rem(index, 2)
    if k == 2:
        return index + 2 - 4 * lax.rem(lax.div(index, 2), 2)
    return index + 3 - 2 * lax.rem(index, 4)


def expert_body(*refs, names, forward, backward, remote, experts):
    r = dict(zip(names, refs))
    up, down, hidden, slope = r["up"], r["down"], r["hidden_s"], r["slope_s"]
    rows, outs = r["rows_s"], r["outs_s"]
    count, width = rows.shape
    peers = r["w"].shape[1]
    half = r["w"].shape[3]
    shard = 2 * half
    size = count // CUTS
    tile = 256
    cuts = [pl.ds(k * size, size) for k in range(CUTS)]
    z = lax.axis_index("expert")
    used = [0]

    def local(src, dst):
        copy = pltpu.make_async_copy(src, dst, r["local"].at[used[0]])
        used[0] += 1
        copy.start()
        return copy

    others = [None] + [{"expert": xor_peer(z, k)} for k in (1, 2, 3)] if remote else None
    if remote:
        barrier = pltpu.get_barrier_semaphore()
        for k in (1, 2, 3):
            pl.semaphore_signal(barrier, inc=1, device_id=others[k], device_id_type=MESH)
    loads = []
    if not remote:
        if forward:
            loads.append(local(r["x"], rows))
        if backward:
            loads.append(local(r["g"], r["d_s"]))
    for t in range(peers):
        for c in range(2):
            loads.append(local(r["w"].at[c, t, 0], up.at[pl.ds(c * half, half), pl.ds(t * shard, shard)]))
            loads.append(local(r["w"].at[c, t, 1], down.at[pl.ds(t * shard + c * half, half), :]))
    if backward and not forward:
        for a, b in (("rows", rows), ("out", outs), ("slope", slope), ("hidden", hidden)):
            loads.append(local(r[a], b))
    if remote:
        pl.semaphore_wait(barrier, 3)

    def one_hot(k):
        index = lax.broadcasted_iota(jnp.int32, (size, r["slot_row"].shape[1]), 0) + k * size
        return jnp.where(index == r["slot_row"][...], 1.0, 0.0).astype(BF16)

    def one_hot_turned(k):
        index = lax.broadcasted_iota(jnp.int32, (r["slot_col"].shape[0], size), 1) + k * size
        return jnp.where(index == r["slot_col"][...], 1.0, 0.0).astype(BF16)

    def dispatch(source, target, stage, base):
        copies = {}
        x = source[...]
        for k in (2, 1, 3):
            stage[k - 1] = dot(one_hot(k), x).astype(BF16)
            copies[k] = pltpu.make_async_remote_copy(
                src_ref=stage.at[k - 1], dst_ref=target.at[cuts[k]],
                send_sem=r["send"].at[base + k - 1], recv_sem=r["recv"].at[base + k - 1],
                device_id=others[k], device_id_type=MESH,
            )
            copies[k].start()
        target[cuts[0], :] = dot(one_hot(0), x).astype(BF16)
        return copies

    def give_back(source, k, base):
        copy = pltpu.make_async_remote_copy(
            src_ref=source.at[cuts[k]], dst_ref=r["back"].at[k - 1],
            send_sem=r["send"].at[base + k - 1], recv_sem=r["recv"].at[base + k - 1],
            device_id=others[k], device_id_type=MESH,
        )
        copy.start()
        return copy

    def combine(source, copies, target):
        total = dot(one_hot_turned(0), source[cuts[0], :])
        for k in (1, 2, 3):
            copies[k].wait_recv()
            total = total + dot(one_hot_turned(k), r["back"][k - 1])
        target[...] = total.astype(BF16)

    def forward_chunk(cut):
        x = rows[cut, :]
        for col in range(0, up.shape[1], tile):
            at = pl.ds(col, tile)
            u = dot(x, up[:, at])
            square = u * u
            gate = 0.5 + 0.5 * jnp.tanh(u * (GELU_C + (GELU_C * GELU_A) * square))
            value = u * gate
            hidden[cut, at] = value.astype(BF16)
            grow = gate + value * (1.0 - gate) * (2 * GELU_C + (6 * GELU_C * GELU_A) * square)
            slope[cut, at] = grow.astype(BF16)
        outs[cut, :] = dot(hidden[cut, :], down[...]).astype(BF16)

    def backward_chunk(cut):
        d = r["d_s"][cut, :]
        for col in range(0, up.shape[1], tile):
            at = pl.ds(col, tile)
            d_hidden = dot_nt(d, down[at, :])
            slope[cut, at] = (d_hidden * slope[cut, at].astype(F32)).astype(BF16)
        x = rows[cut, :]
        logits = dot(x, r["route"][...])
        lane = lax.broadcasted_iota(jnp.int32, logits.shape, 1)
        logits = jnp.where(lane < experts, logits, NEG)
        router = jnp.exp(logits - jnp.max(logits, axis=1, keepdims=True))
        router = router / jnp.sum(router, axis=1, keepdims=True)
        amount = jnp.sum(outs[cut, :].astype(F32) * d.astype(F32), axis=1, keepdims=True)
        d_log = (amount * (jnp.where(lane == z, 1.0, 0.0) - router)).astype(BF16)
        r["log_s"][cut, :] = d_log
        d_rows = dot_nt(slope[cut, :], up[...]) + dot_nt(d_log, r["route"][...])
        r["back_s"][cut, :] = d_rows.astype(BF16)
        return jnp.sum(d_rows * x.astype(F32), axis=0, keepdims=True)

    sent_x = sent_d = None
    saves, returns = [], {}
    if remote and forward:
        sent_x = dispatch(r["x"], rows, r["stage_x"], 0)
    if remote and backward:
        sent_d = dispatch(r["g"], r["d_s"], r["stage_d"], 3)
    for copy in loads:
        copy.wait()
    if forward:
        for k in range(CUTS):
            if remote and k:
                sent_x[k].wait_recv()
            forward_chunk(cuts[k])
            if remote and k and not backward:
                returns[k] = give_back(outs, k, 6)
            if not backward:
                saves.append(local(hidden.at[cuts[k]], r["hidden"].at[cuts[k]]))
                saves.append(local(slope.at[cuts[k]], r["slope"].at[cuts[k]]))
        if not backward:
            saves.append(local(rows, r["rows"]))
        saves.append(local(outs, r["out"]))
    if backward:
        gain = jnp.zeros((1, width), F32)
        for k in range(CUTS):
            if remote and k:
                sent_d[k].wait_recv()
            gain = gain + backward_chunk(cuts[k])
            if remote and k:
                returns[k] = give_back(r["back_s"], k, 6)
        if not remote:
            saves.append(local(r["back_s"], r["result"]))
        r["turned"][...] = rows[...].T
        route = dot_tn(r["log_s"][...], rows[...])
        pad = r["small"].shape[0] - experts - 1
        r["small"][...] = jnp.concatenate([route[:experts], gain, jnp.zeros((pad, width), F32)], axis=0)
        for t in range(peers):
            at = pl.ds(t * shard, shard)
            up[:, at] = dot(r["turned"][...], slope[:, at]).astype(BF16)
            down[at, :] = dot_tn(hidden[:, at], r["d_s"][...]).astype(BF16)
            for c in range(2):
                saves.append(local(up.at[pl.ds(c * half, half), at], r["grads"].at[c, t, 0]))
                saves.append(local(down.at[pl.ds(t * shard + c * half, half), :], r["grads"].at[c, t, 1]))
    if remote:
        combine(r["back_s"] if backward else outs, returns, r["result"])
        for copies in (sent_x, sent_d, returns):
            for k in (1, 2, 3):
                if copies is not None:
                    copies[k].wait_send()
    for copy in saves:
        copy.wait()


def expert_call(w, slots, experts, x=None, g=None, kept=None, route=None, count=None):
    forward, backward, remote = x is not None, g is not None, experts == CUTS
    tokens, width = (x if forward else g).shape
    inner = w.shape[1] * 2 * w.shape[3]
    any_, vmem = pl.BlockSpec(memory_space=pl.ANY), pl.BlockSpec(memory_space=pltpu.VMEM)
    data = vmem if remote else any_
    ins, outs, scratch = [("w", w, any_)], [], []
    shape = jax.ShapeDtypeStruct
    if remote:
        ins += [("slot_row", slots[None, :], vmem), ("slot_col", slots[:, None], vmem)]
    if forward:
        ins.append(("x", x, data))
    if backward:
        ins += [("g", g, data), ("route", route, vmem)]
        if not forward:
            ins += [(name, value, any_) for name, value in zip(("rows", "out", "hidden", "slope"), kept)]
    if remote or backward:
        outs.append(("result", shape((tokens if remote else count, width), BF16), data))
    if forward:
        outs.append(("out", shape((count, width), BF16), any_))
        if not backward:
            outs += [(n, shape((count, s), BF16), any_) for n, s in (("rows", width), ("hidden", inner), ("slope", inner))]
    if backward:
        outs += [("grads", shape(w.shape, BF16), any_), ("small", shape((-(-(experts + 1) // 8) * 8, width), F32), vmem)]
    scratch += [
        ("up", pltpu.VMEM((width, inner), BF16)), ("down", pltpu.VMEM((inner, width), BF16)),
        ("hidden_s", pltpu.VMEM((count, inner), BF16)), ("slope_s", pltpu.VMEM((count, inner), BF16)),
        ("rows_s", pltpu.VMEM((count, width), BF16)), ("outs_s", pltpu.VMEM((count, width), BF16)),
        ("local", pltpu.SemaphoreType.DMA((48,))),
    ]
    if backward:
        scratch += [
            ("d_s", pltpu.VMEM((count, width), BF16)), ("back_s", pltpu.VMEM((count, width), BF16)),
            ("log_s", pltpu.VMEM((count, BLK), BF16)), ("turned", pltpu.VMEM((width, count), BF16)),
        ]
    if remote:
        part = (3, count // CUTS, width)
        scratch += [("back", pltpu.VMEM(part, BF16))]
        scratch += [("stage_x", pltpu.VMEM(part, BF16))] if forward else []
        scratch += [("stage_d", pltpu.VMEM(part, BF16))] if backward else []
        scratch += [("send", pltpu.SemaphoreType.DMA((9,))), ("recv", pltpu.SemaphoreType.DMA((9,)))]
    names = [n for n, _, _ in ins] + [n for n, _, _ in outs] + [n for n, _ in scratch]
    macs = count * width * inner * (2 * forward + 4 * backward)
    params = dict(vmem_limit_bytes=VMEM_LIMIT)
    if remote:
        params.update(collective_id=forward + 2 * backward, has_side_effects=True)
    name = "experts_" + "forward" * forward + "backward" * backward
    results = pl.pallas_call(
        functools.partial(expert_body, names=names, forward=forward, backward=backward, remote=remote, experts=experts),
        in_specs=[spec for _, _, spec in ins],
        out_specs=[spec for _, _, spec in outs],
        out_shape=[s for _, s, _ in outs],
        scratch_shapes=[s for _, s in scratch],
        compiler_params=pltpu.CompilerParams(**params),
        cost_estimate=cost(macs, 10 * inner * width),
        name=name,
    )(*[value for _, value, _ in ins])
    return dict(zip([n for n, _, _ in outs], results))


def experts_forward(w, plan, token_rows, experts, capacity):
    slots, table = plan
    count = experts * capacity
    if experts == CUTS:
        got = expert_call(w, slots, experts, x=token_rows, count=count)
        back = got["result"]
    else:
        rows = send_rows(table, token_rows, experts, capacity)
        got = expert_call(w, slots, experts, x=rows, count=count)
        back = return_rows(table, got["out"], experts, capacity).astype(BF16)
    return back, [got[n] for n in ("rows", "out", "hidden", "slope")]


def experts_backward(w, plan, d_low, kept, route, experts, capacity):
    slots, table = plan
    count = experts * capacity
    if experts == CUTS:
        got = expert_call(w, slots, experts, g=d_low, kept=kept, route=route, count=count)
        return got["result"], got["grads"], got["small"]
    d_sent = send_rows(table, d_low, experts, capacity)
    got = expert_call(w, slots, experts, g=d_sent, kept=kept, route=route, count=count)
    return return_rows(table, got["result"], experts, capacity).astype(BF16), got["grads"], got["small"]


def experts_both(w, plan, token_rows, d_low, route, experts, capacity):
    slots, table = plan
    count = experts * capacity
    if experts == CUTS:
        got = expert_call(w, slots, experts, x=token_rows, g=d_low, route=route, count=count)
        back = got["result"]
    else:
        rows = send_rows(table, token_rows, experts, capacity)
        d_sent = send_rows(table, d_low, experts, capacity)
        got = expert_call(w, slots, experts, x=rows, g=d_sent, route=route, count=count)
        back = return_rows(table, got["result"], experts, capacity).astype(BF16)
    return back, got["out"], got["grads"], got["small"]


def inverse_rms(stream):
    return lax.rsqrt(jnp.mean(stream * stream, axis=-1, keepdims=True) + EPS)


def norm_backward(upstream, stream, inverse, gain):
    weighted = upstream * gain
    inner = jnp.mean(weighted * stream, axis=-1, keepdims=True)
    return inverse * weighted - stream * (inverse * inverse * inverse) * inner


def path_table(segment_ids, path_pos, parent_ids, peers):
    segment = segment_ids[::BLK].reshape(peers, -1)
    position = path_pos[::BLK].reshape(peers, -1)
    t = lax.axis_index("tensor")
    order = jnp.arange(peers, dtype=jnp.int32) ^ t
    match = order[:, None] == jnp.arange(peers, dtype=jnp.int32)[None, :]
    pick = lambda v: jnp.sum(jnp.where(match[:, :, None], v[None], 0), axis=1)
    segment, position = pick(segment), pick(position)
    place = jnp.where(segment == 0, position // BLK, segment + (TRUNK - 1))
    seg, pos, own = segment[0], position[0], place[0]
    names = jnp.arange(parent_ids.shape[-1], dtype=jnp.int32)
    parent = jnp.sum(jnp.where(seg[:, None] == names[None, :], parent_ids[0][None], 0), axis=1)
    leaf = (seg > 0) & (parent > 0)
    parent_place = jnp.where(leaf, parent + (TRUNK - 1), own)
    base_own = jnp.where(seg > 0, pos, BIG)
    base_parent = jnp.where(leaf, TRUNK * BLK, BIG)
    mine = jnp.stack([pos, own, parent_place, base_own, base_parent], axis=1)
    return jnp.concatenate([place.reshape(-1), mine.reshape(-1)]).astype(jnp.int32)


def dispatch_plan(route, experts, capacity):
    count = route.shape[0]
    chosen = route[:, None] == jnp.arange(experts, dtype=jnp.int32)[None, :]
    index = jnp.arange(count, dtype=jnp.int32)
    before = (index[None, :] < index[:, None]).astype(BF16)
    ranks = dot(before, chosen.astype(BF16)).astype(jnp.int32)
    rank = jnp.sum(jnp.where(chosen, ranks, 0), axis=1)
    to = route ^ lax.axis_index("expert") if experts == 4 else route
    slot = to * capacity + rank
    table = slot[None, :] == jnp.arange(experts * capacity, dtype=jnp.int32)[:, None]
    return chosen, (slot, table.astype(BF16))


def send_rows(table, rows, experts, capacity):
    chunks = [
        dot(table[k * capacity : (k + 1) * capacity], rows).astype(BF16) for k in range(experts)
    ]
    return jnp.concatenate(exchange(chunks), axis=0)


def return_rows(table, results, experts, capacity):
    chunks = exchange([results[k * capacity : (k + 1) * capacity] for k in range(experts)])
    return dot_tn(table, jnp.concatenate(chunks, axis=0))


def own_half(x):
    half = x.shape[0] // 2
    return lax.dynamic_slice_in_dim(x, lax.axis_index("dp") * half, half, 0)


def gather_all(x):
    out = lax.all_gather(x, ("dp", "tensor"), axis=0)
    return out.reshape((lax.axis_size("dp"), lax.axis_size("tensor")) + x.shape)


def scatter_all(x):
    flat = x.reshape((-1,) + x.shape[2:])
    return lax.psum_scatter(flat, ("dp", "tensor"), scatter_dimension=0, tiled=True)[0]


def attention_weights(w_mix, w_proj):
    width, _, shard = w_mix.shape
    mix = gather_all(own_half(w_mix.reshape(width, -1)))
    proj = gather_all(own_half(w_proj))
    cores, peers, half, _ = mix.shape
    mix = mix.reshape(cores, peers, half, 3, shard)
    parts = [mix[:, :, :, i].transpose(0, 2, 1, 3).reshape(width, width) for i in range(3)]
    return (*parts, proj.transpose(1, 0, 2, 3).reshape(width, width))


def expert_weights(w_up, w_back):
    return gather_all(jnp.stack([own_half(w_up), own_half(w_back)]))


def swap_cores(half):
    return lax.all_gather(half, "dp", axis=0)


def body(
    hidden_in, route_ids, segment_ids, path_pos, parent_ids, norm_att, w_qkv, w_out, norm_ffn, w_route, w_in, w_down, cotangent,
):
    depth_total = w_qkv.shape[0]
    tokens, width = hidden_in.shape
    experts = w_route.shape[-1]
    capacity = 3 * tokens // (2 * experts)
    peers = lax.axis_size("tensor")
    cores = lax.axis_size("dp")
    shard = width // peers
    half = width // cores
    table = path_table(segment_ids, path_pos, parent_ids, peers)
    plans = [dispatch_plan(route_ids[d, :, 0], experts, capacity) for d in range(depth_total)]
    routes = [jnp.pad(w_route[d], ((0, 0), (0, BLK - experts))) for d in range(depth_total)]
    cotangent = cotangent.astype(F32)

    stream = hidden_in.astype(F32)
    kept = []
    weights, moe = [None] * depth_total, [None] * depth_total
    weights[0] = attention_weights(w_qkv[0], w_out[0])
    for depth in range(depth_total):
        gain_att, gain_ffn = norm_att[depth].astype(F32), norm_ffn[depth].astype(F32)
        chosen, plan = plans[depth]
        inverse_att = inverse_rms(stream)
        normed = (stream * inverse_att * gain_att).astype(BF16)
        normed_all = jnp.concatenate(gather_rows(normed), axis=0)
        if depth == 0:
            moe[0] = expert_weights(w_in[0, 0], w_down[0, 0])
        w_q, w_k, w_v, w_o = weights[depth]
        q = dot(normed, w_q).astype(BF16)
        k = dot(normed_all, w_k).astype(BF16)
        v = dot(normed_all, w_v).astype(BF16)
        heads, lse = attend(table, q, k, v)
        after_att = stream + dot(heads, w_o)
        inverse_ffn = inverse_rms(after_att)
        token_rows = (after_att * inverse_ffn * gain_ffn).astype(BF16)
        if depth + 1 < depth_total:
            weights[depth + 1] = attention_weights(w_qkv[depth + 1], w_out[depth + 1])
            moe[depth + 1] = expert_weights(w_in[depth + 1, 0], w_down[depth + 1, 0])
        router = jax.nn.softmax(dot(token_rows, w_route[depth]), axis=-1)
        gate = jnp.sum(jnp.where(chosen, router, 0.0), axis=1, keepdims=True)
        saved = [stream, inverse_att, normed, normed_all, q, k, v, heads, lse, after_att, inverse_ffn, gate]
        if depth + 1 < depth_total:
            back, held = experts_forward(moe[depth], plan, token_rows, experts, capacity)
            stream = after_att + gate * back.astype(F32)
            saved.append(held)
        else:
            d_low = (gate * cotangent).astype(BF16)
            d_rows, out, g_experts, small = experts_both(
                moe[depth], plan, token_rows, d_low, routes[depth], experts, capacity
            )
            back = return_rows(plan[1], out, experts, capacity)
            hidden_out = (after_att + gate * back).astype(BF16)
            saved.append((d_rows, g_experts, small))
        kept.append(saved)

    upstream = cotangent
    grads, smalls = [None] * depth_total, [None] * depth_total
    for depth in reversed(range(depth_total)):
        stream, inverse_att, normed, normed_all, q, k, v, heads, lse, after_att, inverse_ffn, gate, held = kept[depth]
        gain_att, gain_ffn = norm_att[depth].astype(F32), norm_ffn[depth].astype(F32)
        chosen, plan = plans[depth]
        w_q, w_k, w_v, w_o = weights[depth]
        if depth + 1 < depth_total:
            d_low = (gate * upstream).astype(BF16)
            d_rows, g_experts, small = experts_backward(moe[depth], plan, d_low, held, routes[depth], experts, capacity)
        else:
            d_rows, g_experts, small = held
        g_experts = swap_cores(scatter_all(g_experts)).astype(F32)
        grad_up, grad_down = [g_experts[:, i].reshape(width, width) for i in range(2)]

        dx1 = upstream + norm_backward(d_rows.astype(F32), after_att, inverse_ffn, gain_ffn)
        d_att = dx1.astype(BF16)
        d_heads = dot_nt(d_att, w_o).astype(BF16)
        dq, dk, dv = attend_back(table, q, k, v, d_heads, heads, lse)
        blocks = []
        for j in reversed(range(peers)):
            at = slice(j * tokens, (j + 1) * tokens)
            part = dot_nt(dk[at], w_k) + dot_nt(dv[at], w_v)
            if j == 0:
                part = part + dot_nt(dq, w_q)
            else:
                part = part.astype(BF16)
            blocks.insert(0, part)
        d_normed = scatter_rows(blocks[1:], blocks[0])
        g_q, g_k, g_v = dot_tn(normed, dq), dot_tn(normed_all, dk), dot_tn(normed_all, dv)
        g_o = dot_tn(heads, d_att).astype(BF16)
        att_sum = jnp.sum(g_q * w_q.astype(F32) + g_k * w_k.astype(F32) + g_v * w_v.astype(F32), axis=1)
        g_mix = jnp.concatenate(
            [g.astype(BF16).reshape(cores, half, peers, shard).transpose(0, 2, 1, 3) for g in (g_q, g_k, g_v)], axis=3
        )
        g_o = g_o.reshape(peers, cores, shard // cores, width).transpose(1, 0, 2, 3)
        mix_mine, out_mine = lax.psum((scatter_all(g_mix), scatter_all(g_o)), "expert")
        grad_mix = swap_cores(mix_mine).astype(F32).reshape(width, 3, shard)
        grad_out = swap_cores(out_mine).astype(F32).reshape(shard, width)
        smalls[depth] = jnp.concatenate([small[: experts + 1], att_sum[None]], axis=0)
        grads[depth] = (grad_mix, grad_out, grad_up[None], grad_down[None])
        upstream = dx1 + norm_backward(d_normed, stream, inverse_att, gain_att)
    small = sum_small(jnp.stack(smalls))
    stacked = [jnp.stack([grads[d][m] for d in range(depth_total)]) for m in range(4)]
    grad_route = small[:, :experts].transpose(0, 2, 1)
    grad_ffn = small[:, experts] / norm_ffn.astype(F32)
    grad_att = small[:, experts + 1] / norm_att.astype(F32)
    return (hidden_out, upstream, grad_att, stacked[0], stacked[1], grad_ffn, grad_route, stacked[2], stacked[3])


def solution(mesh):
    in_specs = (
        P(("dp", "expert", "tensor"), None),
        P(None, ("dp", "expert", "tensor"), None),
        P(("dp", "expert")),
        P(("dp", "expert")),
        P(("dp", "expert"), None),
        P(),
        P(None, None, None, "tensor"),
        P(None, "tensor", None),
        P(),
        P(),
        P(None, "expert", None, "tensor"),
        P(None, "expert", "tensor", None),
        P(("dp", "expert", "tensor"), None),
    )
    out_specs = (
        P(("dp", "expert", "tensor"), None),
        P(("dp", "expert", "tensor"), None),
        P(),
        P(None, None, None, "tensor"),
        P(None, "tensor", None),
        P(),
        P(),
        P(None, "expert", None, "tensor"),
        P(None, "expert", "tensor", None),
    )
    return jax.shard_map(body, mesh=mesh, in_specs=in_specs, out_specs=out_specs, check_vma=False)
```

```python
from types import SimpleNamespace

import jax
import jax.numpy as jnp
from jax import lax
from jax.experimental import pallas as pl
from jax.experimental.pallas import tpu as pltpu
from jax.sharding import PartitionSpec as P

HEAD_DIM = 64
BLK = 128
TRUNK = 8
PAIR = 2 * HEAD_DIM
EPS = 1e-06
NEG = -1000000000.0
BIG = 1 << 20
F32 = jnp.float32
BF16 = jnp.bfloat16
VMEM_LIMIT = 58 * 1024 * 1024
DP, EXPERT, TENSOR = "dp", "expert", "tensor"

NT = (((1,), (1,)), ((), ()))
TN = (((0,), (0,)), ((), ()))


def dot(a, b):
    return jnp.dot(a, b, preferred_element_type=F32)


def dot_nt(a, b):
    return lax.dot_general(a, b, NT, preferred_element_type=F32)


def dot_tn(a, b):
    return lax.dot_general(a, b, TN, preferred_element_type=F32)


def cost(macs, moved, trans=0):
    return pl.CostEstimate(flops=macs // 64, bytes_accessed=moved // 64, transcendentals=0)


def xperm(x, axis, k):
    n = lax.axis_size(axis)
    return lax.ppermute(x, axis, [(i, i ^ k) for i in range(n)])


def after(x, dep):
    return lax.optimization_barrier((x, dep))[0]


def sum_small(x):
    for axis in (DP, TENSOR, EXPERT):
        n = lax.axis_size(axis)
        k = 1
        while k < n:
            x = x + xperm(x, axis, k)
            k *= 2
    return x


def exchange(chunks):
    n = len(chunks)
    if n == 4:
        return [chunks[0]] + [xperm(chunks[k], EXPERT, k) for k in range(1, n)]
    out = lax.all_to_all(jnp.stack(chunks), EXPERT, split_axis=0, concat_axis=0, tiled=True)
    return [out[k] for k in range(n)]


def masked_pair(x):
    lane = lax.broadcasted_iota(jnp.int32, x.shape, 1)
    zero = jnp.zeros_like(x)
    return jnp.concatenate([jnp.where(lane < HEAD_DIM, x, zero), jnp.where(lane < HEAD_DIM, zero, x)], axis=0)


def attend_kernel(table, q_ref, k_ref, v_ref, out_ref, lse_ref, keys, values):
    pair = pl.program_id(0)
    blocks = k_ref.shape[0] // BLK
    mine = q_ref.shape[0] // BLK
    trunk = TRUNK * BLK
    for b in range(blocks):
        place = pl.ds(pl.multiple_of(table[b] * BLK, BLK), BLK)
        rows = pl.ds(b * BLK, BLK)
        keys[place, :] = k_ref[rows, :]
        values[place, pl.ds(0, PAIR)] = v_ref[rows, :]
    values[:, pl.ds(PAIR, PAIR)] = jnp.ones((blocks * BLK, PAIR), BF16)
    lane = lax.broadcasted_iota(jnp.int32, (BLK, PAIR), 1)
    for i in range(mine):
        at = blocks + 5 * i
        place_q, own, parent, base_own, base_parent = [table[at + j] for j in range(5)]
        rows = pl.ds(i * BLK, BLK)
        own_rows = pl.ds(pl.multiple_of(own * BLK, BLK), BLK)
        parent_rows = pl.ds(pl.multiple_of(parent * BLK, BLK), BLK)
        q = masked_pair(q_ref[rows, :] * jnp.asarray(HEAD_DIM ** -0.5, BF16))
        row = lax.broadcasted_iota(jnp.int32, (2 * BLK, 1), 0) % BLK
        pos_q = place_q + row
        s_trunk = dot_nt(q, keys[pl.ds(0, trunk), :])
        key_pos = lax.broadcasted_iota(jnp.int32, s_trunk.shape, 1)
        s_trunk = jnp.where(key_pos <= pos_q, s_trunk, NEG)
        s_parent = dot_nt(q, keys[parent_rows, :])
        col = lax.broadcasted_iota(jnp.int32, s_parent.shape, 1)
        s_parent = jnp.where(col + base_parent <= pos_q, s_parent, NEG)
        s_own = dot_nt(q, keys[own_rows, :])
        s_own = jnp.where(col + base_own <= pos_q, s_own, NEG)
        top = jnp.maximum(
            jnp.max(s_trunk, axis=1, keepdims=True),
            jnp.max(jnp.maximum(s_parent, s_own), axis=1, keepdims=True),
        )
        p_trunk = jnp.exp(s_trunk - top).astype(BF16)
        p_parent = jnp.exp(s_parent - top).astype(BF16)
        p_own = jnp.exp(s_own - top).astype(BF16)
        both = dot(p_trunk, values[pl.ds(0, trunk), :])
        both = both + dot(p_parent, values[parent_rows, :]) + dot(p_own, values[own_rows, :])
        total = both[:, PAIR:]
        heads = both[:, :PAIR] / total
        lse = top + jnp.log(total)
        out_ref[rows, :] = jnp.where(lane < HEAD_DIM, heads[:BLK], heads[BLK:]).astype(BF16)
        known = jnp.where(pair == 0, 0.0, lse_ref[rows, :])
        known = jnp.where(lane == 2 * pair, lse[:BLK], known)
        lse_ref[rows, :] = jnp.where(lane == 2 * pair + 1, lse[BLK:], known)


def attend(table, q, k, v):
    mine, width = q.shape
    rows = k.shape[0]
    pairs = width // PAIR
    column = lambda n: pl.BlockSpec((n, PAIR), lambda p, table: (0, p))
    return pl.pallas_call(
        attend_kernel,
        grid_spec=pltpu.PrefetchScalarGridSpec(
            num_scalar_prefetch=1,
            grid=(pairs,),
            in_specs=[column(mine), column(rows), column(rows)],
            out_specs=[column(mine), pl.BlockSpec((mine, PAIR), lambda p, table: (0, 0))],
            scratch_shapes=[pltpu.VMEM((rows, PAIR), BF16), pltpu.VMEM((rows, 2 * PAIR), BF16)],
        ),
        out_shape=[jax.ShapeDtypeStruct((mine, width), BF16), jax.ShapeDtypeStruct((mine, PAIR), F32)],
        compiler_params=pltpu.CompilerParams(vmem_limit_bytes=VMEM_LIMIT),
        cost_estimate=cost(mine * 1280 * width * 8, 4 * rows * width, mine * 1280 * width // HEAD_DIM),
        name="attend",
    )(table, q, k, v)


def attend_back_kernel(
    table, q_ref, k_ref, v_ref, do_ref, o_ref, lse_ref, dq_ref, dk_ref, dv_ref,
    keys, values, keys_t, dk_acc, dv_acc, lse_t,
):
    pair = pl.program_id(0)
    blocks = k_ref.shape[0] // BLK
    mine = q_ref.shape[0] // BLK
    trunk = TRUNK * BLK
    for b in range(blocks):
        place = pl.ds(pl.multiple_of(table[b] * BLK, BLK), BLK)
        rows = pl.ds(b * BLK, BLK)
        keys[place, :] = k_ref[rows, :]
        values[place, :] = v_ref[rows, :]
        keys_t[:, place] = k_ref[rows, :].T
    dk_acc[...] = jnp.zeros_like(dk_acc)
    dv_acc[...] = jnp.zeros_like(dv_acc)

    @pl.when(pair == 0)
    def _():
        for i in range(mine):
            turned = lse_ref[pl.ds(i * BLK, BLK), :].T
            for p in range(lse_t.shape[0]):
                lse_t[p, pl.ds(0, 2), pl.ds(i * BLK, BLK)] = turned[2 * p : 2 * p + 2]

    lane = lax.broadcasted_iota(jnp.int32, (BLK, PAIR), 1)
    scale = jnp.asarray(HEAD_DIM ** -0.5, BF16)
    for i in range(mine):
        at = blocks + 5 * i
        place_q, own, parent, base_own, base_parent = [table[at + j] for j in range(5)]
        rows = pl.ds(i * BLK, BLK)
        q = masked_pair(q_ref[rows, :] * scale)
        do = do_ref[rows, :]
        product = (do.astype(F32) * o_ref[rows, :].astype(F32)).T
        inner = jnp.concatenate(
            [
                jnp.sum(product[:HEAD_DIM], axis=0, keepdims=True),
                jnp.sum(product[HEAD_DIM:], axis=0, keepdims=True),
            ],
            axis=1,
        )
        do = masked_pair(do)
        lse = jnp.concatenate([lse_t[pair, pl.ds(0, 1), rows], lse_t[pair, pl.ds(1, 1), rows]], axis=1)
        pos_q = place_q + lax.broadcasted_iota(jnp.int32, (1, 2 * BLK), 1) % BLK
        dq_t = jnp.zeros((PAIR, 2 * BLK), F32)
        steps = [(j * 2 * BLK, 2 * BLK, j * 2 * BLK) for j in range(TRUNK // 2)]
        steps += [(pl.multiple_of(parent * BLK, BLK), BLK, base_parent)]
        steps += [(pl.multiple_of(own * BLK, BLK), BLK, base_own)]
        for start, size, base in steps:
            here = pl.ds(start, size)
            k_rows, v_rows = keys[here, :], values[here, :]
            scores = dot_nt(k_rows, q)
            key_pos = base + lax.broadcasted_iota(jnp.int32, (size, 1), 0)
            weights = jnp.exp(jnp.where(key_pos <= pos_q, scores - lse, NEG))
            d_weights = dot_nt(v_rows, do)
            d_scores = (weights * (d_weights - inner)).astype(BF16)
            dv_acc[here, :] += dot(weights.astype(BF16), do)
            dk_acc[here, :] += dot(d_scores, q)
            dq_t = dq_t + dot(keys_t[:, here], d_scores)
        dq = dq_t.T * (HEAD_DIM ** -0.5)
        dq_ref[rows, :] = jnp.where(lane < HEAD_DIM, dq[:BLK], dq[BLK:]).astype(BF16)
    for b in range(blocks):
        place = pl.ds(pl.multiple_of(table[b] * BLK, BLK), BLK)
        rows = pl.ds(b * BLK, BLK)
        dk_ref[rows, :] = dk_acc[place, :].astype(BF16)
        dv_ref[rows, :] = dv_acc[place, :].astype(BF16)


def attend_back(table, q, k, v, d_heads, heads, lse):
    mine, width = q.shape
    rows = k.shape[0]
    pairs = width // PAIR
    column = lambda n: pl.BlockSpec((n, PAIR), lambda p, table: (0, p))
    return pl.pallas_call(
        attend_back_kernel,
        grid_spec=pltpu.PrefetchScalarGridSpec(
            num_scalar_prefetch=1,
            grid=(pairs,),
            in_specs=[
                column(mine), column(rows), column(rows), column(mine), column(mine),
                pl.BlockSpec((mine, PAIR), lambda p, table: (0, 0)),
            ],
            out_specs=[column(mine), column(rows), column(rows)],
            scratch_shapes=[
                pltpu.VMEM((rows, PAIR), BF16),
                pltpu.VMEM((rows, PAIR), BF16),
                pltpu.VMEM((PAIR, rows), BF16),
                pltpu.VMEM((rows, PAIR), F32),
                pltpu.VMEM((rows, PAIR), F32),
                pltpu.VMEM((pairs, 8, mine), F32),
            ],
        ),
        out_shape=[
            jax.ShapeDtypeStruct((mine, width), BF16),
            jax.ShapeDtypeStruct((rows, width), BF16),
            jax.ShapeDtypeStruct((rows, width), BF16),
        ],
        compiler_params=pltpu.CompilerParams(vmem_limit_bytes=VMEM_LIMIT),
        cost_estimate=cost(mine * 1280 * width * 20, 8 * rows * width, mine * 1280 * width // HEAD_DIM),
        name="attend_back",
    )(table, q, k, v, d_heads, heads, lse)


GELU_C = 0.7978845608028654
GELU_A = 0.044715
CUTS = 4
MESH = pl.DeviceIdType.MESH
ANY = pl.BlockSpec(memory_space=pl.ANY)
VMEM = pl.BlockSpec(memory_space=pltpu.VMEM)


def low_shape(*dims):
    return jax.ShapeDtypeStruct(dims, BF16)


def low_vmem(*dims):
    return pltpu.VMEM(dims, BF16)


def run_kernel(body, ins, outs, scratch, identity, macs, near, far, **flags):
    scratch = dict(scratch, near=pltpu.SemaphoreType.DMA((near,)))
    params = dict(vmem_limit_bytes=VMEM_LIMIT)
    if far:
        scratch.update(send=pltpu.SemaphoreType.DMA((far,)), recv=pltpu.SemaphoreType.DMA((far,)))
        params.update(collective_id=identity, has_side_effects=True)
    names = [*ins, *outs, *scratch]

    def kernel(*refs):
        body(Moves(SimpleNamespace(**dict(zip(names, refs)))), **flags)

    results = pl.pallas_call(
        kernel,
        in_specs=[spec for _, spec in ins.values()],
        out_specs=[spec for _, spec in outs.values()],
        out_shape=[shape for shape, _ in outs.values()],
        scratch_shapes=list(scratch.values()),
        compiler_params=pltpu.CompilerParams(**params),
        cost_estimate=cost(macs, 0),
        name=body.__name__,
    )(*[value for value, _ in ins.values()])
    return SimpleNamespace(**dict(zip(outs, results)))


def xor_peer(index, k):
    if k == 1:
        return index + 1 - 2 * lax.rem(index, 2)
    if k == 2:
        return index + 2 - 4 * lax.rem(lax.div(index, 2), 2)
    return index + 3 - 2 * lax.rem(index, 4)


class Moves:
    def __init__(self, refs):
        self.refs, self.near, self.far, self.seen, self.left, self.sent = refs, 0, 0, set(), set(), []
        self.c, self.t, self.z = [lax.axis_index(axis) for axis in (DP, TENSOR, EXPERT)]
        self.x_peer, self.y_peer = [{TENSOR: xor_peer(self.t, k)} for k in (1, 2)]
        self.sibling = {DP: 1 - self.c}
        self.z_peers = [{EXPERT: xor_peer(self.z, k)} for k in (1, 2, 3)]

    def local(self, src, dst):
        copy = pltpu.make_async_copy(src, dst, self.refs.near.at[self.near])
        self.near += 1
        copy.start()
        return copy

    def remote(self, src, dst, device):
        copy = pltpu.make_async_remote_copy(
            src_ref=src, dst_ref=dst, send_sem=self.refs.send.at[self.far], recv_sem=self.refs.recv.at[self.far],
            device_id=device, device_id_type=MESH,
        )
        self.far += 1
        copy.start()
        self.sent.append(copy)
        return copy

    def need(self, *copies):
        for copy in copies:
            if id(copy) not in self.seen:
                self.seen.add(id(copy))
                copy.wait()

    def arrived(self, *copies):
        for copy in copies:
            if id(copy) not in self.seen:
                self.seen.add(id(copy))
                copy.wait_recv()

    def finish(self):
        self.gone(*self.sent)

    def gone(self, *copies):
        for copy in copies:
            if id(copy) not in self.left:
                self.left.add(id(copy))
                copy.wait_send()

    def greet(self, devices):
        barrier = pltpu.get_barrier_semaphore()
        for device in devices:
            pl.semaphore_signal(barrier, inc=1, device_id=device, device_id_type=MESH)
        return lambda: pl.semaphore_wait(barrier, len(devices))


def add_low(ref, *more):
    total = ref[...].astype(F32)
    for other in more:
        total = total + other[...].astype(F32)
    return total


class Scatter:
    def __init__(self, moves, pack, core_in, g_in, piece):
        self.moves, self.pack, self.core_in, self.g_in, self.piece = moves, pack, core_in, g_in, piece
        self.peers = core_in.shape[0]
        self.size = pack.shape[1] // 2
        c, t = moves.c, moves.t
        self.index = [t] + [xor_peer(t, k) for k in (1, 2, 3)]
        self.slots = [c * self.peers + i for i in self.index]
        self.flow = [dict(), dict()]

    def rows(self, h):
        return pl.ds(h * self.size, self.size)

    def sides(self, h):
        half = self.size // 2
        return pl.ds(h * self.size, half), pl.ds(h * self.size + half, half)

    def swap(self, h):
        m = self.moves
        there = pl.ds((1 - m.c) * self.peers, self.peers)
        self.flow[h][0] = m.remote(self.pack.at[there, self.rows(h)], self.core_in.at[:, self.rows(h)], m.sibling)

    def out(self, h):
        m, pack, slots, f = self.moves, self.pack, self.slots, self.flow[h]
        left, right = self.sides(h)
        m.arrived(f[0])
        for j in (3, 1, 2, 0):
            pack[slots[j], self.rows(h), :] = add_low(
                pack.at[slots[j], self.rows(h)], self.core_in.at[self.index[j], self.rows(h)]
            ).astype(BF16)
        f[1] = m.remote(pack.at[slots[3], left], self.g_in.at[h, 0], m.x_peer)
        f[2] = m.remote(pack.at[slots[3], right], self.g_in.at[h, 1], m.y_peer)
        f[3] = m.remote(pack.at[slots[1], left], self.g_in.at[h, 2], m.x_peer)
        f[4] = m.remote(pack.at[slots[2], right], self.g_in.at[h, 3], m.y_peer)

    def turn(self, h):
        m, pack, slots, f = self.moves, self.pack, self.slots, self.flow[h]
        left, right = self.sides(h)
        m.arrived(f[1])
        pack[slots[2], left, :] = add_low(pack.at[slots[2], left], self.g_in.at[h, 0]).astype(BF16)
        f[5] = m.remote(pack.at[slots[2], left], self.g_in.at[h, 4], m.y_peer)
        m.arrived(f[2])
        pack[slots[1], right, :] = add_low(pack.at[slots[1], right], self.g_in.at[h, 1]).astype(BF16)
        f[6] = m.remote(pack.at[slots[1], right], self.g_in.at[h, 5], m.x_peer)

    def end(self, h):
        f = self.flow[h]
        self.moves.arrived(f[3], f[4], f[5], f[6])
        for cut, a, b in zip(self.sides(h), (2, 3), (4, 5)):
            total = add_low(self.pack.at[self.slots[0], cut], self.g_in.at[h, a], self.g_in.at[h, b])
            self.piece[cut, :] = total.astype(BF16)


class Gather:
    def __init__(self, moves, pack):
        self.moves, self.pack = moves, pack
        self.half = pack.shape[1] // 2
        self.slots = [moves.c * (pack.shape[0] // 2) + i for i in [moves.t] + [xor_peer(moves.t, k) for k in (1, 2, 3)]]

    def out(self):
        own = self.pack.at[self.slots[0]]
        self.first = [self.moves.remote(own, own, device) for device in (self.moves.x_peer, self.moves.y_peer)]

    def turn(self):
        m = self.moves
        self.swaps, self.second = [], []
        for k, device in ((1, m.y_peer), (2, m.x_peer)):
            m.arrived(self.first[k - 1])
            piece = self.pack.at[self.slots[k], pl.ds((k - 1) * self.half, self.half)]
            self.second.append(m.remote(piece, piece, device))
            self.swap(k)

    def swap(self, k):
        whole = self.pack.at[self.slots[k]]
        self.swaps.append(self.moves.remote(whole, whole, self.moves.sibling))

    def end(self):
        self.moves.arrived(*self.second)
        self.swap(3)
        self.moves.arrived(*self.swaps)


def scatter_scratch(peers, half, width):
    return dict(
        pack_s=low_vmem(2 * peers, half, width), core_in=low_vmem(peers, half, width),
        g_in=low_vmem(2, 6, half // 4, width), piece=low_vmem(half, width),
    )


def one_hot(slot_row, k, size):
    index = lax.broadcasted_iota(jnp.int32, (size, slot_row.shape[1]), 0) + k * size
    return jnp.where(index == slot_row[...], 1.0, 0.0).astype(BF16)


def one_hot_turned(slot_col, k, size):
    index = lax.broadcasted_iota(jnp.int32, (slot_col.shape[0], size), 1) + k * size
    return jnp.where(index == slot_col[...], 1.0, 0.0).astype(BF16)


def combine(m, slot_col, source, copies, back, size):
    total = dot(one_hot_turned(slot_col, 0, size), source[pl.ds(0, size), :])
    for k in (1, 2, 3):
        m.arrived(copies[k])
        total = total + dot(one_hot_turned(slot_col, k, size), back[k - 1])
    return total.astype(BF16)


def expert_part(m, forward, backward, remote, hosted, reduces, fetches, experts):
    r = m.refs
    up, down, hidden, slope, rows, outs = r.up, r.down, r.hidden_s, r.slope_s, r.rows_s, r.outs_s
    count, width = rows.shape
    inner = up.shape[1]
    half = width // 2
    peers = inner // width
    size = count // CUTS
    tile = 256
    cuts = [pl.ds(k * size, size) for k in range(CUTS)]
    met = []
    if remote:
        met += m.z_peers
    if hosted or reduces:
        met += [m.x_peer, m.y_peer]
    if remote:
        met += [m.sibling]
    ready = m.greet(met) if met else None

    def up_at(c, t, start=0, rows=half):
        return up.at[pl.ds(pl.multiple_of(c * half + start, half // 2), rows), pl.ds(pl.multiple_of(t * width, width), width)]

    def down_at(c, t, start=0, rows=half):
        return down.at[pl.ds(pl.multiple_of(t * width + c * half + start, half // 2), rows)]

    loads, weight_loads = [], []
    if not remote:
        if forward:
            loads.append(m.local(r.x, rows))
        if backward:
            loads.append(m.local(r.g, r.d_s))
    if hosted:
        weight_loads.append(m.local(r.own_up, up.at[:, pl.ds(pl.multiple_of(m.t * width, width), width)]))
        weight_loads.append(m.local(r.own_down, down.at[pl.ds(pl.multiple_of(m.t * width, width), width)]))
    else:
        for t in range(peers):
            for c in range(2):
                weight_loads += [m.local(r.w.at[c, t, 0], up_at(c, t)), m.local(r.w.at[c, t, 1], down_at(c, t))]
    if backward and not forward:
        loads += [m.local(a, b) for a, b in ((r.rows, rows), (r.out, outs), (r.slope, slope), (r.hidden, hidden))]
    if ready:
        ready()

    def dispatch(source, target, stage):
        copies = {}
        x = source[...]
        for k in (2, 1, 3):
            stage[k - 1] = dot(one_hot(r.slot_row, k, size), x).astype(BF16)
            copies[k] = m.remote(stage.at[k - 1], target.at[cuts[k]], m.z_peers[k - 1])
        target[cuts[0], :] = dot(one_hot(r.slot_row, 0, size), x).astype(BF16)
        return copies

    def give_back(source, k):
        return m.remote(source.at[cuts[k]], r.back.at[k - 1], m.z_peers[k - 1])

    def forward_block(cut, at):
        u = dot(rows[cut, :], up[:, at])
        square = u * u
        gate = 0.5 + 0.5 * jnp.tanh(u * (GELU_C + (GELU_C * GELU_A) * square))
        value = u * gate
        hidden[cut, at] = value.astype(BF16)
        grow = gate + value * (1.0 - gate) * (2 * GELU_C + (6 * GELU_C * GELU_A) * square)
        slope[cut, at] = grow.astype(BF16)

    def forward_peer(cut, t):
        for col in range(0, width, tile):
            forward_block(cut, pl.ds(pl.multiple_of(t * width + col, tile), tile))

    def forward_down(cut):
        outs[cut, :] = dot(hidden[cut, :], down[...]).astype(BF16)

    def backward_chunk(cut):
        d = r.d_s[cut, :]
        for col in range(0, inner, tile):
            at = pl.ds(col, tile)
            d_hidden = dot_nt(d, down[at, :])
            slope[cut, at] = (d_hidden * slope[cut, at].astype(F32)).astype(BF16)
        x = rows[cut, :]
        logits = dot(x, r.route[...])
        lane = lax.broadcasted_iota(jnp.int32, logits.shape, 1)
        logits = jnp.where(lane < experts, logits, NEG)
        router = jnp.exp(logits - jnp.max(logits, axis=1, keepdims=True))
        router = router / jnp.sum(router, axis=1, keepdims=True)
        amount = jnp.sum(outs[cut, :].astype(F32) * d.astype(F32), axis=1, keepdims=True)
        d_log = (amount * (jnp.where(lane == m.z, 1.0, 0.0) - router)).astype(BF16)
        r.log_s[cut, :] = d_log
        d_rows = dot_nt(slope[cut, :], up[...]) + dot_nt(d_log, r.route[...])
        r.back_s[cut, :] = d_rows.astype(BF16)
        return jnp.sum(d_rows * x.astype(F32), axis=0, keepdims=True)

    sent_x = sent_d = None
    saves, returns = [], {}
    scatter = None
    if fetches:
        next_loads = [m.local(r.next_own.at[pl.ds(c * half, half)], r.next_s.at[c * peers + m.t]) for c in range(2)]
        fetch = Gather(m, r.next_s)
    if hosted:
        first = {}
        for k, device in ((1, m.x_peer), (2, m.y_peer)):
            mine = pl.ds(pl.multiple_of(m.c * half, half), half)
            first[k] = [m.remote(r.own_up.at[mine], up_at(m.c, m.t), device), m.remote(r.own_down.at[mine], down_at(m.c, m.t), device)]
    if reduces:
        scatter = Scatter(m, r.pack_s, r.core_in, r.g_in, r.piece)
        pack_load = m.local(r.pack, r.pack_s)
    if remote and forward:
        sent_x = dispatch(r.x, rows, r.stage_x)
    if remote and backward:
        sent_d = dispatch(r.g, r.d_s, r.stage_d)
    if reduces:
        m.need(pack_load)
        scatter.swap(0)
        scatter.swap(1)
    m.need(*loads, *weight_loads)
    if hosted:
        tens = [m.t] + [xor_peer(m.t, k) for k in (1, 2, 3)]
        onward, swaps = [], {}

        def pass_on(k, device, start):
            m.arrived(*first[k])
            for at in (up_at, down_at):
                piece = at(m.c, tens[k], start, half // 2)
                onward.append(m.remote(piece, piece, device))
            swap(k)

        def swap(k):
            swaps[k] = [m.remote(at(m.c, tens[k]), at(m.c, tens[k]), m.sibling) for at in (up_at, down_at)]

        forward_peer(cuts[0], tens[0])
        m.arrived(sent_x[1])
        forward_peer(cuts[1], tens[0])
        pass_on(1, m.y_peer, 0)
        pass_on(2, m.x_peer, half // 2)
        if fetches:
            m.need(*next_loads)
            fetch.out()
        m.arrived(sent_x[2])
        forward_peer(cuts[2], tens[0])
        m.arrived(sent_x[3])
        forward_peer(cuts[3], tens[0])
        for k in (1, 2, 3):
            if k == 3:
                m.arrived(*onward)
                swap(3)
            m.arrived(*swaps[k])
            for cut in cuts:
                forward_peer(cut, tens[k])
        if fetches:
            fetch.turn()
        for k in (2, 3, 1, 0):
            forward_down(cuts[k])
            if k and not backward:
                returns[k] = give_back(outs, k)
        if not backward:
            for c in range(2):
                for t in range(peers):
                    saves += [m.local(up_at(c, t), r.w.at[c, t, 0]), m.local(down_at(c, t), r.w.at[c, t, 1])]
        if fetches:
            fetch.end()
            saves.append(m.local(r.next_s, r.next_all))
    elif forward:
        for k in range(CUTS):
            if remote and k:
                m.arrived(sent_x[k])
            for t in range(peers):
                forward_peer(cuts[k], t)
            forward_down(cuts[k])
            if remote and k and not backward:
                returns[k] = give_back(outs, k)
    if forward:
        if not backward:
            saves += [m.local(hidden, r.hidden), m.local(slope, r.slope), m.local(rows, r.rows)]
        saves.append(m.local(outs, r.out))
    if backward:
        gain = jnp.zeros((1, width), F32)
        for k in range(CUTS):
            if remote and k:
                m.arrived(sent_d[k])
            gain = gain + backward_chunk(cuts[k])
            if remote and k:
                returns[k] = give_back(r.back_s, k)
            if reduces and k < 2:
                for h in range(2):
                    (scatter.out, scatter.turn)[k](h)
        if not remote:
            saves.append(m.local(r.back_s, r.result))
        if reduces:
            for h in range(2):
                scatter.end(h)
            saves.append(m.local(r.piece, r.summed))
        r.turned[...] = rows[...].T
        route = dot_tn(r.log_s[...], rows[...])
        pad = r.small.shape[0] - experts - 1
        r.small[...] = jnp.concatenate([route[:experts], gain, jnp.zeros((pad, width), F32)], axis=0)
        swapped = []
        if hosted:
            m.gone(*onward, *[copy for k in (1, 2, 3) for copy in swaps[k]])
        for t in range(peers):
            at = pl.ds(t * width, width)
            up[:, at] = dot(r.turned[...], slope[:, at]).astype(BF16)
            down[at, :] = dot_tn(hidden[:, at], r.d_s[...]).astype(BF16)
            if remote:
                swapped.append([m.remote(at(1 - m.c, t), r.grads_in.at[t, i], m.sibling) for i, at in enumerate((up_at, down_at))])
            else:
                for c in range(2):
                    saves += [m.local(up_at(c, t), r.grads.at[c, t, 0]), m.local(down_at(c, t), r.grads.at[c, t, 1])]
    if remote:
        if backward:
            for t in range(peers):
                for i, at in enumerate((up_at, down_at)):
                    m.arrived(swapped[t][i])
                    here = at(m.c, t)
                    here[...] = add_low(here, r.grads_in.at[t, i]).astype(BF16)
                    saves.append(m.local(here, r.grads.at[t, i]))
        r.result[...] = combine(m, r.slot_col, r.back_s if backward else outs, returns, r.back, size)
    m.finish()
    m.need(*saves)


def expert_call(plan, experts, count, w=None, own=None, x=None, g=None, kept=None, route=None, pack=None, fetch=None):
    slots = plan[0]
    forward, backward, remote, hosted, reduces = x is not None, g is not None, experts == CUTS, own is not None, pack is not None
    tokens, width = (x if forward else g).shape
    peers = lax.axis_size(TENSOR)
    half, inner = width // 2, peers * width
    w_shape = low_shape(2, peers, 2, half, width)
    data = VMEM if remote else ANY
    rows_shape, inner_shape = low_shape(count, width), low_shape(count, inner)
    ins, outs = {}, {}
    if hosted:
        ins.update(own_up=(own[0], ANY), own_down=(own[1], ANY))
        if not backward:
            outs.update(w=(w_shape, ANY))
    else:
        ins.update(w=(w, ANY))
    if remote:
        ins.update(slot_row=(slots[None, :], VMEM), slot_col=(slots[:, None], VMEM))
    if forward:
        ins.update(x=(x, data))
    if backward:
        ins.update(g=(g, data), route=(route, VMEM))
        if not forward:
            ins.update(rows=(kept.rows, ANY), out=(kept.out, ANY), hidden=(kept.hidden, ANY), slope=(kept.slope, ANY))
    if remote or backward:
        outs.update(result=(low_shape(tokens if remote else count, width), data))
    if forward:
        outs.update(out=(rows_shape, ANY))
        if not backward:
            outs.update(rows=(rows_shape, ANY), hidden=(inner_shape, ANY), slope=(inner_shape, ANY))
    if backward:
        outs.update(grads=(low_shape(peers, 2, half, width) if remote else w_shape, ANY), small=(jax.ShapeDtypeStruct((-(-(experts + 1) // 8) * 8, width), F32), VMEM))
    scratch = dict(
        up=low_vmem(width, inner), down=low_vmem(inner, width), hidden_s=low_vmem(count, inner), slope_s=low_vmem(count, inner),
        rows_s=low_vmem(count, width), outs_s=low_vmem(count, width),
    )
    if backward:
        scratch.update(
            d_s=low_vmem(count, width), back_s=low_vmem(count, width), log_s=low_vmem(count, BLK), turned=low_vmem(width, count)
        )
    if backward and remote:
        scratch.update(grads_in=low_vmem(peers, 2, half, width))
    if fetch is not None:
        ins.update(next_own=(fetch, ANY))
        outs.update(next_all=(low_shape(2 * peers, half, width), ANY))
        scratch.update(next_s=low_vmem(2 * peers, half, width))
    if reduces:
        ins.update(pack=(pack, ANY))
        outs.update(summed=(low_shape(half, width), ANY))
        scratch.update(scatter_scratch(peers, half, width))
    if remote:
        part = low_vmem(3, count // CUTS, width)
        scratch.update(back=part)
        if forward:
            scratch.update(stage_x=part)
        if backward:
            scratch.update(stage_d=part)
    return run_kernel(
        expert_part, ins, outs, scratch, forward + 2 * backward, count * width * inner, 48, 48 if remote else 0,
        forward=forward, backward=backward, remote=remote, hosted=hosted, reduces=reduces,
        fetches=fetch is not None, experts=experts,
    )


def experts_forward(plan, token_rows, experts, capacity, w, own, fetch):
    count = experts * capacity
    if experts == CUTS:
        got = expert_call(plan, experts, count, own=own, x=token_rows, fetch=fetch)
        return got.result, got
    got = expert_call(plan, experts, count, w=w, x=send_rows(plan[1], token_rows, experts, capacity))
    got.w = w
    return return_rows(plan[1], got.out, experts, capacity).astype(BF16), got


def experts_backward(plan, d_low, kept, route, experts, capacity, pack):
    count = experts * capacity
    if experts == CUTS:
        return expert_call(plan, experts, count, w=kept.w, g=d_low, kept=kept, route=route, pack=pack)
    d_sent = send_rows(plan[1], d_low, experts, capacity)
    got = expert_call(plan, experts, count, w=kept.w, g=d_sent, kept=kept, route=route)
    got.result = return_rows(plan[1], got.result, experts, capacity).astype(BF16)
    got.summed = scatter_all(pack)
    return got


def experts_both(w, own, plan, token_rows, d_low, route, experts, capacity):
    count = experts * capacity
    if experts == CUTS:
        return expert_call(plan, experts, count, own=own, x=token_rows, g=d_low, route=route)
    rows = send_rows(plan[1], token_rows, experts, capacity)
    d_sent = send_rows(plan[1], d_low, experts, capacity)
    got = expert_call(plan, experts, count, w=w, x=rows, g=d_sent, route=route)
    got.result = return_rows(plan[1], got.result, experts, capacity).astype(BF16)
    return got


def project_part(m, hosted):
    r = m.refs
    rows, w = r.n_s, r.w_s
    tokens = r.x.shape[0]
    peers = rows.shape[0] // tokens
    shard = w.shape[1] // peers
    c, t = m.c, m.t
    ready = m.greet([m.x_peer, m.y_peer] + ([m.sibling] if hosted else []))
    at = lambda index: pl.ds(pl.multiple_of(index * shard, shard), shard)
    first_load = m.local(r.x, rows.at[pl.ds(0, tokens)])
    loads = []
    if hosted:
        for i in range(4):
            loads.append(m.local(r.w.at[pl.ds(i * shard, shard)], w.at[i, at(t)]))
    else:
        for i in range(4):
            for j in range(peers):
                piece = r.w.at[i // 2, j, r.w.shape[2] - 1, pl.ds(i % 2 * shard, shard)]
                loads.append(m.local(piece, w.at[i, pl.ds(j * shard, shard)]))
    ready()
    half = tokens // 2
    m.need(first_load)
    cut = lambda j, part: pl.ds(j * tokens + part * half, half)

    def send(j, part, to, device):
        return m.remote(rows.at[cut(j, part)], rows.at[cut(to, part)], device)

    first, second, swaps, kept = {}, [], [], []
    if hosted:
        m.need(*loads)
        for h in range(2):
            mine = w.at[2 * c + h, at(t)]
            first[1, h] = m.remote(mine, mine, m.x_peer)
            first[2, h] = m.remote(mine, mine, m.y_peer)
    a_low, b_high = send(0, 0, 1, m.x_peer), send(0, 1, 2, m.y_peer)
    a_high, b_low = send(0, 1, 1, m.x_peer), send(0, 0, 2, m.y_peer)
    if hosted:
        for h in range(2):
            for k, onward, part in ((1, m.y_peer, 0), (2, m.x_peer, 1)):
                m.arrived(first[k, h])
                start = pl.multiple_of(xor_peer(t, k) * shard + part * (shard // 2), shard // 2)
                piece = w.at[2 * c + h, pl.ds(start, shard // 2)]
                second.append(m.remote(piece, piece, onward))
                whole = w.at[2 * c + h, at(xor_peer(t, k))]
                swaps.append(m.remote(whole, whole, m.sibling))
    m.arrived(a_low)
    c_low = send(1, 0, 3, m.y_peer)
    m.arrived(b_high)
    c_high = send(2, 1, 3, m.x_peer)
    if hosted:
        m.arrived(*second)
        for h in range(2):
            whole = w.at[2 * c + h, at(xor_peer(t, 3))]
            swaps.append(m.remote(whole, whole, m.sibling))
        m.arrived(*swaps)
    else:
        m.need(*loads)
    for i in range(4):
        kept.append(m.local(w.at[i], r.w_all.at[i]))

    def keys_values(start, size):
        here = pl.ds(start, size)
        x = rows[here, :]
        for i, near, far in ((1, r.k_s, r.k), (2, r.v_s, r.v)):
            near[here, :] = dot_nt(x, w[i]).astype(BF16)
            kept.append(m.local(near.at[here], far.at[here]))

    r.q_s[...] = dot_nt(rows[pl.ds(0, tokens), :], w[0]).astype(BF16)
    kept.append(m.local(r.q_s, r.q))
    keys_values(0, tokens)
    m.arrived(a_high)
    keys_values(tokens, tokens)
    m.arrived(b_low)
    keys_values(2 * tokens, tokens)
    m.arrived(c_low)
    keys_values(3 * tokens, half)
    m.arrived(c_high)
    keys_values(3 * tokens + half, half)
    kept.append(m.local(rows, r.n))
    m.finish()
    m.need(*kept)


def project(x, w, hosted, peers):
    tokens, width = x.shape
    every = peers * tokens
    outs = dict(
        q=(low_shape(tokens, width), ANY), k=(low_shape(every, width), ANY), v=(low_shape(every, width), ANY),
        n=(low_shape(every, width), ANY), w_all=(low_shape(4, width, width), ANY),
    )
    scratch = dict(
        n_s=low_vmem(every, width), w_s=low_vmem(4, width, width), q_s=low_vmem(tokens, width),
        k_s=low_vmem(every, width), v_s=low_vmem(every, width),
    )
    return run_kernel(
        project_part, dict(x=(x, ANY), w=(w, ANY)), outs, scratch, 6 + hosted, 9 * tokens * width * width, 40, 24, hosted=hosted
    )


def project_back_part(m, full, returns):
    r = m.refs
    tokens, width = r.dq_s.shape
    peers = r.dk_s.shape[0] // tokens
    shard = width // peers
    c, z = m.c, m.z
    local, remote, need, arrived = m.local, m.remote, m.need, m.arrived
    ready = m.greet([m.x_peer, m.y_peer] + ([m.sibling] if full else []) + (m.z_peers if full or returns else []))
    rows_of = lambda j: pl.ds(j * tokens, tokens)
    w = r.w_s
    weights_in = {i: local(r.w.at[i], w.at[i]) for i in (1, 2)}
    parts_in = {}
    for j in (3, 1, 2, 0):
        parts_in[j] = [local(a.at[rows_of(j)], b.at[rows_of(j)]) for a, b in ((r.dk, r.dk_s), (r.dv, r.dv_s))]
    above_in = local(r.above, r.above_s) if full else None
    rest_in = [local(a, b) for a, b in ((r.n, r.n_s), (r.dq, r.dq_s), (r.heads, r.heads_s), (r.d_att, r.d_att_s))]
    weights_in[0] = local(r.w.at[0], w.at[0])
    swaps_in = [local(e, r.e_s.at[l, c]) for l, e in enumerate((r.e0, r.e1))] if full else []
    ready()
    tops, ends = pl.ds(0, tokens // 2), pl.ds(tokens // 2, tokens // 2)

    def partial(j):
        at = rows_of(j)
        return dot(r.dk_s[at, :], w[1]) + dot(r.dv_s[at, :], w[2])

    over_x, over_y = {}, {}

    def rows_out(which):
        need(weights_in[1], weights_in[2])
        for j in which:
            stage = {1: r.p1, 2: r.p2, 3: r.p3}[j]
            need(*parts_in[j])
            stage[...] = partial(j).astype(BF16)
            if j != 2:
                over_x[j] = remote(stage.at[tops], r.row_in.at[j // 2], m.x_peer)
            if j != 1:
                over_y[j] = remote(stage.at[ends], r.row_in.at[2 + j // 3], m.y_peer)

    def rows_turn():
        arrived(over_x[3])
        r.p2[tops, :] = add_low(r.p2.at[tops], r.row_in.at[1]).astype(BF16)
        over_y[1] = remote(r.p2.at[tops], r.row_in.at[4], m.y_peer)
        arrived(over_y[3])
        r.p1[ends, :] = add_low(r.p1.at[ends], r.row_in.at[3]).astype(BF16)
        over_x[2] = remote(r.p1.at[ends], r.row_in.at[5], m.x_peer)

    def rows_own():
        need(*parts_in[0], weights_in[0], rest_in[1])
        r.dn[...] = partial(0) + dot(r.dq_s[...], w[0])

    def rows_end():
        for copy, slot, cut in ((over_x[1], 0, tops), (over_y[2], 2, ends), (over_y[1], 4, tops), (over_x[2], 5, ends)):
            arrived(copy)
            r.dn[cut, :] += r.row_in[slot].astype(F32)

    pack = r.pack_s
    part = lambda i: pl.ds(i % 2 * shard, shard)

    def weight_grad(i):
        need(*rest_in, weights_in[0], *[p for j in (3, 1, 2, 0) for p in parts_in[j]])
        if i == 0:
            g = dot_tn(r.dq_s[...], r.n_s[rows_of(0), :])
        elif i == 3:
            g = dot_tn(r.heads_s[...], r.d_att_s[...])
        else:
            g = dot_tn((r.dk_s if i == 1 else r.dv_s)[...], r.n_s[...])
        low = g.astype(BF16)
        for j in range(peers):
            pack[i // 2 * peers + j, part(i), :] = low[j * shard : (j + 1) * shard]
        return jnp.sum(g * w[i].astype(F32), axis=0, keepdims=True) if i < 3 else 0.0

    if not full:
        copies = {}
        if returns:
            size = r.out.shape[0] // CUTS
            out_in = local(r.out.at[pl.ds(0, size)], r.out_s)
            for k in (2, 3, 1):
                copies[k] = remote(r.out.at[pl.ds(k * size, size)], r.back.at[k - 1], m.z_peers[k - 1])
        rows_out((3, 1, 2))
        total = weight_grad(1)
        rows_turn()
        rows_own()
        total = total + weight_grad(2) + weight_grad(0) + weight_grad(3)
        r.att[...] = jnp.broadcast_to(total, r.att.shape)
        saved = local(pack, r.pack)
        if returns:
            need(out_in)
            r.result[...] = combine(m, r.slot_col, r.out_s, copies, r.back, size)
        rows_end()
        m.finish()
        need(saved)
        return

    mini = shard // 4
    at_z = lambda h, index: pl.ds(pl.multiple_of(h * shard + index * mini, mini), mini)
    both, z_in = r.both, r.z_in

    def z_out(source, layer, h):
        return [remote(source.at[at_z(h, xor_peer(z, k))], z_in.at[layer * 2 + h, k - 1], m.z_peers[k - 1]) for k in (1, 2, 3)]

    def z_sum(source, copies, layer, h):
        arrived(*copies)
        here = both.at[layer, c, at_z(h, z)]
        both[layer, c, at_z(h, z), :] = add_low(
            source.at[at_z(h, z)], *[z_in.at[layer * 2 + h, k] for k in range(3)]
        ).astype(BF16)
        return [remote(here, here, device) for device in m.z_peers]

    def core_out(copies, layer, h):
        arrived(*copies)
        here = both.at[layer, c, pl.ds(h * shard, shard)]
        return remote(here, here, m.sibling)

    scatter = Scatter(m, pack, r.core_in, r.g_in, r.piece)
    need(above_in)
    above = [z_out(r.above_s, 1, h) for h in range(2)]
    rows_out((3,))
    total = weight_grad(3) + weight_grad(1)
    scatter.swap(1)
    total = total + weight_grad(0) + weight_grad(2)
    scatter.swap(0)
    small_s, small_r = r.small_s, r.small_r
    row = lax.broadcasted_iota(jnp.int32, r.small.shape, 0)
    att_row = r.small_in.shape[0] // 2 - 1
    small_s[0] = jnp.where(row == att_row, total, r.small_in[...])
    small_1 = remote(small_s.at[0], small_r.at[0], m.sibling)
    scatter.out(1)
    scatter.out(0)
    above = [z_sum(r.above_s, above[h], 1, h) for h in range(2)]
    rows_out((1, 2))
    arrived(small_1)
    small_s[1] = small_s[0] + small_r[0]
    small_2 = remote(small_s.at[1], small_r.at[1], m.x_peer)
    scatter.turn(1)
    scatter.turn(0)
    rows_turn()
    above = [core_out(above[h], 1, h) for h in range(2)]
    need(*swaps_in)
    e_copies = [remote(r.e_s.at[l, c], r.e_s.at[l, c], m.sibling) for l in range(2)]
    rows_own()
    arrived(small_2)
    small_s[2] = small_s[1] + small_r[1]
    small_3 = remote(small_s.at[2], small_r.at[2], m.y_peer)
    scatter.end(1)
    piece_1 = z_out(r.piece, 0, 1)
    scatter.end(0)
    piece_0 = z_out(r.piece, 0, 0)
    arrived(small_3)
    small_s[3] = small_s[2] + small_r[2]
    last = [remote(small_s.at[3], small_r.at[2 + k], m.z_peers[k - 1]) for k in (1, 2, 3)]
    piece_1 = z_sum(r.piece, piece_1, 0, 1)
    piece_0 = z_sum(r.piece, piece_0, 0, 0)
    arrived(*above, *e_copies)
    saved = [local(both.at[1], r.g1), local(r.e_s, r.e)]
    piece_1 = core_out(piece_1, 0, 1)
    piece_0 = core_out(piece_0, 0, 0)
    rows_end()
    arrived(*last)
    r.small[...] = small_s[3] + small_r[3] + small_r[4] + small_r[5]
    arrived(piece_1, piece_0)
    saved.append(local(both.at[0], r.g0))
    m.finish()
    need(*saved)


def project_back(w, dq, dk, dv, normed_all, heads, d_att, above=None, small=None, swaps=None, out=None, slots=None):
    full, returns = above is not None, out is not None
    tokens, width = dq.shape
    rows = dk.shape[0]
    half = width // 2
    peers = rows // tokens
    shape = jax.ShapeDtypeStruct
    ins = dict(
        w=(w, ANY), dq=(dq, ANY), dk=(dk, ANY), dv=(dv, ANY), n=(normed_all, ANY), heads=(heads, ANY), d_att=(d_att, ANY),
    )
    outs = dict(dn=(shape((tokens, width), F32), VMEM))
    some, every = low_vmem(tokens, width), low_vmem(rows, width)
    scratch = dict(
        w_s=low_vmem(3, width, width), dq_s=some, dk_s=every, dv_s=every, n_s=every, heads_s=some, d_att_s=some,
        p1=some, p2=some, p3=some, row_in=low_vmem(6, tokens // 2, width),
    )
    if full:
        ins.update(above=(above, ANY), small_in=(small, VMEM), e0=(swaps[0], ANY), e1=(swaps[1], ANY))
        e_dims = (2, 2) + swaps[0].shape
        outs.update(
            g0=(low_shape(2, half, width), ANY), g1=(low_shape(2, half, width), ANY), e=(low_shape(*e_dims), ANY),
            small=(shape(small.shape, F32), VMEM),
        )
        scratch.update(
            scatter_scratch(peers, half, width), above_s=low_vmem(half, width), e_s=low_vmem(*e_dims),
            small_s=pltpu.VMEM((4,) + small.shape, F32), small_r=pltpu.VMEM((6,) + small.shape, F32),
            z_in=low_vmem(4, 3, half // 8, width), both=low_vmem(2, 2, half, width),
        )
    else:
        outs.update(pack=(low_shape(2 * peers, half, width), ANY), att=(shape((8, width), F32), VMEM))
        scratch.update(pack_s=low_vmem(2 * peers, half, width))
        if returns:
            ins.update(out=(out, ANY), slot_col=(slots[:, None], VMEM))
            outs.update(result=(low_shape(tokens, width), VMEM))
            size = out.shape[0] // CUTS
            scratch.update(out_s=low_vmem(size, width), back=low_vmem(3, size, width))
    return run_kernel(
        project_back_part, ins, outs, scratch, 4 + full, 4 * rows * width * width, 24, 64, full=full, returns=returns
    )


def inverse_rms(stream):
    return lax.rsqrt(jnp.mean(stream * stream, axis=-1, keepdims=True) + EPS)


def norm_backward(upstream, stream, inverse, gain):
    weighted = upstream * gain
    inner = jnp.mean(weighted * stream, axis=-1, keepdims=True)
    return inverse * weighted - stream * (inverse * inverse * inverse) * inner


def path_table(segment_ids, path_pos, parent_ids, peers):
    segment = segment_ids[::BLK].reshape(peers, -1)
    position = path_pos[::BLK].reshape(peers, -1)
    t = lax.axis_index(TENSOR)
    order = jnp.arange(peers, dtype=jnp.int32) ^ t
    match = order[:, None] == jnp.arange(peers, dtype=jnp.int32)[None, :]
    pick = lambda v: jnp.sum(jnp.where(match[:, :, None], v[None], 0), axis=1)
    segment, position = pick(segment), pick(position)
    place = jnp.where(segment == 0, position // BLK, segment + (TRUNK - 1))
    seg, pos, own = segment[0], position[0], place[0]
    names = jnp.arange(parent_ids.shape[-1], dtype=jnp.int32)
    parent = jnp.sum(jnp.where(seg[:, None] == names[None, :], parent_ids[0][None], 0), axis=1)
    leaf = (seg > 0) & (parent > 0)
    parent_place = jnp.where(leaf, parent + (TRUNK - 1), own)
    base_own = jnp.where(seg > 0, pos, BIG)
    base_parent = jnp.where(leaf, TRUNK * BLK, BIG)
    mine = jnp.stack([pos, own, parent_place, base_own, base_parent], axis=1)
    return jnp.concatenate([place.reshape(-1), mine.reshape(-1)]).astype(jnp.int32)


def dispatch_plan(route, experts, capacity):
    count = route.shape[0]
    chosen = route[:, None] == jnp.arange(experts, dtype=jnp.int32)[None, :]
    index = jnp.arange(count, dtype=jnp.int32)
    before = (index[None, :] < index[:, None]).astype(BF16)
    ranks = dot(before, chosen.astype(BF16)).astype(jnp.int32)
    rank = jnp.sum(jnp.where(chosen, ranks, 0), axis=1)
    to = route ^ lax.axis_index(EXPERT) if experts == 4 else route
    slot = to * capacity + rank
    table = slot[None, :] == jnp.arange(experts * capacity, dtype=jnp.int32)[:, None]
    return chosen, (slot, table.astype(BF16))


def send_rows(table, rows, experts, capacity):
    chunks = [
        dot(table[k * capacity : (k + 1) * capacity], rows).astype(BF16) for k in range(experts)
    ]
    return jnp.concatenate(exchange(chunks), axis=0)


def return_rows(table, results, experts, capacity):
    chunks = exchange([results[k * capacity : (k + 1) * capacity] for k in range(experts)])
    return dot_tn(table, jnp.concatenate(chunks, axis=0))


def own_half(x):
    half = x.shape[0] // 2
    return lax.dynamic_slice_in_dim(x, lax.axis_index(DP) * half, half, 0)


def gather_all(x):
    out = lax.all_gather(x, (DP, TENSOR), axis=0)
    return out.reshape((lax.axis_size(DP), lax.axis_size(TENSOR)) + x.shape)


def scatter_experts(x):
    if x.ndim == 4:
        return lax.psum_scatter(x, TENSOR, scatter_dimension=0, tiled=True)[0]
    return scatter_all(x)


def scatter_all(x):
    flat = x.reshape((-1,) + x.shape[2:])
    return lax.psum_scatter(flat, (DP, TENSOR), scatter_dimension=0, tiled=True)[0]


def pack_attention(w_mix, w_proj):
    width = w_mix.shape[0]
    return jnp.concatenate([w_mix.transpose(1, 2, 0).reshape(-1, width), w_proj], axis=0)


def pack_experts(w_up, w_back):
    return jnp.stack([own_half(w_up), own_half(w_back)])


def swap_cores(half):
    return lax.all_gather(half, DP, axis=0)


def body(
    hidden_in, route_ids, segment_ids, path_pos, parent_ids, norm_att, w_qkv, w_out, norm_ffn, w_route, w_in, w_down, cotangent,
):
    depth_total = w_qkv.shape[0]
    tokens, width = hidden_in.shape
    experts = w_route.shape[-1]
    capacity = 3 * tokens // (2 * experts)
    peers = lax.axis_size(TENSOR)
    shard = width // peers
    table = path_table(segment_ids, path_pos, parent_ids, peers)
    plans = [dispatch_plan(route_ids[d, :, 0], experts, capacity) for d in range(depth_total)]
    routes = [jnp.pad(w_route[d], ((0, 0), (0, BLK - experts))) for d in range(depth_total)]
    cotangent = cotangent.astype(F32)

    stream = hidden_in.astype(F32)
    kept = []
    packed = [pack_attention(w_qkv[d], w_out[d]) for d in range(depth_total)]
    own = [(w_in[d, 0], w_down[d, 0]) for d in range(depth_total)]
    weights = None
    for depth in range(depth_total):
        gain_att, gain_ffn = norm_att[depth].astype(F32), norm_ffn[depth].astype(F32)
        chosen, plan = plans[depth]
        last = depth + 1 == depth_total
        inverse_att = inverse_rms(stream)
        normed = (stream * inverse_att * gain_att).astype(BF16)
        proj = project(normed, packed[0] if depth == 0 else weights, depth == 0, peers)
        w_here = None if experts == CUTS else gather_all(pack_experts(*own[depth]))
        heads, lse = attend(table, proj.q, proj.k, proj.v)
        after_att = stream + dot(heads, proj.w_all[3])
        inverse_ffn = inverse_rms(after_att)
        token_rows = (after_att * inverse_ffn * gain_ffn).astype(BF16)
        router = jax.nn.softmax(dot(token_rows, w_route[depth]), axis=-1)
        gate = jnp.sum(jnp.where(chosen, router, 0.0), axis=1, keepdims=True)
        if last:
            d_low = (gate * cotangent).astype(BF16)
            held = experts_both(w_here, own[depth], plan, token_rows, d_low, routes[depth], experts, capacity)
            if experts != CUTS:
                back = return_rows(plan[1], held.out, experts, capacity).astype(BF16)
        else:
            back, held = experts_forward(plan, token_rows, experts, capacity, w_here, own[depth], packed[depth + 1])
            if experts == CUTS:
                weights = held.next_all.reshape((2, peers, 1) + held.next_all.shape[1:])
            else:
                weights = gather_all(own_half(packed[depth + 1]))[:, :, None]
        kept.append((stream, inverse_att, proj, heads, lse, after_att, inverse_ffn, gate, held))
        if not last:
            stream = after_att + gate * back.astype(F32)

    upstream = cotangent
    grads_e, grads_a, smalls = [None] * depth_total, [None] * depth_total, [None] * depth_total
    above = None
    for depth in reversed(range(depth_total)):
        stream, inverse_att, proj, heads, lse, after_att, inverse_ffn, gate, held = kept[depth]
        gain_att, gain_ffn = norm_att[depth].astype(F32), norm_ffn[depth].astype(F32)
        chosen, plan = plans[depth]
        last = depth + 1 == depth_total
        if not last:
            d_low = (gate * upstream).astype(BF16)
            held = experts_backward(plan, d_low, held, routes[depth], experts, capacity, above)
            above = held.summed
        dx1 = upstream + norm_backward(held.result.astype(F32), after_att, inverse_ffn, gain_ffn)
        d_att = dx1.astype(BF16)
        d_heads = dot_nt(d_att, proj.w_all[3]).astype(BF16)
        dq, dk, dv = attend_back(table, proj.q, proj.k, proj.v, d_heads, heads, lse)
        args = (proj.w_all, dq, dk, dv, proj.n, heads, d_att)
        if depth == 0 and experts == CUTS:
            grads_e[0] = scatter_experts(held.grads)
            lines = lambda n: jnp.zeros((n, width), F32)
            part = jnp.concatenate([held.small[: experts + 1], lines(3), smalls[1], lines(2)], axis=0)
            got = project_back(*args, above=above, small=part, swaps=grads_e)
            grads_a = [got.g0, got.g1]
            grads_e = [got.e[0], got.e[1]]
            total = got.small
            small = jnp.stack([
                jnp.concatenate([total[: experts + 1], total[7:8]], axis=0), total[8 : 8 + experts + 2]
            ])
        else:
            if last and experts == CUTS:
                got = project_back(*args, out=held.out, slots=plan[0])
                back = got.result
            else:
                got = project_back(*args)
            if last:
                hidden_out = (after_att + gate * back.astype(F32)).astype(BF16)
            if above is not None:
                grads_a[depth + 1] = swap_cores(lax.psum(above, EXPERT))
            above = got.pack.reshape((2, peers) + got.pack.shape[1:])
            if experts == CUTS:
                above = got.pack
            smalls[depth] = jnp.concatenate([held.small[: experts + 1], got.att[:1]], axis=0)
            grads_e[depth] = scatter_experts(after(held.grads, got.dn))
            if depth == 0:
                grads_a[0] = swap_cores(lax.psum(scatter_all(above), EXPERT))
                small = sum_small(jnp.stack(smalls))
                grads_e = [swap_cores(g) for g in grads_e]
        upstream = dx1 + norm_backward(got.dn, stream, inverse_att, gain_att)
    grad_up, grad_down = [
        jnp.stack([g[:, i].reshape(width, width) for g in grads_e])[:, None].astype(F32) for i in range(2)
    ]
    grads_a = jnp.stack([g.reshape(width, width) for g in grads_a]).astype(F32)
    grad_mix = grads_a[:, : 3 * shard].reshape(depth_total, 3, shard, width).transpose(0, 3, 1, 2)
    grad_out = grads_a[:, 3 * shard :]
    grad_route = small[:, :experts].transpose(0, 2, 1)
    grad_ffn = small[:, experts] / norm_ffn.astype(F32)
    grad_att = small[:, experts + 1] / norm_att.astype(F32)
    return (hidden_out, upstream, grad_att, grad_mix, grad_out, grad_ffn, grad_route, grad_up, grad_down)


def solution(mesh):
    in_specs = (
        P((DP, EXPERT, TENSOR), None),
        P(None, (DP, EXPERT, TENSOR), None),
        P((DP, EXPERT)),
        P((DP, EXPERT)),
        P((DP, EXPERT), None),
        P(),
        P(None, None, None, TENSOR),
        P(None, TENSOR, None),
        P(),
        P(),
        P(None, EXPERT, None, TENSOR),
        P(None, EXPERT, TENSOR, None),
        P((DP, EXPERT, TENSOR), None),
    )
    out_specs = (
        P((DP, EXPERT, TENSOR), None),
        P((DP, EXPERT, TENSOR), None),
        P(),
        P(None, None, None, TENSOR),
        P(None, TENSOR, None),
        P(),
        P(),
        P(None, EXPERT, None, TENSOR),
        P(None, EXPERT, TENSOR, None),
    )
    return jax.shard_map(body, mesh=mesh, in_specs=in_specs, out_specs=out_specs, check_vma=False)
```

```python
from types import SimpleNamespace

import jax
import jax.numpy as jnp
from jax import lax
from jax.experimental import pallas as pl
from jax.experimental.pallas import tpu as pltpu
from jax.sharding import PartitionSpec as P

HEAD_DIM = 64
BLK = 128
TRUNK = 8
PAIR = 2 * HEAD_DIM
EPS = 1e-06
NEG = -1000000000.0
BIG = 1 << 20
F32 = jnp.float32
BF16 = jnp.bfloat16
VMEM_LIMIT = 58 * 1024 * 1024
DP, EXPERT, TENSOR = "dp", "expert", "tensor"

NT = (((1,), (1,)), ((), ()))
TN = (((0,), (0,)), ((), ()))


def dot(a, b):
    return jnp.dot(a, b, preferred_element_type=F32)


def dot_nt(a, b):
    return lax.dot_general(a, b, NT, preferred_element_type=F32)


def dot_tn(a, b):
    return lax.dot_general(a, b, TN, preferred_element_type=F32)


def cost(macs, moved, trans=0):
    return pl.CostEstimate(flops=macs // 64, bytes_accessed=moved // 64, transcendentals=0)


def xperm(x, axis, k):
    n = lax.axis_size(axis)
    return lax.ppermute(x, axis, [(i, i ^ k) for i in range(n)])


def after(x, dep):
    return lax.optimization_barrier((x, dep))[0]


def sum_small(x):
    for axis in (DP, TENSOR, EXPERT):
        n = lax.axis_size(axis)
        k = 1
        while k < n:
            x = x + xperm(x, axis, k)
            k *= 2
    return x


def exchange(chunks):
    n = len(chunks)
    if n == 4:
        return [chunks[0]] + [xperm(chunks[k], EXPERT, k) for k in range(1, n)]
    out = lax.all_to_all(jnp.stack(chunks), EXPERT, split_axis=0, concat_axis=0, tiled=True)
    return [out[k] for k in range(n)]


def masked_pair(x):
    lane = lax.broadcasted_iota(jnp.int32, x.shape, 1)
    zero = jnp.zeros_like(x)
    return jnp.concatenate([jnp.where(lane < HEAD_DIM, x, zero), jnp.where(lane < HEAD_DIM, zero, x)], axis=0)


def path_spans(table, at, trunk):
    own, parent, base_own, base_parent = [table[at + j] for j in range(1, 5)]
    block = lambda place: pl.ds(pl.multiple_of(place * BLK, BLK), BLK)
    return [(pl.ds(0, trunk), 0), (block(parent), base_parent), (block(own), base_own)]


def attend_kernel(table, q_ref, k_ref, v_ref, out_ref, lse_ref, keys, values_t):
    blocks = k_ref.shape[0] // BLK
    mine = q_ref.shape[0] // BLK
    trunk = TRUNK * BLK
    for b in range(blocks):
        place = pl.ds(pl.multiple_of(table[b] * BLK, BLK), BLK)
        rows = pl.ds(b * BLK, BLK)
        keys[place, :] = k_ref[rows, :]
        values_t[pl.ds(0, PAIR), place] = v_ref[rows, :].T
    values_t[pl.ds(PAIR, 16), :] = jnp.ones((16, blocks * BLK), BF16)
    lane = lax.broadcasted_iota(jnp.int32, (BLK, PAIR), 1)

    def scores_of(i):
        at = blocks + 5 * i
        q = masked_pair(q_ref[pl.ds(i * BLK, BLK), :] * jnp.asarray(HEAD_DIM ** -0.5, BF16))
        pos_q = table[at] + lax.broadcasted_iota(jnp.int32, (1, 2 * BLK), 1) % BLK
        parts = []
        for here, base in path_spans(table, at, trunk):
            scores = dot_nt(keys[here, :], q)
            key_pos = base + lax.broadcasted_iota(jnp.int32, (here.size, 1), 0)
            parts.append(jnp.where(key_pos <= pos_q, scores, NEG))
        top = parts[0].max(axis=0, keepdims=True)
        for part in parts[1:]:
            top = jnp.maximum(top, part.max(axis=0, keepdims=True))
        return parts, top

    coming = scores_of(0)
    for i in range(mine):
        parts, top = coming
        if i + 1 < mine:
            coming = scores_of(i + 1)
        rows = pl.ds(i * BLK, BLK)
        both = jnp.zeros((PAIR + 16, 2 * BLK), F32)
        for (here, _), part in zip(path_spans(table, blocks + 5 * i, trunk), parts):
            both = both + dot(values_t[:, here], jnp.exp(part - top).astype(BF16))
        total = both[PAIR : PAIR + 1]
        heads = (both[:PAIR] / total).T
        lse = top + jnp.log(total)
        out_ref[rows, :] = jnp.where(lane < HEAD_DIM, heads[:BLK], heads[BLK:]).astype(BF16)
        lse_ref[0, pl.ds(0, 1), rows] = lse[:, :BLK]
        lse_ref[0, pl.ds(1, 1), rows] = lse[:, BLK:]


def attend(table, q, k, v):
    mine, width = q.shape
    rows = k.shape[0]
    pairs = width // PAIR
    column = lambda n: pl.BlockSpec((n, PAIR), lambda p, table: (0, p))
    return pl.pallas_call(
        attend_kernel,
        grid_spec=pltpu.PrefetchScalarGridSpec(
            num_scalar_prefetch=1,
            grid=(pairs,),
            in_specs=[column(mine), column(rows), column(rows)],
            out_specs=[column(mine), pl.BlockSpec((1, 8, mine), lambda p, table: (p, 0, 0))],
            scratch_shapes=[pltpu.VMEM((rows, PAIR), BF16), pltpu.VMEM((PAIR + 16, rows), BF16)],
        ),
        out_shape=[jax.ShapeDtypeStruct((mine, width), BF16), jax.ShapeDtypeStruct((pairs, 8, mine), F32)],
        compiler_params=pltpu.CompilerParams(vmem_limit_bytes=VMEM_LIMIT),
        cost_estimate=cost(mine * 1280 * width * 8, 4 * rows * width, mine * 1280 * width // HEAD_DIM),
        name="attend",
    )(table, q, k, v)


def attend_back_kernel(
    table, q_ref, k_ref, v_ref, do_ref, o_ref, lse_ref, dq_ref, dk_ref, dv_ref, keys, values, keys_t, dk_acc, dv_acc,
):
    blocks = k_ref.shape[0] // BLK
    mine = q_ref.shape[0] // BLK
    trunk = TRUNK * BLK
    for b in range(blocks):
        place = pl.ds(pl.multiple_of(table[b] * BLK, BLK), BLK)
        rows = pl.ds(b * BLK, BLK)
        keys[place, :] = k_ref[rows, :]
        values[place, :] = v_ref[rows, :]
        keys_t[:, place] = k_ref[rows, :].T
    dk_acc[...] = jnp.zeros_like(dk_acc)
    dv_acc[...] = jnp.zeros_like(dv_acc)
    lane = lax.broadcasted_iota(jnp.int32, (BLK, PAIR), 1)

    def weights_of(i):
        at = blocks + 5 * i
        rows = pl.ds(i * BLK, BLK)
        q = masked_pair(q_ref[rows, :] * jnp.asarray(HEAD_DIM ** -0.5, BF16))
        do = do_ref[rows, :]
        product = (do.astype(F32) * o_ref[rows, :].astype(F32)).T
        inner = jnp.concatenate(
            [jnp.sum(product[:HEAD_DIM], axis=0, keepdims=True), jnp.sum(product[HEAD_DIM:], axis=0, keepdims=True)], axis=1
        )
        do = masked_pair(do)
        lse = jnp.concatenate([lse_ref[0, pl.ds(0, 1), rows], lse_ref[0, pl.ds(1, 1), rows]], axis=1)
        pos_q = table[at] + lax.broadcasted_iota(jnp.int32, (1, 2 * BLK), 1) % BLK
        parts = []
        for here, base in path_spans(table, at, trunk):
            scores = dot_nt(keys[here, :], q)
            key_pos = base + lax.broadcasted_iota(jnp.int32, (here.size, 1), 0)
            weights = jnp.exp(jnp.where(key_pos <= pos_q, scores - lse, NEG))
            d_weights = dot_nt(values[here, :], do)
            parts.append((weights.astype(BF16), (weights * (d_weights - inner)).astype(BF16)))
        return q, do, parts

    coming = weights_of(0)
    for i in range(mine):
        q, do, parts = coming
        if i + 1 < mine:
            coming = weights_of(i + 1)
        dq_t = jnp.zeros((PAIR, 2 * BLK), F32)
        for (here, _), (weights, d_scores) in zip(path_spans(table, blocks + 5 * i, trunk), parts):
            dv_acc[here, :] += dot(weights, do)
            dk_acc[here, :] += dot(d_scores, q)
            dq_t = dq_t + dot(keys_t[:, here], d_scores)
        dq = dq_t.T * (HEAD_DIM ** -0.5)
        dq_ref[pl.ds(i * BLK, BLK), :] = jnp.where(lane < HEAD_DIM, dq[:BLK], dq[BLK:]).astype(BF16)
    for b in range(blocks):
        place = pl.ds(pl.multiple_of(table[b] * BLK, BLK), BLK)
        rows = pl.ds(b * BLK, BLK)
        dk_ref[rows, :] = dk_acc[place, :].astype(BF16)
        dv_ref[rows, :] = dv_acc[place, :].astype(BF16)


def attend_back(table, q, k, v, d_heads, heads, lse):
    mine, width = q.shape
    rows = k.shape[0]
    pairs = width // PAIR
    column = lambda n: pl.BlockSpec((n, PAIR), lambda p, table: (0, p))
    return pl.pallas_call(
        attend_back_kernel,
        grid_spec=pltpu.PrefetchScalarGridSpec(
            num_scalar_prefetch=1,
            grid=(pairs,),
            in_specs=[
                column(mine), column(rows), column(rows), column(mine), column(mine),
                pl.BlockSpec((1, 8, mine), lambda p, table: (p, 0, 0)),
            ],
            out_specs=[column(mine), column(rows), column(rows)],
            scratch_shapes=[
                pltpu.VMEM((rows, PAIR), BF16),
                pltpu.VMEM((rows, PAIR), BF16),
                pltpu.VMEM((PAIR, rows), BF16),
                pltpu.VMEM((rows, PAIR), F32),
                pltpu.VMEM((rows, PAIR), F32),
            ],
        ),
        out_shape=[
            jax.ShapeDtypeStruct((mine, width), BF16),
            jax.ShapeDtypeStruct((rows, width), BF16),
            jax.ShapeDtypeStruct((rows, width), BF16),
        ],
        compiler_params=pltpu.CompilerParams(vmem_limit_bytes=VMEM_LIMIT),
        cost_estimate=cost(mine * 1280 * width * 20, 8 * rows * width, mine * 1280 * width // HEAD_DIM),
        name="attend_back",
    )(table, q, k, v, d_heads, heads, lse)


GELU_C = 0.7978845608028654
GELU_A = 0.044715
CUTS = 4
MESH = pl.DeviceIdType.MESH
ANY = pl.BlockSpec(memory_space=pl.ANY)
VMEM = pl.BlockSpec(memory_space=pltpu.VMEM)


def low_shape(*dims):
    return jax.ShapeDtypeStruct(dims, BF16)


def low_vmem(*dims):
    return pltpu.VMEM(dims, BF16)


def run_kernel(body, ins, outs, scratch, identity, macs, near, far, **flags):
    scratch = dict(scratch, near=pltpu.SemaphoreType.DMA((near,)))
    params = dict(vmem_limit_bytes=VMEM_LIMIT)
    if far:
        scratch.update(send=pltpu.SemaphoreType.DMA((far,)), recv=pltpu.SemaphoreType.DMA((far,)))
        params.update(collective_id=identity, has_side_effects=True)
    names = [*ins, *outs, *scratch]

    def kernel(*refs):
        body(Moves(SimpleNamespace(**dict(zip(names, refs)))), **flags)

    results = pl.pallas_call(
        kernel,
        in_specs=[spec for _, spec in ins.values()],
        out_specs=[spec for _, spec in outs.values()],
        out_shape=[shape for shape, _ in outs.values()],
        scratch_shapes=list(scratch.values()),
        compiler_params=pltpu.CompilerParams(**params),
        cost_estimate=cost(macs, 0),
        name=body.__name__,
    )(*[value for value, _ in ins.values()])
    return SimpleNamespace(**dict(zip(outs, results)))


def xor_peer(index, k):
    if k == 1:
        return index + 1 - 2 * lax.rem(index, 2)
    if k == 2:
        return index + 2 - 4 * lax.rem(lax.div(index, 2), 2)
    return index + 3 - 2 * lax.rem(index, 4)


class Moves:
    def __init__(self, refs):
        self.refs, self.near, self.far, self.seen, self.left, self.sent = refs, 0, 0, set(), set(), []
        self.c, self.t, self.z = [lax.axis_index(axis) for axis in (DP, TENSOR, EXPERT)]
        self.x_peer, self.y_peer = [{TENSOR: xor_peer(self.t, k)} for k in (1, 2)]
        self.sibling = {DP: 1 - self.c}
        self.z_peers = [{EXPERT: xor_peer(self.z, k)} for k in (1, 2, 3)]

    def local(self, src, dst):
        copy = pltpu.make_async_copy(src, dst, self.refs.near.at[self.near])
        self.near += 1
        copy.start()
        return copy

    def remote(self, src, dst, device):
        copy = pltpu.make_async_remote_copy(
            src_ref=src, dst_ref=dst, send_sem=self.refs.send.at[self.far], recv_sem=self.refs.recv.at[self.far],
            device_id=device, device_id_type=MESH,
        )
        self.far += 1
        copy.start()
        self.sent.append(copy)
        return copy

    def need(self, *copies):
        for copy in copies:
            if id(copy) not in self.seen:
                self.seen.add(id(copy))
                copy.wait()

    def arrived(self, *copies):
        for copy in copies:
            if id(copy) not in self.seen:
                self.seen.add(id(copy))
                copy.wait_recv()

    def finish(self):
        self.gone(*self.sent)

    def gone(self, *copies):
        for copy in copies:
            if id(copy) not in self.left:
                self.left.add(id(copy))
                copy.wait_send()

    def greet(self, devices):
        barrier = pltpu.get_barrier_semaphore()
        for device in devices:
            pl.semaphore_signal(barrier, inc=1, device_id=device, device_id_type=MESH)
        return lambda: pl.semaphore_wait(barrier, len(devices))


def add_low(ref, *more):
    total = ref[...].astype(F32)
    for other in more:
        total = total + other[...].astype(F32)
    return total


class Scatter:
    def __init__(self, moves, pack, core_in, g_in, piece):
        self.moves, self.pack, self.core_in, self.g_in, self.piece = moves, pack, core_in, g_in, piece
        self.peers = lax.axis_size(TENSOR)
        self.size = pack.shape[1] // 2
        c, t = moves.c, moves.t
        self.index = [t] + [xor_peer(t, k) for k in (1, 2, 3)]
        self.slots = self.index if core_in is None else [c * self.peers + i for i in self.index]
        self.flow = [dict(), dict()]

    def rows(self, h):
        return pl.ds(h * self.size, self.size)

    def sides(self, h):
        half = self.size // 2
        return pl.ds(h * self.size, half), pl.ds(h * self.size + half, half)

    def swap(self, h):
        m = self.moves
        there = pl.ds((1 - m.c) * self.peers, self.peers)
        self.flow[h][0] = m.remote(self.pack.at[there, self.rows(h)], self.core_in.at[:, self.rows(h)], m.sibling)

    def out(self, h):
        m, pack, slots, f = self.moves, self.pack, self.slots, self.flow[h]
        left, right = self.sides(h)
        if self.core_in is not None:
            m.arrived(f[0])
            for j in (3, 1, 2, 0):
                pack[slots[j], self.rows(h), :] = add_low(
                    pack.at[slots[j], self.rows(h)], self.core_in.at[self.index[j], self.rows(h)]
                ).astype(BF16)
        f[1] = m.remote(pack.at[slots[3], left], self.g_in.at[h, 0], m.x_peer)
        f[2] = m.remote(pack.at[slots[3], right], self.g_in.at[h, 1], m.y_peer)
        f[3] = m.remote(pack.at[slots[1], left], self.g_in.at[h, 2], m.x_peer)
        f[4] = m.remote(pack.at[slots[2], right], self.g_in.at[h, 3], m.y_peer)

    def turn(self, h):
        m, pack, slots, f = self.moves, self.pack, self.slots, self.flow[h]
        left, right = self.sides(h)
        m.arrived(f[1])
        pack[slots[2], left, :] = add_low(pack.at[slots[2], left], self.g_in.at[h, 0]).astype(BF16)
        f[5] = m.remote(pack.at[slots[2], left], self.g_in.at[h, 4], m.y_peer)
        m.arrived(f[2])
        pack[slots[1], right, :] = add_low(pack.at[slots[1], right], self.g_in.at[h, 1]).astype(BF16)
        f[6] = m.remote(pack.at[slots[1], right], self.g_in.at[h, 5], m.x_peer)

    def end(self, h):
        f = self.flow[h]
        self.moves.arrived(f[3], f[4], f[5], f[6])
        for cut, a, b in zip(self.sides(h), (2, 3), (4, 5)):
            total = add_low(self.pack.at[self.slots[0], cut], self.g_in.at[h, a], self.g_in.at[h, b])
            self.piece[cut, :] = total.astype(BF16)


class ExpertScatter:
    def __init__(self, moves, pack, own, keep, inbox):
        self.m, self.pack, self.own, self.keep, self.inbox = moves, pack, own, keep, inbox
        half = own.shape[1] // 2
        self.left, self.right = pl.ds(0, half), pl.ds(half, half)
        self.index = [moves.t] + [xor_peer(moves.t, k) for k in (1, 2, 3)]

    def load(self):
        p, i, m = self.pack, self.index, self.m
        return [
            m.local(p.at[i[0]], self.own),
            m.local(p.at[i[2], :, self.left], self.keep.at[0]),
            m.local(p.at[i[1], :, self.right], self.keep.at[1]),
        ]

    def out(self):
        p, i, m = self.pack, self.index, self.m
        self.flow = [
            m.remote(p.at[i[3], :, self.left], self.inbox.at[0], m.x_peer),
            m.remote(p.at[i[3], :, self.right], self.inbox.at[1], m.y_peer),
            m.remote(p.at[i[1], :, self.left], self.inbox.at[2], m.x_peer),
            m.remote(p.at[i[2], :, self.right], self.inbox.at[3], m.y_peer),
        ]

    def turn(self):
        m = self.m
        self.second = []
        for n, device in enumerate((m.y_peer, m.x_peer)):
            if self.flow:
                m.arrived(self.flow[n])
            self.keep[n] = add_low(self.keep.at[n], self.inbox.at[n]).astype(BF16)
            self.second.append(m.remote(self.keep.at[n], self.inbox.at[4 + n], device))

    def end(self):
        self.m.arrived(*self.flow, *self.second)
        for n, cut in enumerate((self.left, self.right)):
            self.own[:, cut, :] = add_low(self.own.at[:, cut], self.inbox.at[2 + n], self.inbox.at[4 + n]).astype(BF16)


def expert_scatter_scratch(half, width):
    return dict(e_own=low_vmem(2, half, width), e_keep=low_vmem(2, 2, half // 2, width), e_in=low_vmem(6, 2, half // 2, width))


class Gather:
    def __init__(self, moves, pack):
        self.moves, self.pack = moves, pack
        self.half = pack.shape[1] // 2
        self.slots = [moves.c * (pack.shape[0] // 2) + i for i in [moves.t] + [xor_peer(moves.t, k) for k in (1, 2, 3)]]

    def out(self):
        own = self.pack.at[self.slots[0]]
        self.first = [self.moves.remote(own, own, device) for device in (self.moves.x_peer, self.moves.y_peer)]

    def turn(self):
        m = self.moves
        self.swaps, self.second = [], []
        for k, device in ((1, m.y_peer), (2, m.x_peer)):
            m.arrived(self.first[k - 1])
            piece = self.pack.at[self.slots[k], pl.ds((k - 1) * self.half, self.half)]
            self.second.append(m.remote(piece, piece, device))
            self.swap(k)

    def swap(self, k):
        whole = self.pack.at[self.slots[k]]
        self.swaps.append(self.moves.remote(whole, whole, self.moves.sibling))

    def end(self):
        self.moves.arrived(*self.second)
        self.swap(3)
        self.moves.arrived(*self.swaps)


def attention_rows(r, depth, i):
    return r.w_qkv.at[depth, i] if i < 3 else r.w_out.at[depth]


def scatter_scratch(peers, half, width):
    return dict(
        pack_s=low_vmem(2 * peers, half, width), core_in=low_vmem(peers, half, width),
        g_in=low_vmem(2, 6, half // 4, width), piece=low_vmem(half, width),
    )


def one_hot(slot_row, k, size):
    index = lax.broadcasted_iota(jnp.int32, (size, slot_row.shape[1]), 0) + k * size
    return jnp.where(index == slot_row[...], 1.0, 0.0).astype(BF16)


def one_hot_turned(slot_col, k, size):
    index = lax.broadcasted_iota(jnp.int32, (slot_col.shape[0], size), 1) + k * size
    return jnp.where(index == slot_col[...], 1.0, 0.0).astype(BF16)


def combine(m, slot_col, source, copies, back, size):
    total = dot(one_hot_turned(slot_col, 0, size), source[pl.ds(0, size), :])
    for k in (1, 2, 3):
        m.arrived(copies[k])
        total = total + dot(one_hot_turned(slot_col, k, size), back[k - 1])
    return total.astype(BF16)


def expert_part(m, forward, backward, remote, hosted, reduces, fetches, experts, depth):
    r = m.refs
    if hosted:
        own_up, own_down = r.w_in.at[depth, 0], r.w_down.at[depth, 0]
    up, down, hidden, slope, rows, outs = r.up, r.down, r.hidden_s, r.slope_s, r.rows_s, r.outs_s
    count, width = rows.shape
    inner = up.shape[1]
    half = width // 2
    peers = inner // width
    size = count // CUTS
    tile = 256
    cuts = [pl.ds(k * size, size) for k in range(CUTS)]
    met = []
    if remote:
        met += m.z_peers
    if hosted or reduces:
        met += [m.x_peer, m.y_peer]
    if remote:
        met += [m.sibling]
    ready = m.greet(met) if met else None

    def up_at(c, t, start=0, rows=half):
        return up.at[pl.ds(pl.multiple_of(c * half + start, half // 2), rows), pl.ds(pl.multiple_of(t * width, width), width)]

    def down_at(c, t, start=0, rows=half):
        return down.at[pl.ds(pl.multiple_of(t * width + c * half + start, half // 2), rows)]

    loads, weight_loads = [], []
    if not remote:
        if forward:
            loads.append(m.local(r.x, rows))
        if backward:
            loads.append(m.local(r.g, r.d_s))
    if hosted:
        weight_loads.append(m.local(own_up, up.at[:, pl.ds(pl.multiple_of(m.t * width, width), width)]))
        weight_loads.append(m.local(own_down, down.at[pl.ds(pl.multiple_of(m.t * width, width), width)]))
    else:
        for t in range(peers):
            for c in range(2):
                weight_loads += [m.local(r.w.at[c, t, 0], up_at(c, t)), m.local(r.w.at[c, t, 1], down_at(c, t))]
    if backward and not forward:
        loads += [m.local(a, b) for a, b in ((r.rows, rows), (r.out, outs), (r.slope, slope), (r.hidden, hidden))]
    if ready:
        ready()

    def dispatch(source, target, stage):
        copies = {}
        x = source[...]
        for k in (2, 1, 3):
            stage[k - 1] = dot(one_hot(r.slot_row, k, size), x).astype(BF16)
            copies[k] = m.remote(stage.at[k - 1], target.at[cuts[k]], m.z_peers[k - 1])
        target[cuts[0], :] = dot(one_hot(r.slot_row, 0, size), x).astype(BF16)
        return copies

    def give_back(source, k):
        return m.remote(source.at[cuts[k]], r.back.at[k - 1], m.z_peers[k - 1])

    def forward_block(cut, at):
        u = dot(rows[cut, :], up[:, at])
        square = u * u
        gate = 0.5 + 0.5 * jnp.tanh(u * (GELU_C + (GELU_C * GELU_A) * square))
        value = u * gate
        hidden[cut, at] = value.astype(BF16)
        grow = gate + value * (1.0 - gate) * (2 * GELU_C + (6 * GELU_C * GELU_A) * square)
        slope[cut, at] = grow.astype(BF16)

    def forward_peer(cut, t):
        for col in range(0, width, tile):
            forward_block(cut, pl.ds(pl.multiple_of(t * width + col, tile), tile))

    def forward_down(cut):
        outs[cut, :] = dot(hidden[cut, :], down[...]).astype(BF16)

    def backward_chunk(cut):
        d = r.d_s[cut, :]
        for col in range(0, inner, tile):
            at = pl.ds(col, tile)
            d_hidden = dot_nt(d, down[at, :])
            slope[cut, at] = (d_hidden * slope[cut, at].astype(F32)).astype(BF16)
        x = rows[cut, :]
        logits = dot(x, r.route[...])
        lane = lax.broadcasted_iota(jnp.int32, logits.shape, 1)
        logits = jnp.where(lane < experts, logits, NEG)
        router = jnp.exp(logits - jnp.max(logits, axis=1, keepdims=True))
        router = router / jnp.sum(router, axis=1, keepdims=True)
        amount = jnp.sum(outs[cut, :].astype(F32) * d.astype(F32), axis=1, keepdims=True)
        d_log = (amount * (jnp.where(lane == m.z, 1.0, 0.0) - router)).astype(BF16)
        r.log_s[cut, :] = d_log
        d_rows = dot_nt(slope[cut, :], up[...]) + dot_nt(d_log, r.route[...])
        r.back_s[cut, :] = d_rows.astype(BF16)
        return jnp.sum(d_rows * x.astype(F32), axis=0, keepdims=True)

    sent_x = sent_d = None
    saves, returns = [], {}
    scatter = None
    if fetches:
        shard = half // 2
        next_loads = [
            m.local(attention_rows(r, depth + 1, i), r.next_s.at[i // 2 * peers + m.t, pl.ds(i % 2 * shard, shard)]) for i in range(4)
        ]
        fetch = Gather(m, r.next_s)
    if hosted:
        first = {}
        for k, device in ((1, m.x_peer), (2, m.y_peer)):
            mine = pl.ds(pl.multiple_of(m.c * half, half), half)
            first[k] = [m.remote(own_up.at[mine], up_at(m.c, m.t), device), m.remote(own_down.at[mine], down_at(m.c, m.t), device)]
    if reduces:
        scatter = Scatter(m, r.pack_s, r.core_in, r.g_in, r.piece)
        pack_load = m.local(r.pack, r.pack_s)
        e_scatter = ExpertScatter(m, r.e_pack, r.e_own, r.e_keep, r.e_in)
        e_loads = e_scatter.load()
    if remote and forward:
        sent_x = dispatch(r.x, rows, r.stage_x)
    if remote and backward:
        sent_d = dispatch(r.g, r.d_s, r.stage_d)
    if reduces:
        m.need(pack_load)
        scatter.swap(0)
        scatter.swap(1)
    m.need(*loads, *weight_loads)
    if hosted:
        tens = [m.t] + [xor_peer(m.t, k) for k in (1, 2, 3)]
        onward, swaps = [], {}

        def pass_on(k, device, start):
            m.arrived(*first[k])
            for at in (up_at, down_at):
                piece = at(m.c, tens[k], start, half // 2)
                onward.append(m.remote(piece, piece, device))
            swap(k)

        def swap(k):
            swaps[k] = [m.remote(at(m.c, tens[k]), at(m.c, tens[k]), m.sibling) for at in (up_at, down_at)]

        forward_peer(cuts[0], tens[0])
        m.arrived(sent_x[1])
        forward_peer(cuts[1], tens[0])
        pass_on(1, m.y_peer, 0)
        pass_on(2, m.x_peer, half // 2)
        if fetches:
            m.need(*next_loads)
            fetch.out()
        m.arrived(sent_x[2], sent_x[3])
        forward_peer(pl.ds(2 * size, 2 * size), tens[0])
        for k in (1, 2, 3):
            if k == 3:
                m.arrived(*onward)
                swap(3)
            m.arrived(*swaps[k])
            forward_peer(pl.ds(0, count), tens[k])
        if fetches:
            fetch.turn()
        for first_k in (2, 0):
            forward_down(pl.ds(first_k * size, 2 * size))
            for k in (first_k, first_k + 1):
                if k and not backward:
                    returns[k] = give_back(outs, k)
        if not backward:
            for c in range(2):
                for t in range(peers):
                    saves += [m.local(up_at(c, t), r.w.at[c, t, 0]), m.local(down_at(c, t), r.w.at[c, t, 1])]
        if fetches:
            fetch.end()
            saves.append(m.local(r.next_s, r.next_all))
    elif forward:
        for k in range(CUTS):
            if remote and k:
                m.arrived(sent_x[k])
            for t in range(peers):
                forward_peer(cuts[k], t)
            forward_down(cuts[k])
            if remote and k and not backward:
                returns[k] = give_back(outs, k)
    if forward:
        if not backward:
            saves += [m.local(hidden, r.hidden), m.local(slope, r.slope), m.local(rows, r.rows)]
        saves.append(m.local(outs, r.out))
    if backward:
        gain = jnp.zeros((1, width), F32)
        for k in range(CUTS):
            if remote and k:
                m.arrived(sent_d[k])
            gain = gain + backward_chunk(cuts[k])
            if remote and k:
                returns[k] = give_back(r.back_s, k)
            if reduces and k == 0:
                scatter.out(0)
                scatter.out(1)
                e_scatter.out()
            if reduces and k == 2:
                scatter.turn(0)
                scatter.turn(1)
        if not remote:
            saves.append(m.local(r.back_s, r.result))
        if reduces:
            m.need(*e_loads)
            e_scatter.turn()
        r.turned[...] = rows[...].T
        route = dot_tn(r.log_s[...], rows[...])
        pad = r.small.shape[0] - experts - 1
        r.small[...] = jnp.concatenate([route[:experts], gain, jnp.zeros((pad, width), F32)], axis=0)
        swapped = []
        if hosted:
            m.gone(*onward, *[copy for k in (1, 2, 3) for copy in swaps[k]])
        for t in range(peers):
            at = pl.ds(t * width, width)
            up[:, at] = dot(r.turned[...], slope[:, at]).astype(BF16)
            down[at, :] = dot_tn(hidden[:, at], r.d_s[...]).astype(BF16)
            if remote:
                swapped.append([m.remote(at(1 - m.c, t), r.grads_in.at[t, i], m.sibling) for i, at in enumerate((up_at, down_at))])
            else:
                for c in range(2):
                    saves += [m.local(up_at(c, t), r.grads.at[c, t, 0]), m.local(down_at(c, t), r.grads.at[c, t, 1])]
    if reduces:
        for h in range(2):
            scatter.end(h)
        e_scatter.end()
        saves += [m.local(r.piece, r.summed), m.local(r.e_own, r.e_summed)]
    if remote:
        if backward:
            for t in range(peers):
                for i, at in enumerate((up_at, down_at)):
                    m.arrived(swapped[t][i])
                    here = at(m.c, t)
                    here[...] = add_low(here, r.grads_in.at[t, i]).astype(BF16)
                    saves.append(m.local(here, r.grads.at[t, i]))
            if reduces:
                for i, at in enumerate((up_at, down_at)):
                    for box, k, start in ((r.to_x.at[0], 3, 0), (r.to_x.at[1], 1, 0), (r.to_y.at[0], 3, 1), (r.to_y.at[1], 2, 1)):
                        saves.append(m.local(at(m.c, xor_peer(m.t, k), start * (half // 2), half // 2), box.at[i]))
        r.result[...] = combine(m, r.slot_col, r.back_s if backward else outs, returns, r.back, size)
    m.finish()
    m.need(*saves)


def expert_call(plan, experts, count, w=None, own=None, x=None, g=None, kept=None, route=None, pack=None, fetch=None, depth=0):
    slots = plan[0]
    forward, backward, remote, hosted, reduces = x is not None, g is not None, experts == CUTS, own is not None, pack is not None
    tokens, width = (x if forward else g).shape
    peers = lax.axis_size(TENSOR)
    half, inner = width // 2, peers * width
    w_shape = low_shape(2, peers, 2, half, width)
    data = VMEM if remote else ANY
    rows_shape, inner_shape = low_shape(count, width), low_shape(count, inner)
    ins, outs = {}, {}
    if hosted:
        ins.update(w_in=(own[0], ANY), w_down=(own[1], ANY))
        if not backward:
            outs.update(w=(w_shape, ANY))
    else:
        ins.update(w=(w, ANY))
    if remote:
        ins.update(slot_row=(slots[None, :], VMEM), slot_col=(slots[:, None], VMEM))
    if forward:
        ins.update(x=(x, data))
    if backward:
        ins.update(g=(g, data), route=(route, VMEM))
        if not forward:
            ins.update(rows=(kept.rows, ANY), out=(kept.out, ANY), hidden=(kept.hidden, ANY), slope=(kept.slope, ANY))
    if remote or backward:
        outs.update(result=(low_shape(tokens if remote else count, width), data))
    if forward:
        outs.update(out=(rows_shape, ANY))
        if not backward:
            outs.update(rows=(rows_shape, ANY), hidden=(inner_shape, ANY), slope=(inner_shape, ANY))
    if backward:
        outs.update(grads=(low_shape(peers, 2, half, width) if remote else w_shape, ANY))
        outs.update(small=(jax.ShapeDtypeStruct((-(-(experts + 1) // 8) * 8, width), F32), VMEM))
    scratch = dict(
        up=low_vmem(width, inner), down=low_vmem(inner, width), hidden_s=low_vmem(count, inner), slope_s=low_vmem(count, inner),
        rows_s=low_vmem(count, width), outs_s=low_vmem(count, width),
    )
    if backward:
        scratch.update(
            d_s=low_vmem(count, width), back_s=low_vmem(count, width), log_s=low_vmem(count, BLK), turned=low_vmem(width, count)
        )
    if backward and remote:
        scratch.update(grads_in=low_vmem(peers, 2, half, width))
    if fetch is not None:
        ins.update(w_qkv=(fetch[0], ANY), w_out=(fetch[1], ANY))
        outs.update(next_all=(low_shape(2 * peers, half, width), ANY))
        scratch.update(next_s=low_vmem(2 * peers, half, width))
    if reduces:
        ins.update(pack=(pack[0], ANY), e_pack=(pack[1], ANY))
        box = (low_shape(2, 2, half // 2, width), ANY)
        outs.update(summed=(low_shape(half, width), ANY), e_summed=(low_shape(2, half, width), ANY), to_x=box, to_y=box)
        scratch.update(scatter_scratch(peers, half, width), **expert_scatter_scratch(half, width))
    if remote:
        part = low_vmem(3, count // CUTS, width)
        scratch.update(back=part)
        if forward:
            scratch.update(stage_x=part)
        if backward:
            scratch.update(stage_d=part)
    return run_kernel(
        expert_part, ins, outs, scratch, forward + 2 * backward, count * width * inner, 64, 48 if remote else 0,
        forward=forward, backward=backward, remote=remote, hosted=hosted, reduces=reduces,
        fetches=fetch is not None, experts=experts, depth=depth,
    )


def experts_forward(plan, token_rows, experts, capacity, w, own, fetch, depth):
    count = experts * capacity
    if experts == CUTS:
        got = expert_call(plan, experts, count, own=own, x=token_rows, fetch=fetch, depth=depth)
        return got.result, got
    got = expert_call(plan, experts, count, w=w, x=send_rows(plan[1], token_rows, experts, capacity))
    got.w = w
    return return_rows(plan[1], got.out, experts, capacity).astype(BF16), got


def experts_backward(plan, d_low, kept, route, experts, capacity, pack):
    count = experts * capacity
    if experts == CUTS:
        return expert_call(plan, experts, count, w=kept.w, g=d_low, kept=kept, route=route, pack=pack)
    d_sent = send_rows(plan[1], d_low, experts, capacity)
    got = expert_call(plan, experts, count, w=kept.w, g=d_sent, kept=kept, route=route)
    got.result = return_rows(plan[1], got.result, experts, capacity).astype(BF16)
    got.summed = scatter_all(pack)
    return got


def experts_both(w, own, plan, token_rows, d_low, route, experts, capacity, depth):
    count = experts * capacity
    if experts == CUTS:
        return expert_call(plan, experts, count, own=own, x=token_rows, g=d_low, route=route, depth=depth)
    rows = send_rows(plan[1], token_rows, experts, capacity)
    d_sent = send_rows(plan[1], d_low, experts, capacity)
    got = expert_call(plan, experts, count, w=w, x=rows, g=d_sent, route=route)
    got.result = return_rows(plan[1], got.result, experts, capacity).astype(BF16)
    return got


def project_part(m, hosted):
    r = m.refs
    rows, w = r.n_s, r.w_s
    tokens = r.x.shape[0]
    peers = rows.shape[0] // tokens
    shard = w.shape[1] // peers
    c, t = m.c, m.t
    ready = m.greet([m.x_peer, m.y_peer] + ([m.sibling] if hosted else []))
    at = lambda index: pl.ds(pl.multiple_of(index * shard, shard), shard)
    first_load = m.local(r.x, rows.at[pl.ds(0, tokens)])
    loads = []
    if hosted:
        for i in range(4):
            loads.append(m.local(attention_rows(r, 0, i), w.at[i, at(t)]))
    else:
        for i in range(4):
            for j in range(peers):
                piece = r.w.at[i // 2, j, r.w.shape[2] - 1, pl.ds(i % 2 * shard, shard)]
                loads.append(m.local(piece, w.at[i, pl.ds(j * shard, shard)]))
    ready()
    half = tokens // 2
    m.need(first_load)
    cut = lambda j, part: pl.ds(j * tokens + part * half, half)

    def send(j, part, to, device):
        return m.remote(rows.at[cut(j, part)], rows.at[cut(to, part)], device)

    first, second, swaps, kept = {}, [], [], []
    if hosted:
        m.need(*loads)
        for h in range(2):
            mine = w.at[2 * c + h, at(t)]
            first[1, h] = m.remote(mine, mine, m.x_peer)
            first[2, h] = m.remote(mine, mine, m.y_peer)
    a_low, b_high = send(0, 0, 1, m.x_peer), send(0, 1, 2, m.y_peer)
    a_high, b_low = send(0, 1, 1, m.x_peer), send(0, 0, 2, m.y_peer)
    if hosted:
        for h in range(2):
            for k, onward, part in ((1, m.y_peer, 0), (2, m.x_peer, 1)):
                m.arrived(first[k, h])
                start = pl.multiple_of(xor_peer(t, k) * shard + part * (shard // 2), shard // 2)
                piece = w.at[2 * c + h, pl.ds(start, shard // 2)]
                second.append(m.remote(piece, piece, onward))
                whole = w.at[2 * c + h, at(xor_peer(t, k))]
                swaps.append(m.remote(whole, whole, m.sibling))
    m.arrived(a_low)
    c_low = send(1, 0, 3, m.y_peer)
    m.arrived(b_high)
    c_high = send(2, 1, 3, m.x_peer)
    if hosted:
        m.arrived(*second)
        for h in range(2):
            whole = w.at[2 * c + h, at(xor_peer(t, 3))]
            swaps.append(m.remote(whole, whole, m.sibling))
        m.arrived(*swaps)
    else:
        m.need(*loads)
    for i in range(4):
        kept.append(m.local(w.at[i], r.w_all.at[i]))

    def keys_values(start, size):
        here = pl.ds(start, size)
        x = rows[here, :]
        for i, near, far in ((1, r.k_s, r.k), (2, r.v_s, r.v)):
            near[here, :] = dot_nt(x, w[i]).astype(BF16)
            kept.append(m.local(near.at[here], far.at[here]))

    r.q_s[...] = dot_nt(rows[pl.ds(0, tokens), :], w[0]).astype(BF16)
    kept.append(m.local(r.q_s, r.q))
    keys_values(0, tokens)
    m.arrived(a_high)
    keys_values(tokens, tokens)
    m.arrived(b_low)
    keys_values(2 * tokens, tokens)
    m.arrived(c_low)
    keys_values(3 * tokens, half)
    m.arrived(c_high)
    keys_values(3 * tokens + half, half)
    kept.append(m.local(rows, r.n))
    m.finish()
    m.need(*kept)


def project(x, w, hosted, peers):
    tokens, width = x.shape
    every = peers * tokens
    outs = dict(
        q=(low_shape(tokens, width), ANY), k=(low_shape(every, width), ANY), v=(low_shape(every, width), ANY),
        n=(low_shape(every, width), ANY), w_all=(low_shape(4, width, width), ANY),
    )
    scratch = dict(
        n_s=low_vmem(every, width), w_s=low_vmem(4, width, width), q_s=low_vmem(tokens, width),
        k_s=low_vmem(every, width), v_s=low_vmem(every, width),
    )
    given = dict(w_qkv=(w[0], ANY), w_out=(w[1], ANY)) if hosted else dict(w=(w, ANY))
    return run_kernel(
        project_part, dict(x=(x, ANY), **given), outs, scratch, 6 + hosted, 9 * tokens * width * width, 40, 24, hosted=hosted
    )


def project_back_part(m, full, returns):
    r = m.refs
    tokens, width = r.dq_s.shape
    peers = r.dk_s.shape[0] // tokens
    shard = width // peers
    c, z = m.c, m.z
    local, remote, need, arrived = m.local, m.remote, m.need, m.arrived
    ready = m.greet([m.x_peer, m.y_peer] + ([m.sibling] if full else []) + (m.z_peers if full or returns else []))
    rows_of = lambda j: pl.ds(j * tokens, tokens)
    w = r.w_s
    weights_in = {i: local(r.w.at[i], w.at[i]) for i in (1, 2)}
    parts_in = {}
    for j in (3, 1, 2, 0):
        parts_in[j] = [local(a.at[rows_of(j)], b.at[rows_of(j)]) for a, b in ((r.dk, r.dk_s), (r.dv, r.dv_s))]
    above_in = local(r.above, r.above_s) if full else None
    rest_in = [local(a, b) for a, b in ((r.n, r.n_s), (r.dq, r.dq_s), (r.heads, r.heads_s), (r.d_att, r.d_att_s))]
    weights_in[0] = local(r.w.at[0], w.at[0])
    swaps_in = []
    if full:
        e_scatter = ExpertScatter(m, r.e0, r.e_own, r.e_keep, r.e_in)
        e_scatter.flow = []
        e_loads = [local(a.at[n], r.e_in.at[2 * n + i]) for n in range(2) for i, a in enumerate((r.from_x, r.from_y))]
        e_loads += e_scatter.load()
        swaps_in = [local(r.e1.at[i], r.e_s.at[i, 1, c]) for i in range(2)]
    ready()
    tops, ends = pl.ds(0, tokens // 2), pl.ds(tokens // 2, tokens // 2)

    def partial(j):
        at = rows_of(j)
        return dot(r.dk_s[at, :], w[1]) + dot(r.dv_s[at, :], w[2])

    over_x, over_y = {}, {}

    stages = {1: r.p1, 2: r.p2, 3: r.p3}

    def rows_part(*which):
        need(weights_in[1], weights_in[2])
        for j in which:
            need(*parts_in[j])
            stages[j][...] = partial(j).astype(BF16)

    def rows_send(*which):
        for j in which:
            if j != 2:
                over_x[j] = remote(stages[j].at[tops], r.row_in.at[j // 2], m.x_peer)
            if j != 1:
                over_y[j] = remote(stages[j].at[ends], r.row_in.at[2 + j // 3], m.y_peer)

    def rows_turn():
        arrived(over_x[3])
        r.p2[tops, :] = add_low(r.p2.at[tops], r.row_in.at[1]).astype(BF16)
        over_y[1] = remote(r.p2.at[tops], r.row_in.at[4], m.y_peer)
        arrived(over_y[3])
        r.p1[ends, :] = add_low(r.p1.at[ends], r.row_in.at[3]).astype(BF16)
        over_x[2] = remote(r.p1.at[ends], r.row_in.at[5], m.x_peer)

    def rows_own():
        need(*parts_in[0], weights_in[0], rest_in[1])
        r.dn[...] = partial(0) + dot(r.dq_s[...], w[0])

    def rows_end():
        for copy, slot, cut in ((over_x[1], 0, tops), (over_y[2], 2, ends), (over_y[1], 4, tops), (over_x[2], 5, ends)):
            arrived(copy)
            r.dn[cut, :] += r.row_in[slot].astype(F32)

    pack = r.pack_s
    part = lambda i: pl.ds(i % 2 * shard, shard)

    def weight_grad(i):
        need(*rest_in, weights_in[0], *[p for j in (3, 1, 2, 0) for p in parts_in[j]])
        if i == 0:
            g = dot_tn(r.dq_s[...], r.n_s[rows_of(0), :])
        elif i == 3:
            g = dot_tn(r.heads_s[...], r.d_att_s[...])
        else:
            g = dot_tn((r.dk_s if i == 1 else r.dv_s)[...], r.n_s[...])
        low = g.astype(BF16)
        for j in range(peers):
            pack[i // 2 * peers + j, part(i), :] = low[j * shard : (j + 1) * shard]
        return jnp.sum(g * w[i].astype(F32), axis=0, keepdims=True) if i < 3 else 0.0

    if not full:
        copies = {}
        if returns:
            size = r.out.shape[0] // CUTS
            out_in = local(r.out.at[pl.ds(0, size)], r.out_s)
            for k in (2, 3, 1):
                copies[k] = remote(r.out.at[pl.ds(k * size, size)], r.back.at[k - 1], m.z_peers[k - 1])
        for j in (3, 1, 2):
            rows_part(j)
            rows_send(j)
        total = weight_grad(1)
        rows_turn()
        rows_own()
        total = total + weight_grad(2) + weight_grad(0) + weight_grad(3)
        r.att[...] = jnp.broadcast_to(total, r.att.shape)
        saved = local(pack, r.pack)
        if returns:
            need(out_in)
            r.result[...] = combine(m, r.slot_col, r.out_s, copies, r.back, size)
        rows_end()
        m.finish()
        need(saved)
        return

    mini = shard // 4
    at_z = lambda h, index: pl.ds(pl.multiple_of(h * shard + index * mini, mini), mini)
    both, z_in = r.both, r.z_in

    def z_out(source, layer, h):
        return [remote(source.at[at_z(h, xor_peer(z, k))], z_in.at[layer * 2 + h, k - 1], m.z_peers[k - 1]) for k in (1, 2, 3)]

    def z_sum(source, copies, layer, h):
        arrived(*copies)
        here = both.at[layer, c, at_z(h, z)]
        both[layer, c, at_z(h, z), :] = add_low(
            source.at[at_z(h, z)], *[z_in.at[layer * 2 + h, k] for k in range(3)]
        ).astype(BF16)
        return [remote(here, here, device) for device in m.z_peers]

    def core_out(copies, layer, h):
        arrived(*copies)
        here = both.at[layer, c, pl.ds(h * shard, shard)]
        return remote(here, here, m.sibling)

    scatter = Scatter(m, pack, r.core_in, r.g_in, r.piece)
    need(above_in)
    above = [z_out(r.above_s, 1, h) for h in range(2)]
    rows_part(3)
    rows_send(3)
    total = weight_grad(3) + weight_grad(1)
    scatter.swap(1)
    need(*e_loads)
    e_scatter.turn()
    total = total + weight_grad(0) + weight_grad(2)
    scatter.swap(0)
    small_s, small_r = r.small_s, r.small_r
    row = lax.broadcasted_iota(jnp.int32, r.small.shape, 0)
    att_row = r.small_in.shape[0] // 2 - 1
    small_s[0] = jnp.where(row == att_row, total, r.small_in[...])
    small_1 = remote(small_s.at[0], small_r.at[0], m.sibling)
    above = [z_sum(r.above_s, above[h], 1, h) for h in range(2)]
    arrived(small_1)
    small_s[1] = small_s[0] + small_r[0]
    small_2 = [remote(small_s.at[1], small_r.at[k], m.z_peers[k - 1]) for k in (1, 2, 3)]
    scatter.out(1)
    scatter.out(0)
    rows_part(1)
    rows_part(2)
    arrived(*small_2)
    small_s[2] = small_s[1] + small_r[1] + small_r[2] + small_r[3]
    scatter.turn(1)
    small_3 = remote(small_s.at[2], small_r.at[4], m.x_peer)
    scatter.turn(0)
    rows_send(1, 2)
    above = [core_out(above[h], 1, h) for h in range(2)]
    need(*swaps_in)
    e_copies = [remote(r.e_s.at[i, 1, c], r.e_s.at[i, 1, c], m.sibling) for i in range(2)]
    rows_own()
    scatter.end(1)
    piece_1 = z_out(r.piece, 0, 1)
    scatter.end(0)
    piece_0 = z_out(r.piece, 0, 0)
    arrived(small_3)
    small_s[3] = small_s[2] + small_r[4]
    rows_turn()
    small_4 = remote(small_s.at[3], small_r.at[5], m.y_peer)
    piece_1 = z_sum(r.piece, piece_1, 0, 1)
    piece_0 = z_sum(r.piece, piece_0, 0, 0)
    e_scatter.end()
    for i in range(2):
        r.e_s[i, 0, c] = r.e_own[i]
        e_copies.append(remote(r.e_s.at[i, 0, c], r.e_s.at[i, 0, c], m.sibling))
    arrived(*e_copies)
    saved = [local(r.e_s.at[0], r.e_up), local(r.e_s.at[1], r.e_down)]
    piece_1 = core_out(piece_1, 0, 1)
    piece_0 = core_out(piece_0, 0, 0)
    rows_end()
    arrived(*above, piece_1, piece_0)
    saved.append(local(both, r.g))
    arrived(small_4)
    r.small[...] = small_s[3] + small_r[5]
    m.finish()
    need(*saved)


def project_back(w, dq, dk, dv, normed_all, heads, d_att, above=None, small=None, swaps=None, out=None, slots=None):
    full, returns = above is not None, out is not None
    tokens, width = dq.shape
    rows = dk.shape[0]
    half = width // 2
    peers = rows // tokens
    shape = jax.ShapeDtypeStruct
    ins = dict(
        w=(w, ANY), dq=(dq, ANY), dk=(dk, ANY), dv=(dv, ANY), n=(normed_all, ANY), heads=(heads, ANY), d_att=(d_att, ANY),
    )
    outs = dict(dn=(shape((tokens, width), F32), VMEM))
    some, every = low_vmem(tokens, width), low_vmem(rows, width)
    scratch = dict(
        w_s=low_vmem(3, width, width), dq_s=some, dk_s=every, dv_s=every, n_s=every, heads_s=some, d_att_s=some,
        p1=some, p2=some, p3=some, row_in=low_vmem(6, tokens // 2, width),
    )
    if full:
        ins.update(above=(above, ANY), small_in=(small, VMEM), e0=(swaps[0], ANY), e1=(swaps[1], ANY), from_x=(swaps[2], ANY), from_y=(swaps[3], ANY))
        twice = (low_shape(2, 2, half, width), ANY)
        outs.update(g=twice, e_up=twice, e_down=twice, small=(shape(small.shape, F32), VMEM))
        scratch.update(
            scatter_scratch(peers, half, width), **expert_scatter_scratch(half, width), above_s=low_vmem(half, width), e_s=low_vmem(2, 2, 2, half, width),
            small_s=pltpu.VMEM((4,) + small.shape, F32), small_r=pltpu.VMEM((6,) + small.shape, F32),
            z_in=low_vmem(4, 3, half // 8, width), both=low_vmem(2, 2, half, width),
        )
    else:
        outs.update(pack=(low_shape(2 * peers, half, width), ANY), att=(shape((8, width), F32), VMEM))
        scratch.update(pack_s=low_vmem(2 * peers, half, width))
        if returns:
            ins.update(out=(out, ANY), slot_col=(slots[:, None], VMEM))
            outs.update(result=(low_shape(tokens, width), VMEM))
            size = out.shape[0] // CUTS
            scratch.update(out_s=low_vmem(size, width), back=low_vmem(3, size, width))
    return run_kernel(
        project_back_part, ins, outs, scratch, 4 + full, 4 * rows * width * width, 32, 96, full=full, returns=returns
    )


def inverse_rms(stream):
    return lax.rsqrt(jnp.mean(stream * stream, axis=-1, keepdims=True) + EPS)


def norm_backward(upstream, stream, inverse, gain):
    weighted = upstream * gain
    inner = jnp.mean(weighted * stream, axis=-1, keepdims=True)
    return inverse * weighted - stream * (inverse * inverse * inverse) * inner


def path_table(segment_ids, path_pos, parent_ids, peers):
    segment = segment_ids[::BLK].reshape(peers, -1)
    position = path_pos[::BLK].reshape(peers, -1)
    t = lax.axis_index(TENSOR)
    order = jnp.arange(peers, dtype=jnp.int32) ^ t
    match = order[:, None] == jnp.arange(peers, dtype=jnp.int32)[None, :]
    pick = lambda v: jnp.sum(jnp.where(match[:, :, None], v[None], 0), axis=1)
    segment, position = pick(segment), pick(position)
    place = jnp.where(segment == 0, position // BLK, segment + (TRUNK - 1))
    seg, pos, own = segment[0], position[0], place[0]
    names = jnp.arange(parent_ids.shape[-1], dtype=jnp.int32)
    parent = jnp.sum(jnp.where(seg[:, None] == names[None, :], parent_ids[0][None], 0), axis=1)
    leaf = (seg > 0) & (parent > 0)
    parent_place = jnp.where(leaf, parent + (TRUNK - 1), own)
    base_own = jnp.where(seg > 0, pos, BIG)
    base_parent = jnp.where(leaf, TRUNK * BLK, BIG)
    mine = jnp.stack([pos, own, parent_place, base_own, base_parent], axis=1)
    return jnp.concatenate([place.reshape(-1), mine.reshape(-1)]).astype(jnp.int32)


def dispatch_plan(route, experts, capacity):
    count = route.shape[0]
    chosen = route[:, None] == jnp.arange(experts, dtype=jnp.int32)[None, :]
    index = jnp.arange(count, dtype=jnp.int32)
    before = (index[None, :] < index[:, None]).astype(BF16)
    ranks = dot(before, chosen.astype(BF16)).astype(jnp.int32)
    rank = jnp.sum(jnp.where(chosen, ranks, 0), axis=1)
    to = route ^ lax.axis_index(EXPERT) if experts == 4 else route
    slot = to * capacity + rank
    table = slot[None, :] == jnp.arange(experts * capacity, dtype=jnp.int32)[:, None]
    return chosen, (slot, table.astype(BF16))


def send_rows(table, rows, experts, capacity):
    chunks = [
        dot(table[k * capacity : (k + 1) * capacity], rows).astype(BF16) for k in range(experts)
    ]
    return jnp.concatenate(exchange(chunks), axis=0)


def return_rows(table, results, experts, capacity):
    chunks = exchange([results[k * capacity : (k + 1) * capacity] for k in range(experts)])
    return dot_tn(table, jnp.concatenate(chunks, axis=0))


def own_half(x):
    half = x.shape[0] // 2
    return lax.dynamic_slice_in_dim(x, lax.axis_index(DP) * half, half, 0)


def gather_all(x):
    out = lax.all_gather(x, (DP, TENSOR), axis=0)
    return out.reshape((lax.axis_size(DP), lax.axis_size(TENSOR)) + x.shape)


def scatter_all(x):
    flat = x.reshape((-1,) + x.shape[2:])
    return lax.psum_scatter(flat, (DP, TENSOR), scatter_dimension=0, tiled=True)[0]


def pack_attention(w_mix, w_proj):
    width = w_mix.shape[0]
    return jnp.concatenate([w_mix.transpose(1, 2, 0).reshape(-1, width), w_proj], axis=0)


def pack_experts(w_up, w_back):
    return jnp.stack([own_half(w_up), own_half(w_back)])


def swap_cores(half):
    return lax.all_gather(half, DP, axis=0)


def body(
    hidden_in, route_ids, segment_ids, path_pos, parent_ids, norm_att, w_qkv, w_out, norm_ffn, w_route, w_in, w_down, cotangent,
):
    depth_total = w_qkv.shape[0]
    tokens, width = hidden_in.shape
    experts = w_route.shape[-1]
    capacity = 3 * tokens // (2 * experts)
    peers = lax.axis_size(TENSOR)
    shard = width // peers
    table = path_table(segment_ids, path_pos, parent_ids, peers)
    plans = [dispatch_plan(route_ids[d, :, 0], experts, capacity) for d in range(depth_total)]
    routes = [jnp.pad(w_route[d], ((0, 0), (0, BLK - experts))) for d in range(depth_total)]
    cotangent = cotangent.astype(F32)

    stream = hidden_in.astype(F32)
    kept = []
    turned = (w_qkv.transpose(0, 2, 3, 1), w_out)
    own = (w_in, w_down)
    weights = None
    for depth in range(depth_total):
        gain_att, gain_ffn = norm_att[depth].astype(F32), norm_ffn[depth].astype(F32)
        chosen, plan = plans[depth]
        last = depth + 1 == depth_total
        inverse_att = inverse_rms(stream)
        normed = (stream * inverse_att * gain_att).astype(BF16)
        proj = project(normed, turned if depth == 0 else weights, depth == 0, peers)
        w_here = None if experts == CUTS else gather_all(pack_experts(w_in[depth, 0], w_down[depth, 0]))
        heads, lse = attend(table, proj.q, proj.k, proj.v)
        after_att = stream + dot(heads, proj.w_all[3])
        inverse_ffn = inverse_rms(after_att)
        token_rows = (after_att * inverse_ffn * gain_ffn).astype(BF16)
        router = jax.nn.softmax(dot(token_rows, w_route[depth]), axis=-1)
        gate = jnp.sum(jnp.where(chosen, router, 0.0), axis=1, keepdims=True)
        if last:
            d_low = (gate * cotangent).astype(BF16)
            held = experts_both(w_here, own, plan, token_rows, d_low, routes[depth], experts, capacity, depth)
            if experts != CUTS:
                back = return_rows(plan[1], held.out, experts, capacity).astype(BF16)
        else:
            back, held = experts_forward(plan, token_rows, experts, capacity, w_here, own, turned, depth)
            if experts == CUTS:
                weights = held.next_all.reshape((2, peers, 1) + held.next_all.shape[1:])
            else:
                weights = gather_all(own_half(pack_attention(w_qkv[depth + 1], w_out[depth + 1])))[:, :, None]
        kept.append((stream, inverse_att, proj, heads, lse, after_att, inverse_ffn, gate, held))
        if not last:
            stream = after_att + gate * back.astype(F32)

    upstream = cotangent
    grads_e, grads_a, smalls = [None] * depth_total, [None] * depth_total, [None] * depth_total
    above = None
    for depth in reversed(range(depth_total)):
        stream, inverse_att, proj, heads, lse, after_att, inverse_ffn, gate, held = kept[depth]
        gain_att, gain_ffn = norm_att[depth].astype(F32), norm_ffn[depth].astype(F32)
        chosen, plan = plans[depth]
        last = depth + 1 == depth_total
        if not last:
            d_low = (gate * upstream).astype(BF16)
            held = experts_backward(plan, d_low, held, routes[depth], experts, capacity, above)
            above = held.summed
        dx1 = upstream + norm_backward(held.result.astype(F32), after_att, inverse_ffn, gain_ffn)
        d_att = dx1.astype(BF16)
        d_heads = dot_nt(d_att, proj.w_all[3]).astype(BF16)
        dq, dk, dv = attend_back(table, proj.q, proj.k, proj.v, d_heads, heads, lse)
        args = (proj.w_all, dq, dk, dv, proj.n, heads, d_att)
        if depth == 0 and experts == CUTS:
            swaps = (held.grads, held.e_summed, xperm(held.to_x, TENSOR, 1), xperm(held.to_y, TENSOR, 2))
            lines = lambda n: jnp.zeros((n, width), F32)
            part = jnp.concatenate([held.small[: experts + 1], lines(3), smalls[1], lines(2)], axis=0)
            got = project_back(*args, above=above, small=part, swaps=swaps)
            grads_a, grads_e = got.g, (got.e_up, got.e_down)
            total = got.small
            small = jnp.stack([
                jnp.concatenate([total[: experts + 1], total[7:8]], axis=0), total[8 : 8 + experts + 2]
            ])
        else:
            if last and experts == CUTS:
                got = project_back(*args, out=held.out, slots=plan[0])
                back = got.result
            else:
                got = project_back(*args)
            if last:
                hidden_out = (after_att + gate * back.astype(F32)).astype(BF16)
            if above is not None:
                grads_a[depth + 1] = swap_cores(lax.psum(above, EXPERT))
            above = got.pack.reshape((2, peers) + got.pack.shape[1:])
            if experts == CUTS:
                above = (got.pack, held.grads)
            else:
                grads_e[depth] = scatter_all(after(held.grads, got.dn))
            smalls[depth] = jnp.concatenate([held.small[: experts + 1], got.att[:1]], axis=0)
            if depth == 0:
                grads_a[0] = swap_cores(lax.psum(scatter_all(above), EXPERT))
                small = sum_small(jnp.stack(smalls))
                grads_e = jnp.stack([swap_cores(g) for g in grads_e]).transpose(2, 0, 1, 3, 4)
                grads_a = jnp.stack(grads_a)
        upstream = dx1 + norm_backward(got.dn, stream, inverse_att, gain_att)
    grad_up, grad_down = [g.reshape(depth_total, 1, width, width).astype(F32) for g in grads_e]
    grads_a = grads_a.reshape(depth_total, width, width).astype(F32)
    grad_mix = grads_a[:, : 3 * shard].reshape(depth_total, 3, shard, width).transpose(0, 3, 1, 2)
    grad_out = grads_a[:, 3 * shard :]
    grad_route = small[:, :experts].transpose(0, 2, 1)
    grad_ffn = small[:, experts] / norm_ffn.astype(F32)
    grad_att = small[:, experts + 1] / norm_att.astype(F32)
    return (hidden_out, upstream, grad_att, grad_mix, grad_out, grad_ffn, grad_route, grad_up, grad_down)


def solution(mesh):
    in_specs = (
        P((DP, EXPERT, TENSOR), None),
        P(None, (DP, EXPERT, TENSOR), None),
        P((DP, EXPERT)),
        P((DP, EXPERT)),
        P((DP, EXPERT), None),
        P(),
        P(None, None, None, TENSOR),
        P(None, TENSOR, None),
        P(),
        P(),
        P(None, EXPERT, None, TENSOR),
        P(None, EXPERT, TENSOR, None),
        P((DP, EXPERT, TENSOR), None),
    )
    out_specs = (
        P((DP, EXPERT, TENSOR), None),
        P((DP, EXPERT, TENSOR), None),
        P(),
        P(None, None, None, TENSOR),
        P(None, TENSOR, None),
        P(),
        P(),
        P(None, EXPERT, None, TENSOR),
        P(None, EXPERT, TENSOR, None),
    )
    return jax.shard_map(body, mesh=mesh, in_specs=in_specs, out_specs=out_specs, check_vma=False)
```

```python
from types import SimpleNamespace

import jax
import jax.numpy as jnp
from jax import lax
from jax.experimental import pallas as pl
from jax.experimental.pallas import tpu as pltpu
from jax.sharding import PartitionSpec as P

HEAD_DIM = 64
BLK = 128
TRUNK = 8
PAIR = 2 * HEAD_DIM
EPS = 1e-06
NEG = -1000000000.0
BIG = 1 << 20
F32 = jnp.float32
BF16 = jnp.bfloat16
VMEM_LIMIT = 58 * 1024 * 1024
DP, EXPERT, TENSOR = "dp", "expert", "tensor"

NT = (((1,), (1,)), ((), ()))
TN = (((0,), (0,)), ((), ()))


def dot(a, b):
    return jnp.dot(a, b, preferred_element_type=F32)


def dot_nt(a, b):
    return lax.dot_general(a, b, NT, preferred_element_type=F32)


def dot_tn(a, b):
    return lax.dot_general(a, b, TN, preferred_element_type=F32)


def cost(macs, moved, trans=0):
    return pl.CostEstimate(flops=macs // 64, bytes_accessed=moved // 64, transcendentals=0)


def xperm(x, axis, k):
    n = lax.axis_size(axis)
    return lax.ppermute(x, axis, [(i, i ^ k) for i in range(n)])


def after(x, dep):
    return lax.optimization_barrier((x, dep))[0]


def sum_small(x):
    for axis in (DP, TENSOR, EXPERT):
        n = lax.axis_size(axis)
        k = 1
        while k < n:
            x = x + xperm(x, axis, k)
            k *= 2
    return x


def exchange(chunks):
    n = len(chunks)
    if n == 4:
        return [chunks[0]] + [xperm(chunks[k], EXPERT, k) for k in range(1, n)]
    out = lax.all_to_all(jnp.stack(chunks), EXPERT, split_axis=0, concat_axis=0, tiled=True)
    return [out[k] for k in range(n)]


def masked_pair(x):
    lane = lax.broadcasted_iota(jnp.int32, x.shape, 1)
    zero = jnp.zeros_like(x)
    return jnp.concatenate([jnp.where(lane < HEAD_DIM, x, zero), jnp.where(lane < HEAD_DIM, zero, x)], axis=0)


def path_spans(table, at, trunk):
    own, parent, base_own, base_parent = [table[at + j] for j in range(1, 5)]
    block = lambda place: pl.ds(pl.multiple_of(place * BLK, BLK), BLK)
    return [(pl.ds(0, trunk), 0), (block(parent), base_parent), (block(own), base_own)]


def attend_kernel(table, q_ref, k_ref, v_ref, out_ref, lse_ref, keys, values_t):
    blocks = k_ref.shape[0] // BLK
    mine = q_ref.shape[0] // BLK
    trunk = TRUNK * BLK
    for b in range(blocks):
        place = pl.ds(pl.multiple_of(table[b] * BLK, BLK), BLK)
        rows = pl.ds(b * BLK, BLK)
        keys[place, :] = k_ref[rows, :]
        values_t[pl.ds(0, PAIR), place] = v_ref[rows, :].T
    values_t[pl.ds(PAIR, 16), :] = jnp.ones((16, blocks * BLK), BF16)
    lane = lax.broadcasted_iota(jnp.int32, (BLK, PAIR), 1)

    def scores_of(i):
        at = blocks + 5 * i
        q = masked_pair(q_ref[pl.ds(i * BLK, BLK), :] * jnp.asarray(HEAD_DIM ** -0.5, BF16))
        pos_q = table[at] + lax.broadcasted_iota(jnp.int32, (1, 2 * BLK), 1) % BLK
        parts = []
        for here, base in path_spans(table, at, trunk):
            scores = dot_nt(keys[here, :], q)
            key_pos = base + lax.broadcasted_iota(jnp.int32, (here.size, 1), 0)
            parts.append(jnp.where(key_pos <= pos_q, scores, NEG))
        top = parts[0].max(axis=0, keepdims=True)
        for part in parts[1:]:
            top = jnp.maximum(top, part.max(axis=0, keepdims=True))
        return parts, top

    coming = scores_of(0)
    for i in range(mine):
        parts, top = coming
        if i + 1 < mine:
            coming = scores_of(i + 1)
        rows = pl.ds(i * BLK, BLK)
        both = jnp.zeros((PAIR + 16, 2 * BLK), F32)
        for (here, _), part in zip(path_spans(table, blocks + 5 * i, trunk), parts):
            both = both + dot(values_t[:, here], jnp.exp(part - top).astype(BF16))
        total = both[PAIR : PAIR + 1]
        heads = (both[:PAIR] / total).T
        lse = top + jnp.log(total)
        out_ref[rows, :] = jnp.where(lane < HEAD_DIM, heads[:BLK], heads[BLK:]).astype(BF16)
        lse_ref[0, pl.ds(0, 1), rows] = lse[:, :BLK]
        lse_ref[0, pl.ds(1, 1), rows] = lse[:, BLK:]


def attend(table, q, k, v):
    mine, width = q.shape
    rows = k.shape[0]
    pairs = width // PAIR
    column = lambda n: pl.BlockSpec((n, PAIR), lambda p, table: (0, p))
    return pl.pallas_call(
        attend_kernel,
        grid_spec=pltpu.PrefetchScalarGridSpec(
            num_scalar_prefetch=1,
            grid=(pairs,),
            in_specs=[column(mine), column(rows), column(rows)],
            out_specs=[column(mine), pl.BlockSpec((1, 8, mine), lambda p, table: (p, 0, 0))],
            scratch_shapes=[pltpu.VMEM((rows, PAIR), BF16), pltpu.VMEM((PAIR + 16, rows), BF16)],
        ),
        out_shape=[jax.ShapeDtypeStruct((mine, width), BF16), jax.ShapeDtypeStruct((pairs, 8, mine), F32)],
        compiler_params=pltpu.CompilerParams(vmem_limit_bytes=VMEM_LIMIT),
        cost_estimate=cost(mine * 1280 * width * 8, 4 * rows * width, mine * 1280 * width // HEAD_DIM),
        name="attend",
    )(table, q, k, v)


def attend_back_kernel(
    table, q_ref, k_ref, v_ref, do_ref, o_ref, lse_ref, dq_ref, dk_ref, dv_ref, keys, values, keys_t, dk_acc, dv_acc,
):
    blocks = k_ref.shape[0] // BLK
    mine = q_ref.shape[0] // BLK
    trunk = TRUNK * BLK
    for b in range(blocks):
        place = pl.ds(pl.multiple_of(table[b] * BLK, BLK), BLK)
        rows = pl.ds(b * BLK, BLK)
        keys[place, :] = k_ref[rows, :]
        values[place, :] = v_ref[rows, :]
        keys_t[:, place] = k_ref[rows, :].T
    dk_acc[...] = jnp.zeros_like(dk_acc)
    dv_acc[...] = jnp.zeros_like(dv_acc)
    lane = lax.broadcasted_iota(jnp.int32, (BLK, PAIR), 1)

    def weights_of(i):
        at = blocks + 5 * i
        rows = pl.ds(i * BLK, BLK)
        q = masked_pair(q_ref[rows, :] * jnp.asarray(HEAD_DIM ** -0.5, BF16))
        do = do_ref[rows, :]
        product = (do.astype(F32) * o_ref[rows, :].astype(F32)).T
        inner = jnp.concatenate(
            [jnp.sum(product[:HEAD_DIM], axis=0, keepdims=True), jnp.sum(product[HEAD_DIM:], axis=0, keepdims=True)], axis=1
        )
        do = masked_pair(do)
        lse = jnp.concatenate([lse_ref[0, pl.ds(0, 1), rows], lse_ref[0, pl.ds(1, 1), rows]], axis=1)
        pos_q = table[at] + lax.broadcasted_iota(jnp.int32, (1, 2 * BLK), 1) % BLK
        parts = []
        for here, base in path_spans(table, at, trunk):
            scores = dot_nt(keys[here, :], q)
            key_pos = base + lax.broadcasted_iota(jnp.int32, (here.size, 1), 0)
            weights = jnp.exp(jnp.where(key_pos <= pos_q, scores - lse, NEG))
            d_weights = dot_nt(values[here, :], do)
            parts.append((weights.astype(BF16), (weights * (d_weights - inner)).astype(BF16)))
        return q, do, parts

    coming = weights_of(0)
    for i in range(mine):
        q, do, parts = coming
        if i + 1 < mine:
            coming = weights_of(i + 1)
        dq_t = jnp.zeros((PAIR, 2 * BLK), F32)
        for (here, _), (weights, d_scores) in zip(path_spans(table, blocks + 5 * i, trunk), parts):
            dv_acc[here, :] += dot(weights, do)
            dk_acc[here, :] += dot(d_scores, q)
            dq_t = dq_t + dot(keys_t[:, here], d_scores)
        dq = dq_t.T * (HEAD_DIM ** -0.5)
        dq_ref[pl.ds(i * BLK, BLK), :] = jnp.where(lane < HEAD_DIM, dq[:BLK], dq[BLK:]).astype(BF16)
    for b in range(blocks):
        place = pl.ds(pl.multiple_of(table[b] * BLK, BLK), BLK)
        rows = pl.ds(b * BLK, BLK)
        dk_ref[rows, :] = dk_acc[place, :].astype(BF16)
        dv_ref[rows, :] = dv_acc[place, :].astype(BF16)


def attend_back(table, q, k, v, d_heads, heads, lse):
    mine, width = q.shape
    rows = k.shape[0]
    pairs = width // PAIR
    column = lambda n: pl.BlockSpec((n, PAIR), lambda p, table: (0, p))
    return pl.pallas_call(
        attend_back_kernel,
        grid_spec=pltpu.PrefetchScalarGridSpec(
            num_scalar_prefetch=1,
            grid=(pairs,),
            in_specs=[
                column(mine), column(rows), column(rows), column(mine), column(mine),
                pl.BlockSpec((1, 8, mine), lambda p, table: (p, 0, 0)),
            ],
            out_specs=[column(mine), column(rows), column(rows)],
            scratch_shapes=[
                pltpu.VMEM((rows, PAIR), BF16),
                pltpu.VMEM((rows, PAIR), BF16),
                pltpu.VMEM((PAIR, rows), BF16),
                pltpu.VMEM((rows, PAIR), F32),
                pltpu.VMEM((rows, PAIR), F32),
            ],
        ),
        out_shape=[
            jax.ShapeDtypeStruct((mine, width), BF16),
            jax.ShapeDtypeStruct((rows, width), BF16),
            jax.ShapeDtypeStruct((rows, width), BF16),
        ],
        compiler_params=pltpu.CompilerParams(vmem_limit_bytes=VMEM_LIMIT),
        cost_estimate=cost(mine * 1280 * width * 20, 8 * rows * width, mine * 1280 * width // HEAD_DIM),
        name="attend_back",
    )(table, q, k, v, d_heads, heads, lse)


GELU_C = 0.7978845608028654
GELU_A = 0.044715
CUTS = 4
MESH = pl.DeviceIdType.MESH
ANY = pl.BlockSpec(memory_space=pl.ANY)
VMEM = pl.BlockSpec(memory_space=pltpu.VMEM)


def low_shape(*dims):
    return jax.ShapeDtypeStruct(dims, BF16)


def low_vmem(*dims):
    return pltpu.VMEM(dims, BF16)


def run_kernel(body, ins, outs, scratch, identity, macs, near, far, **flags):
    scratch = dict(scratch, near=pltpu.SemaphoreType.DMA((near,)))
    params = dict(vmem_limit_bytes=VMEM_LIMIT)
    if far:
        scratch.update(send=pltpu.SemaphoreType.DMA((far,)), recv=pltpu.SemaphoreType.DMA((far,)))
        params.update(collective_id=identity, has_side_effects=True)
    names = [*ins, *outs, *scratch]

    def kernel(*refs):
        body(Moves(SimpleNamespace(**dict(zip(names, refs)))), **flags)

    results = pl.pallas_call(
        kernel,
        in_specs=[spec for _, spec in ins.values()],
        out_specs=[spec for _, spec in outs.values()],
        out_shape=[shape for shape, _ in outs.values()],
        scratch_shapes=list(scratch.values()),
        compiler_params=pltpu.CompilerParams(**params),
        cost_estimate=cost(macs, 0),
        name=body.__name__,
    )(*[value for value, _ in ins.values()])
    return SimpleNamespace(**dict(zip(outs, results)))


def xor_peer(index, k):
    if k == 1:
        return index + 1 - 2 * lax.rem(index, 2)
    if k == 2:
        return index + 2 - 4 * lax.rem(lax.div(index, 2), 2)
    return index + 3 - 2 * lax.rem(index, 4)


class Moves:
    def __init__(self, refs):
        self.refs, self.near, self.far, self.seen, self.left, self.sent = refs, 0, 0, set(), set(), []
        self.c, self.t, self.z = [lax.axis_index(axis) for axis in (DP, TENSOR, EXPERT)]
        self.x_peer, self.y_peer = [{TENSOR: xor_peer(self.t, k)} for k in (1, 2)]
        self.sibling = {DP: 1 - self.c}
        self.z_peers = [{EXPERT: xor_peer(self.z, k)} for k in (1, 2, 3)]

    def local(self, src, dst):
        assert self.near < self.refs.near.shape[0]
        copy = pltpu.make_async_copy(src, dst, self.refs.near.at[self.near])
        self.near += 1
        copy.start()
        return copy

    def remote(self, src, dst, device):
        assert self.far < self.refs.send.shape[0]
        copy = pltpu.make_async_remote_copy(
            src_ref=src, dst_ref=dst, send_sem=self.refs.send.at[self.far], recv_sem=self.refs.recv.at[self.far],
            device_id=device, device_id_type=MESH,
        )
        self.far += 1
        copy.start()
        self.sent.append(copy)
        return copy

    def need(self, *copies):
        for copy in copies:
            if id(copy) not in self.seen:
                self.seen.add(id(copy))
                copy.wait()

    def arrived(self, *copies):
        for copy in copies:
            if id(copy) not in self.seen:
                self.seen.add(id(copy))
                copy.wait_recv()

    def finish(self):
        self.gone(*self.sent)

    def gone(self, *copies):
        for copy in copies:
            if id(copy) not in self.left:
                self.left.add(id(copy))
                copy.wait_send()

    def greet(self, devices):
        barrier = pltpu.get_barrier_semaphore()
        for device in devices:
            pl.semaphore_signal(barrier, inc=1, device_id=device, device_id_type=MESH)
        return lambda: pl.semaphore_wait(barrier, len(devices))


def add_low(ref, *more):
    total = ref[...].astype(F32)
    for other in more:
        total = total + other[...].astype(F32)
    return total


class Scatter:
    def __init__(self, moves, pack, core_in, g_in, piece):
        self.moves, self.pack, self.core_in, self.g_in, self.piece = moves, pack, core_in, g_in, piece
        self.peers = lax.axis_size(TENSOR)
        self.size = pack.shape[1] // 2
        c, t = moves.c, moves.t
        self.index = [t] + [xor_peer(t, k) for k in (1, 2, 3)]
        self.slots = self.index if core_in is None else [c * self.peers + i for i in self.index]
        self.flow = [dict(), dict()]

    def rows(self, h):
        return pl.ds(h * self.size, self.size)

    def sides(self, h):
        half = self.size // 2
        return pl.ds(h * self.size, half), pl.ds(h * self.size + half, half)

    def swap(self, h):
        m = self.moves
        there = pl.ds((1 - m.c) * self.peers, self.peers)
        self.flow[h][0] = m.remote(self.pack.at[there, self.rows(h)], self.core_in.at[:, self.rows(h)], m.sibling)

    def out(self, h):
        m, pack, slots, f = self.moves, self.pack, self.slots, self.flow[h]
        left, right = self.sides(h)
        if self.core_in is not None:
            m.arrived(f[0])
            for j in (3, 1, 2, 0):
                pack[slots[j], self.rows(h), :] = add_low(
                    pack.at[slots[j], self.rows(h)], self.core_in.at[self.index[j], self.rows(h)]
                ).astype(BF16)
        f[1] = m.remote(pack.at[slots[3], left], self.g_in.at[h, 0], m.x_peer)
        f[2] = m.remote(pack.at[slots[3], right], self.g_in.at[h, 1], m.y_peer)
        f[3] = m.remote(pack.at[slots[1], left], self.g_in.at[h, 2], m.x_peer)
        f[4] = m.remote(pack.at[slots[2], right], self.g_in.at[h, 3], m.y_peer)

    def turn(self, h):
        m, pack, slots, f = self.moves, self.pack, self.slots, self.flow[h]
        left, right = self.sides(h)
        m.arrived(f[1])
        pack[slots[2], left, :] = add_low(pack.at[slots[2], left], self.g_in.at[h, 0]).astype(BF16)
        f[5] = m.remote(pack.at[slots[2], left], self.g_in.at[h, 4], m.y_peer)
        m.arrived(f[2])
        pack[slots[1], right, :] = add_low(pack.at[slots[1], right], self.g_in.at[h, 1]).astype(BF16)
        f[6] = m.remote(pack.at[slots[1], right], self.g_in.at[h, 5], m.x_peer)

    def end(self, h):
        f = self.flow[h]
        self.moves.arrived(f[3], f[4], f[5], f[6])
        for cut, a, b in zip(self.sides(h), (2, 3), (4, 5)):
            total = add_low(self.pack.at[self.slots[0], cut], self.g_in.at[h, a], self.g_in.at[h, b])
            self.piece[cut, :] = total.astype(BF16)


class ExpertScatter:
    def __init__(self, moves, pack, own, keep, inbox):
        self.m, self.pack, self.own, self.keep, self.inbox = moves, pack, own, keep, inbox
        half = own.shape[1] // 2
        self.left, self.right = pl.ds(0, half), pl.ds(half, half)
        self.index = [moves.t] + [xor_peer(moves.t, k) for k in (1, 2, 3)]

    def load(self):
        p, i, m = self.pack, self.index, self.m
        return [
            m.local(p.at[i[0]], self.own),
            m.local(p.at[i[2], :, self.left], self.keep.at[0]),
            m.local(p.at[i[1], :, self.right], self.keep.at[1]),
        ]

    def out(self):
        p, i, m = self.pack, self.index, self.m
        self.flow = [
            m.remote(p.at[i[3], :, self.left], self.inbox.at[0], m.x_peer),
            m.remote(p.at[i[3], :, self.right], self.inbox.at[1], m.y_peer),
            m.remote(p.at[i[1], :, self.left], self.inbox.at[2], m.x_peer),
            m.remote(p.at[i[2], :, self.right], self.inbox.at[3], m.y_peer),
        ]

    def turn(self):
        m = self.m
        self.second = []
        for n, device in enumerate((m.y_peer, m.x_peer)):
            if self.flow:
                m.arrived(self.flow[n])
            self.keep[n] = add_low(self.keep.at[n], self.inbox.at[n]).astype(BF16)
            self.second.append(m.remote(self.keep.at[n], self.inbox.at[4 + n], device))

    def end(self):
        self.m.arrived(*self.flow, *self.second)
        for n, cut in enumerate((self.left, self.right)):
            self.own[:, cut, :] = add_low(self.own.at[:, cut], self.inbox.at[2 + n], self.inbox.at[4 + n]).astype(BF16)


def expert_scatter_scratch(half, width):
    return dict(e_own=low_vmem(2, half, width), e_keep=low_vmem(2, 2, half // 2, width), e_in=low_vmem(6, 2, half // 2, width))


class Gather:
    def __init__(self, moves, pack):
        self.moves, self.pack = moves, pack
        self.half = pack.shape[1] // 2
        self.slots = [moves.c * (pack.shape[0] // 2) + i for i in [moves.t] + [xor_peer(moves.t, k) for k in (1, 2, 3)]]

    def out(self):
        own = self.pack.at[self.slots[0]]
        self.first = [self.moves.remote(own, own, device) for device in (self.moves.x_peer, self.moves.y_peer)]

    def turn(self):
        m = self.moves
        self.swaps, self.second = [], []
        for k, device in ((1, m.y_peer), (2, m.x_peer)):
            m.arrived(self.first[k - 1])
            piece = self.pack.at[self.slots[k], pl.ds((k - 1) * self.half, self.half)]
            self.second.append(m.remote(piece, piece, device))
            self.swap(k)

    def swap(self, k):
        whole = self.pack.at[self.slots[k]]
        self.swaps.append(self.moves.remote(whole, whole, self.moves.sibling))

    def end(self):
        self.moves.arrived(*self.second)
        self.swap(3)
        self.moves.arrived(*self.swaps)


def attention_rows(r, depth, i):
    return r.w_qkv.at[depth, i] if i < 3 else r.w_out.at[depth]


def scatter_scratch(peers, half, width):
    return dict(
        pack_s=low_vmem(2 * peers, half, width), core_in=low_vmem(peers, half, width),
        g_in=low_vmem(2, 6, half // 4, width), piece=low_vmem(half, width),
    )


def one_hot(slot_row, k, size):
    index = lax.broadcasted_iota(jnp.int32, (size, slot_row.shape[1]), 0) + k * size
    return jnp.where(index == slot_row[...], 1.0, 0.0).astype(BF16)


def combine(m, slot_row, source, copies, back, size):
    total = dot_tn(one_hot(slot_row, 0, size), source[pl.ds(0, size), :])
    for k in (1, 2, 3):
        m.arrived(copies[k])
        total = total + dot_tn(one_hot(slot_row, k, size), back[k - 1])
    return total.astype(BF16)


def expert_part(m, forward, backward, remote, hosted, reduces, fetches, experts, depth):
    r = m.refs
    if hosted:
        own_up, own_down = r.w_in.at[depth, 0], r.w_down.at[depth, 0]
    up, down, hidden, slope, rows, outs = r.up, r.down, r.hidden_s, r.slope_s, r.rows_s, r.outs_s
    count, width = rows.shape
    inner = up.shape[1]
    half = width // 2
    peers = inner // width
    size = count // CUTS
    tile = 256
    cuts = [pl.ds(k * size, size) for k in range(CUTS)]
    met = []
    if remote:
        met += m.z_peers
    if hosted or reduces:
        met += [m.x_peer, m.y_peer]
    if remote:
        met += [m.sibling]
    ready = m.greet(met) if met else None

    def up_at(c, t, start=0, rows=half):
        return up.at[pl.ds(pl.multiple_of(c * half + start, half // 2), rows), pl.ds(pl.multiple_of(t * width, width), width)]

    def down_at(c, t, start=0, rows=half):
        return down.at[pl.ds(pl.multiple_of(t * width + c * half + start, half // 2), rows)]

    loads, weight_loads = [], []
    if not remote:
        if forward:
            loads.append(m.local(r.x, rows))
        if backward:
            loads.append(m.local(r.g, r.d_s))
    if hosted:
        weight_loads.append(m.local(own_up, up.at[:, pl.ds(pl.multiple_of(m.t * width, width), width)]))
        weight_loads.append(m.local(own_down, down.at[pl.ds(pl.multiple_of(m.t * width, width), width)]))
    else:
        for t in range(peers):
            for c in range(2):
                weight_loads += [m.local(r.w.at[c, t, 0], up_at(c, t)), m.local(r.w.at[c, t, 1], down_at(c, t))]
    if backward and not forward:
        loads += [m.local(a, b) for a, b in ((r.rows, rows), (r.out, outs), (r.slope, slope), (r.hidden, hidden))]
    if ready:
        ready()

    def dispatch(source, target, stage):
        copies = {}
        x = source[...]
        for k in (2, 1, 3):
            stage[k - 1] = dot(one_hot(r.slot_row, k, size), x).astype(BF16)
            copies[k] = m.remote(stage.at[k - 1], target.at[cuts[k]], m.z_peers[k - 1])
        target[cuts[0], :] = dot(one_hot(r.slot_row, 0, size), x).astype(BF16)
        return copies

    def give_back(source, k):
        return m.remote(source.at[cuts[k]], r.back.at[k - 1], m.z_peers[k - 1])

    def forward_block(cut, at):
        u = dot(rows[cut, :], up[:, at])
        square = u * u
        gate = 0.5 + 0.5 * jnp.tanh(u * (GELU_C + (GELU_C * GELU_A) * square))
        value = u * gate
        hidden[cut, at] = value.astype(BF16)
        grow = gate + value * (1.0 - gate) * (2 * GELU_C + (6 * GELU_C * GELU_A) * square)
        slope[cut, at] = grow.astype(BF16)

    def forward_peer(cut, t):
        for col in range(0, width, tile):
            forward_block(cut, pl.ds(pl.multiple_of(t * width + col, tile), tile))

    def forward_down(cut):
        outs[cut, :] = dot(hidden[cut, :], down[...]).astype(BF16)

    def backward_chunk(cut):
        d = r.d_s[cut, :]
        for col in range(0, inner, tile):
            at = pl.ds(col, tile)
            d_hidden = dot_nt(d, down[at, :])
            slope[cut, at] = (d_hidden * slope[cut, at].astype(F32)).astype(BF16)
        x = rows[cut, :]
        logits = dot(x, r.route[depth])
        lane = lax.broadcasted_iota(jnp.int32, logits.shape, 1)
        logits = jnp.where(lane < experts, logits, NEG)
        router = jnp.exp(logits - jnp.max(logits, axis=1, keepdims=True))
        router = router / jnp.sum(router, axis=1, keepdims=True)
        amount = jnp.sum(outs[cut, :].astype(F32) * d.astype(F32), axis=1, keepdims=True)
        d_log = (amount * (jnp.where(lane == m.z, 1.0, 0.0) - router)).astype(BF16)
        r.log_s[cut, :] = d_log
        d_rows = dot_nt(slope[cut, :], up[...]) + dot_nt(d_log, r.route[depth])
        r.back_s[cut, :] = d_rows.astype(BF16)
        return jnp.sum(d_rows * x.astype(F32), axis=0, keepdims=True)

    sent_x = sent_d = None
    saves, returns = [], {}
    scatter = None
    if fetches:
        shard = half // 2
        next_loads = [
            m.local(attention_rows(r, depth + 1, i), r.next_s.at[i // 2 * peers + m.t, pl.ds(i % 2 * shard, shard)]) for i in range(4)
        ]
        fetch = Gather(m, r.next_s)
    if hosted:
        first = {}
        mine = pl.ds(pl.multiple_of(m.c * half, half), half)
        for at, own in ((up_at, own_up), (down_at, own_down)):
            for k, device in ((1, m.x_peer), (2, m.y_peer)):
                first[at, k] = m.remote(own.at[mine], at(m.c, m.t), device)
    if reduces:
        scatter = Scatter(m, r.pack_s, r.core_in, r.g_in, r.piece)
        pack_load = m.local(r.pack, r.pack_s)
        e_scatter = ExpertScatter(m, r.e_pack, r.e_own, r.e_keep, r.e_in)
        e_scatter.out()
        e_loads = e_scatter.load()
    if remote and forward:
        sent_x = dispatch(r.x, rows, r.stage_x)
    if remote and backward:
        sent_d = dispatch(r.g, r.d_s, r.stage_d)
    if reduces:
        m.need(pack_load)
        scatter.swap(0)
        scatter.swap(1)
    m.need(*loads, *weight_loads)
    if hosted:
        tens = [m.t] + [xor_peer(m.t, k) for k in (1, 2, 3)]
        onward, swaps = {up_at: [], down_at: []}, {}

        def pass_on(at):
            for k, device in ((1, m.y_peer), (2, m.x_peer)):
                m.arrived(first[at, k])
                piece = at(m.c, tens[k], (k - 1) * (half // 2), half // 2)
                onward[at].append(m.remote(piece, piece, device))
                swap(at, k)

        def swap(at, k):
            swaps[at, k] = m.remote(at(m.c, tens[k]), at(m.c, tens[k]), m.sibling)

        forward_peer(cuts[0], tens[0])
        m.arrived(sent_x[1])
        forward_peer(cuts[1], tens[0])
        pass_on(up_at)
        pass_on(down_at)
        m.arrived(sent_x[2], sent_x[3])
        forward_peer(pl.ds(2 * size, 2 * size), tens[0])
        for k in (1, 2, 3):
            if k == 3:
                m.arrived(*onward[up_at])
                swap(up_at, 3)
            m.arrived(swaps[up_at, k])
            if k < 3:
                forward_peer(pl.ds(0, count), tens[k])
        m.arrived(*onward[down_at])
        swap(down_at, 3)
        if fetches:
            m.need(*next_loads)
            fetch.out()
        for first_k in (2, 0):
            pair = pl.ds(first_k * size, 2 * size)
            forward_peer(pair, tens[3])
            m.arrived(*[swaps[down_at, k] for k in (1, 2, 3)])
            forward_down(pair)
            for k in (first_k, first_k + 1):
                if k and not backward:
                    returns[k] = give_back(outs, k)
        if not backward:
            for c in range(2):
                for t in range(peers):
                    saves += [m.local(up_at(c, t), r.w.at[c, t, 0]), m.local(down_at(c, t), r.w.at[c, t, 1])]
        if fetches:
            fetch.turn()
            fetch.end()
            saves.append(m.local(r.next_s, r.next_all))
    elif forward:
        for k in range(CUTS):
            if remote and k:
                m.arrived(sent_x[k])
            for t in range(peers):
                forward_peer(cuts[k], t)
            forward_down(cuts[k])
            if remote and k and not backward:
                returns[k] = give_back(outs, k)
    if forward:
        if not backward:
            saves += [m.local(hidden, r.hidden), m.local(slope, r.slope), m.local(rows, r.rows)]
        saves.append(m.local(outs, r.out))
    if backward:
        gain = jnp.zeros((1, width), F32)
        for k in range(CUTS):
            if remote and k:
                m.arrived(sent_d[k])
            gain = gain + backward_chunk(cuts[k])
            if remote and k:
                returns[k] = give_back(r.back_s, k)
            if reduces and k == 0:
                scatter.out(0)
                scatter.out(1)
            if reduces and k == 2:
                scatter.turn(0)
                scatter.turn(1)
        if not remote:
            saves.append(m.local(r.back_s, r.result))
        if reduces:
            m.need(*e_loads)
            e_scatter.turn()
        r.turned[...] = rows[...].T
        route = dot_tn(r.log_s[...], rows[...])
        pad = r.small.shape[0] - experts - 1
        r.small[...] = jnp.concatenate([route[:experts], gain, jnp.zeros((pad, width), F32)], axis=0)
        swapped = []
        if hosted:
            m.gone(*onward[up_at], *onward[down_at], *swaps.values())
        for t in range(peers):
            at = pl.ds(t * width, width)
            up[:, at] = dot(r.turned[...], slope[:, at]).astype(BF16)
            down[at, :] = dot_tn(hidden[:, at], r.d_s[...]).astype(BF16)
            if remote:
                swapped.append([m.remote(at(1 - m.c, t), r.grads_in.at[t, i], m.sibling) for i, at in enumerate((up_at, down_at))])
            else:
                for c in range(2):
                    saves += [m.local(up_at(c, t), r.grads.at[c, t, 0]), m.local(down_at(c, t), r.grads.at[c, t, 1])]
    if reduces:
        for h in range(2):
            scatter.end(h)
        e_scatter.end()
        saves += [m.local(r.piece, r.summed), m.local(r.e_own, r.e_summed)]
    if remote:
        if backward:
            for t in range(peers):
                for i, at in enumerate((up_at, down_at)):
                    m.arrived(swapped[t][i])
                    here = at(m.c, t)
                    here[...] = add_low(here, r.grads_in.at[t, i]).astype(BF16)
                    saves.append(m.local(here, r.grads.at[t, i]))
            if reduces:
                for i, at in enumerate((up_at, down_at)):
                    for box, k, start in ((r.to_x.at[0], 3, 0), (r.to_x.at[1], 1, 0), (r.to_y.at[0], 3, 1), (r.to_y.at[1], 2, 1)):
                        saves.append(m.local(at(m.c, xor_peer(m.t, k), start * (half // 2), half // 2), box.at[i]))
        r.result[...] = combine(m, r.slot_row, r.back_s if backward else outs, returns, r.back, size)
    m.finish()
    m.need(*saves)


def expert_call(plan, experts, count, w=None, own=None, x=None, g=None, kept=None, route=None, pack=None, fetch=None, depth=0):
    slots = plan[0]
    forward, backward, remote, hosted, reduces = x is not None, g is not None, experts == CUTS, own is not None, pack is not None
    tokens, width = (x if forward else g).shape
    peers = lax.axis_size(TENSOR)
    half, inner = width // 2, peers * width
    w_shape = low_shape(2, peers, 2, half, width)
    data = VMEM if remote else ANY
    rows_shape, inner_shape = low_shape(count, width), low_shape(count, inner)
    ins, outs = {}, {}
    if hosted:
        ins.update(w_in=(own[0], ANY), w_down=(own[1], ANY))
        if not backward:
            outs.update(w=(w_shape, ANY))
    else:
        ins.update(w=(w, ANY))
    if remote:
        ins.update(slot_row=(slots[None, :], VMEM))
    if forward:
        ins.update(x=(x, data))
    if backward:
        ins.update(g=(g, data), route=(route, VMEM))
        if not forward:
            ins.update(rows=(kept.rows, ANY), out=(kept.out, ANY), hidden=(kept.hidden, ANY), slope=(kept.slope, ANY))
    if remote or backward:
        outs.update(result=(low_shape(tokens if remote else count, width), data))
    if forward:
        outs.update(out=(rows_shape, ANY))
        if not backward:
            outs.update(rows=(rows_shape, ANY), hidden=(inner_shape, ANY), slope=(inner_shape, ANY))
    if backward:
        outs.update(grads=(low_shape(peers, 2, half, width) if remote else w_shape, ANY))
        outs.update(small=(jax.ShapeDtypeStruct((-(-(experts + 2) // 8) * 8, width), F32), VMEM))
    scratch = dict(
        up=low_vmem(width, inner), down=low_vmem(inner, width), hidden_s=low_vmem(count, inner), slope_s=low_vmem(count, inner),
        rows_s=low_vmem(count, width), outs_s=low_vmem(count, width),
    )
    if backward:
        scratch.update(
            d_s=low_vmem(count, width), back_s=low_vmem(count, width), log_s=low_vmem(count, BLK), turned=low_vmem(width, count)
        )
    if backward and remote:
        scratch.update(grads_in=low_vmem(peers, 2, half, width))
    if fetch is not None:
        ins.update(w_qkv=(fetch[0], ANY), w_out=(fetch[1], ANY))
        outs.update(next_all=(low_shape(2 * peers, half, width), ANY))
        scratch.update(next_s=low_vmem(2 * peers, half, width))
    if reduces:
        ins.update(pack=(pack[0], ANY), e_pack=(pack[1], ANY))
        box = (low_shape(2, 2, half // 2, width), ANY)
        outs.update(summed=(low_shape(half, width), ANY), e_summed=(low_shape(2, half, width), ANY), to_x=box, to_y=box)
        scratch.update(scatter_scratch(peers, half, width), **expert_scatter_scratch(half, width))
    if remote:
        part = low_vmem(3, count // CUTS, width)
        scratch.update(back=part)
        if forward:
            scratch.update(stage_x=part)
        if backward:
            scratch.update(stage_d=part)
    return run_kernel(
        expert_part, ins, outs, scratch, forward + 2 * backward, count * width * inner, 64, 48 if remote else 0,
        forward=forward, backward=backward, remote=remote, hosted=hosted, reduces=reduces,
        fetches=fetch is not None, experts=experts, depth=depth,
    )


def experts_forward(plan, token_rows, experts, capacity, w, own, fetch, depth):
    count = experts * capacity
    if experts == CUTS:
        got = expert_call(plan, experts, count, own=own, x=token_rows, fetch=fetch, depth=depth)
        return got.result, got
    got = expert_call(plan, experts, count, w=w, x=send_rows(plan[1], token_rows, experts, capacity))
    got.w = w
    return return_rows(plan[1], got.out, experts, capacity).astype(BF16), got


def experts_backward(plan, d_low, kept, route, experts, capacity, pack, depth):
    count = experts * capacity
    if experts == CUTS:
        return expert_call(plan, experts, count, w=kept.w, g=d_low, kept=kept, route=route, pack=pack, depth=depth)
    d_sent = send_rows(plan[1], d_low, experts, capacity)
    got = expert_call(plan, experts, count, w=kept.w, g=d_sent, kept=kept, route=route, depth=depth)
    got.result = return_rows(plan[1], got.result, experts, capacity).astype(BF16)
    got.summed = scatter_all(pack)
    return got


def experts_both(w, own, plan, token_rows, d_low, route, experts, capacity, depth):
    count = experts * capacity
    if experts == CUTS:
        return expert_call(plan, experts, count, own=own, x=token_rows, g=d_low, route=route, depth=depth)
    rows = send_rows(plan[1], token_rows, experts, capacity)
    d_sent = send_rows(plan[1], d_low, experts, capacity)
    got = expert_call(plan, experts, count, w=w, x=rows, g=d_sent, route=route, depth=depth)
    got.result = return_rows(plan[1], got.result, experts, capacity).astype(BF16)
    return got


def project_part(m, hosted):
    r = m.refs
    rows, w = r.n_s, r.w_s
    tokens = r.x.shape[0]
    peers = rows.shape[0] // tokens
    shard = w.shape[1] // peers
    c, t = m.c, m.t
    ready = m.greet([m.x_peer, m.y_peer] + ([m.sibling] if hosted else []))
    at = lambda index: pl.ds(pl.multiple_of(index * shard, shard), shard)
    first_load = m.local(r.x, rows.at[pl.ds(0, tokens)])
    loads = []
    if hosted:
        for i in range(4):
            loads.append(m.local(attention_rows(r, 0, i), w.at[i, at(t)]))
    else:
        for i in range(4):
            for j in range(peers):
                piece = r.w.at[i // 2, j, r.w.shape[2] - 1, pl.ds(i % 2 * shard, shard)]
                loads.append(m.local(piece, w.at[i, pl.ds(j * shard, shard)]))
    ready()
    half = tokens // 2
    m.need(first_load)
    cut = lambda j, part: pl.ds(j * tokens + part * half, half)

    def send(j, part, to, device):
        return m.remote(rows.at[cut(j, part)], rows.at[cut(to, part)], device)

    first, second, swaps, kept = {}, [], [], []
    if hosted:
        m.need(*loads)
        for h in range(2):
            mine = w.at[2 * c + h, at(t)]
            first[1, h] = m.remote(mine, mine, m.x_peer)
            first[2, h] = m.remote(mine, mine, m.y_peer)
    a_low, b_high = send(0, 0, 1, m.x_peer), send(0, 1, 2, m.y_peer)
    if hosted:
        for h in range(2):
            for k, onward, part in ((1, m.y_peer, 0), (2, m.x_peer, 1)):
                m.arrived(first[k, h])
                start = pl.multiple_of(xor_peer(t, k) * shard + part * (shard // 2), shard // 2)
                piece = w.at[2 * c + h, pl.ds(start, shard // 2)]
                second.append(m.remote(piece, piece, onward))
                whole = w.at[2 * c + h, at(xor_peer(t, k))]
                swaps.append(m.remote(whole, whole, m.sibling))
    a_high, b_low = send(0, 1, 1, m.x_peer), send(0, 0, 2, m.y_peer)
    m.arrived(a_low)
    c_low = send(1, 0, 3, m.y_peer)
    m.arrived(b_high)
    c_high = send(2, 1, 3, m.x_peer)
    if hosted:
        m.arrived(*second)
        for h in range(2):
            whole = w.at[2 * c + h, at(xor_peer(t, 3))]
            swaps.append(m.remote(whole, whole, m.sibling))
        m.arrived(*swaps)
    else:
        m.need(*loads)
    for i in range(4):
        kept.append(m.local(w.at[i], r.w_all.at[i]))

    def keys_values(start, size):
        here = pl.ds(start, size)
        x = rows[here, :]
        for i, near, far in ((1, r.k_s, r.k), (2, r.v_s, r.v)):
            near[here, :] = dot_nt(x, w[i]).astype(BF16)
            kept.append(m.local(near.at[here], far.at[here]))

    r.q_s[...] = dot_nt(rows[pl.ds(0, tokens), :], w[0]).astype(BF16)
    kept.append(m.local(r.q_s, r.q))
    keys_values(0, tokens)
    m.arrived(a_high)
    keys_values(tokens, tokens)
    m.arrived(b_low)
    keys_values(2 * tokens, tokens)
    r.turned_s[...] = w[3].T
    kept.append(m.local(r.turned_s, r.out_turned))
    m.arrived(c_low)
    keys_values(3 * tokens, half)
    m.arrived(c_high)
    keys_values(3 * tokens + half, half)
    kept.append(m.local(rows, r.n))
    m.finish()
    m.need(*kept)


def project(x, w, hosted, peers):
    tokens, width = x.shape
    every = peers * tokens
    outs = dict(
        q=(low_shape(tokens, width), ANY), k=(low_shape(every, width), ANY), v=(low_shape(every, width), ANY),
        n=(low_shape(every, width), ANY), w_all=(low_shape(4, width, width), ANY),
        out_turned=(low_shape(width, width), ANY),
    )
    scratch = dict(
        n_s=low_vmem(every, width), w_s=low_vmem(4, width, width), q_s=low_vmem(tokens, width),
        k_s=low_vmem(every, width), v_s=low_vmem(every, width), turned_s=low_vmem(width, width),
    )
    given = dict(w_qkv=(w[0], ANY), w_out=(w[1], ANY)) if hosted else dict(w=(w, ANY))
    return run_kernel(
        project_part, dict(x=(x, ANY), **given), outs, scratch, 6 + hosted, 9 * tokens * width * width, 40, 24, hosted=hosted
    )


def project_back_part(m, full, returns):
    r = m.refs
    tokens, width = r.dq_s.shape
    peers = r.dk_s.shape[0] // tokens
    shard = width // peers
    c, z = m.c, m.z
    local, remote, need, arrived = m.local, m.remote, m.need, m.arrived
    ready = m.greet([m.x_peer, m.y_peer] + ([m.sibling] if full else []) + (m.z_peers if full or returns else []))
    rows_of = lambda j: pl.ds(j * tokens, tokens)
    w = r.w_s
    weights_in = {i: local(r.w.at[i], w.at[i]) for i in (1, 2)}
    parts_in = {}
    for j in (3, 1, 2, 0):
        parts_in[j] = [local(a.at[rows_of(j)], b.at[rows_of(j)]) for a, b in ((r.dk, r.dk_s), (r.dv, r.dv_s))]
    above_in = local(r.above, r.above_s) if full else None
    rest_in = [local(a, b) for a, b in ((r.n, r.n_s), (r.dq, r.dq_s), (r.heads, r.heads_s), (r.d_att, r.d_att_s))]
    weights_in[0] = local(r.w.at[0], w.at[0])
    swaps_in = []
    if full:
        e_scatter = ExpertScatter(m, r.e0, r.e_own, r.e_keep, r.e_in)
        e_scatter.flow = []
        e_loads = [local(a.at[n], r.e_in.at[2 * n + i]) for n in range(2) for i, a in enumerate((r.from_x, r.from_y))]
        e_loads += e_scatter.load()
        swaps_in = [local(r.e1.at[i], r.e_s.at[i, 1, c]) for i in range(2)]
    ready()
    tops, ends = pl.ds(0, tokens // 2), pl.ds(tokens // 2, tokens // 2)

    def partial(j):
        at = rows_of(j)
        return dot(r.dk_s[at, :], w[1]) + dot(r.dv_s[at, :], w[2])

    over_x, over_y = {}, {}

    stages = {1: r.p1, 2: r.p2, 3: r.p3}

    def rows_part(*which):
        need(weights_in[1], weights_in[2])
        for j in which:
            need(*parts_in[j])
            stages[j][...] = partial(j).astype(BF16)

    def rows_send(*which):
        for j in which:
            if j != 2:
                over_x[j] = remote(stages[j].at[tops], r.row_in.at[j // 2], m.x_peer)
            if j != 1:
                over_y[j] = remote(stages[j].at[ends], r.row_in.at[2 + j // 3], m.y_peer)

    def rows_turn():
        arrived(over_x[3])
        r.p2[tops, :] = add_low(r.p2.at[tops], r.row_in.at[1]).astype(BF16)
        over_y[1] = remote(r.p2.at[tops], r.row_in.at[4], m.y_peer)
        arrived(over_y[3])
        r.p1[ends, :] = add_low(r.p1.at[ends], r.row_in.at[3]).astype(BF16)
        over_x[2] = remote(r.p1.at[ends], r.row_in.at[5], m.x_peer)

    def rows_own():
        need(*parts_in[0], weights_in[0], rest_in[1])
        r.dn[...] = partial(0) + dot(r.dq_s[...], w[0])

    def rows_end():
        for copy, slot, cut in ((over_x[1], 0, tops), (over_y[2], 2, ends), (over_y[1], 4, tops), (over_x[2], 5, ends)):
            arrived(copy)
            r.dn[cut, :] += r.row_in[slot].astype(F32)

    pack = r.pack_s
    part = lambda i: pl.ds(i % 2 * shard, shard)

    def weight_grad(i):
        need(*rest_in, weights_in[0], *[p for j in (3, 1, 2, 0) for p in parts_in[j]])
        if i == 0:
            g = dot_tn(r.dq_s[...], r.n_s[rows_of(0), :])
        elif i == 3:
            g = dot_tn(r.heads_s[...], r.d_att_s[...])
        else:
            g = dot_tn((r.dk_s if i == 1 else r.dv_s)[...], r.n_s[...])
        low = g.astype(BF16)
        for j in range(peers):
            pack[i // 2 * peers + j, part(i), :] = low[j * shard : (j + 1) * shard]
        return jnp.sum(g * w[i].astype(F32), axis=0, keepdims=True) if i < 3 else 0.0

    if not full:
        copies = {}
        if returns:
            size = r.out.shape[0] // CUTS
            out_in = local(r.out.at[pl.ds(0, size)], r.out_s)
            for k in (2, 3, 1):
                copies[k] = remote(r.out.at[pl.ds(k * size, size)], r.back.at[k - 1], m.z_peers[k - 1])
        for j in (3, 1, 2):
            rows_part(j)
            rows_send(j)
        total = weight_grad(1)
        rows_turn()
        rows_own()
        total = total + weight_grad(2) + weight_grad(0) + weight_grad(3)
        r.att[...] = jnp.broadcast_to(total, r.att.shape)
        saved = local(pack, r.pack)
        if returns:
            need(out_in)
            r.result[...] = combine(m, r.slot_row, r.out_s, copies, r.back, size)
        rows_end()
        m.finish()
        need(saved)
        return

    mini = shard // 4
    at_z = lambda h, index: pl.ds(pl.multiple_of(h * shard + index * mini, mini), mini)
    both, z_in = r.both, r.z_in

    def z_out(source, layer, h):
        return [remote(source.at[at_z(h, xor_peer(z, k))], z_in.at[layer * 2 + h, k - 1], m.z_peers[k - 1]) for k in (1, 2, 3)]

    def z_sum(source, copies, layer, h):
        arrived(*copies)
        here = both.at[layer, c, at_z(h, z)]
        both[layer, c, at_z(h, z), :] = add_low(
            source.at[at_z(h, z)], *[z_in.at[layer * 2 + h, k] for k in range(3)]
        ).astype(BF16)
        return [remote(here, here, device) for device in m.z_peers]

    def core_out(copies, layer, h):
        arrived(*copies)
        here = both.at[layer, c, pl.ds(h * shard, shard)]
        return remote(here, here, m.sibling)

    scatter = Scatter(m, pack, r.core_in, r.g_in, r.piece)
    need(above_in)
    above = [z_out(r.above_s, 1, h) for h in range(2)]
    rows_part(3)
    rows_send(3)
    total = weight_grad(3) + weight_grad(1)
    scatter.swap(1)
    need(*e_loads)
    e_scatter.turn()
    total = total + weight_grad(0) + weight_grad(2)
    scatter.swap(0)
    small_s, small_r = r.small_s, r.small_r
    row = lax.broadcasted_iota(jnp.int32, r.small.shape, 0)
    att_row = r.small_in.shape[0] // 2 - 1
    small_s[0] = jnp.where(row == att_row, total, r.small_in[...])
    small_1 = remote(small_s.at[0], small_r.at[0], m.sibling)
    above = [z_sum(r.above_s, above[h], 1, h) for h in range(2)]
    arrived(small_1)
    small_s[1] = small_s[0] + small_r[0]
    small_2 = [remote(small_s.at[1], small_r.at[k], m.z_peers[k - 1]) for k in (1, 2, 3)]
    scatter.out(1)
    scatter.out(0)
    rows_part(1)
    rows_part(2)
    arrived(*small_2)
    small_s[2] = small_s[1] + small_r[1] + small_r[2] + small_r[3]
    scatter.turn(1)
    small_3 = remote(small_s.at[2], small_r.at[4], m.x_peer)
    scatter.turn(0)
    rows_send(1, 2)
    above = [core_out(above[h], 1, h) for h in range(2)]
    need(*swaps_in)
    e_copies = [remote(r.e_s.at[i, 1, c], r.e_s.at[i, 1, c], m.sibling) for i in range(2)]
    rows_own()
    scatter.end(1)
    piece_1 = z_out(r.piece, 0, 1)
    scatter.end(0)
    piece_0 = z_out(r.piece, 0, 0)
    arrived(small_3)
    small_s[3] = small_s[2] + small_r[4]
    rows_turn()
    small_4 = remote(small_s.at[3], small_r.at[5], m.y_peer)
    piece_1 = z_sum(r.piece, piece_1, 0, 1)
    piece_0 = z_sum(r.piece, piece_0, 0, 0)
    e_scatter.end()
    for i in range(2):
        r.e_s[i, 0, c] = r.e_own[i]
        e_copies.append(remote(r.e_s.at[i, 0, c], r.e_s.at[i, 0, c], m.sibling))
    arrived(*e_copies)
    saved = [local(r.e_s.at[0], r.e_up), local(r.e_s.at[1], r.e_down)]
    piece_1 = core_out(piece_1, 0, 1)
    piece_0 = core_out(piece_0, 0, 0)
    rows_end()
    arrived(*above, piece_1, piece_0)
    for l in range(2):
        saved += [
            local(both.at[l, 0], r.g_mix.at[l, pl.ds(0, 2 * shard)]),
            local(both.at[l, 1, pl.ds(0, shard)], r.g_mix.at[l, pl.ds(2 * shard, shard)]),
            local(both.at[l, 1, pl.ds(shard, shard)], r.g_out.at[l]),
        ]
    arrived(small_4)
    r.small[...] = small_s[3] + small_r[5]
    m.finish()
    need(*saved)


def project_back(w, dq, dk, dv, normed_all, heads, d_att, above=None, small=None, swaps=None, out=None, slots=None):
    full, returns = above is not None, out is not None
    tokens, width = dq.shape
    rows = dk.shape[0]
    half = width // 2
    peers = rows // tokens
    shape = jax.ShapeDtypeStruct
    ins = dict(
        w=(w, ANY), dq=(dq, ANY), dk=(dk, ANY), dv=(dv, ANY), n=(normed_all, ANY), heads=(heads, ANY), d_att=(d_att, ANY),
    )
    outs = dict(dn=(shape((tokens, width), F32), VMEM))
    some, every = low_vmem(tokens, width), low_vmem(rows, width)
    scratch = dict(
        w_s=low_vmem(3, width, width), dq_s=some, dk_s=every, dv_s=every, n_s=every, heads_s=some, d_att_s=some,
        p1=some, p2=some, p3=some, row_in=low_vmem(6, tokens // 2, width),
    )
    if full:
        ins.update(above=(above, ANY), small_in=(small, VMEM), e0=(swaps[0], ANY), e1=(swaps[1], ANY), from_x=(swaps[2], ANY), from_y=(swaps[3], ANY))
        twice = (low_shape(2, 2, half, width), ANY)
        outs.update(
            g_mix=(low_shape(2, 3 * width // 4, width), ANY), g_out=(low_shape(2, width // 4, width), ANY), e_up=twice, e_down=twice,
            small=(shape(small.shape, F32), VMEM),
        )
        scratch.update(
            scatter_scratch(peers, half, width), **expert_scatter_scratch(half, width), above_s=low_vmem(half, width), e_s=low_vmem(2, 2, 2, half, width),
            small_s=pltpu.VMEM((4,) + small.shape, F32), small_r=pltpu.VMEM((6,) + small.shape, F32),
            z_in=low_vmem(4, 3, half // 8, width), both=low_vmem(2, 2, half, width),
        )
    else:
        outs.update(pack=(low_shape(2 * peers, half, width), ANY), att=(shape((8, width), F32), VMEM))
        scratch.update(pack_s=low_vmem(2 * peers, half, width))
        if returns:
            ins.update(out=(out, ANY), slot_row=(slots[None, :], VMEM))
            outs.update(result=(low_shape(tokens, width), VMEM))
            size = out.shape[0] // CUTS
            scratch.update(out_s=low_vmem(size, width), back=low_vmem(3, size, width))
    return run_kernel(
        project_back_part, ins, outs, scratch, 4 + full, 4 * rows * width * width, 40, 96, full=full, returns=returns
    )


def inverse_rms(stream):
    return lax.rsqrt(jnp.mean(stream * stream, axis=-1, keepdims=True) + EPS)


def norm_backward(upstream, stream, inverse, gain):
    weighted = upstream * gain
    inner = jnp.mean(weighted * stream, axis=-1, keepdims=True)
    return inverse * weighted - stream * (inverse * inverse * inverse) * inner


def path_table(segment_ids, path_pos, parent_ids, peers):
    segment = segment_ids[::BLK].reshape(peers, -1)
    position = path_pos[::BLK].reshape(peers, -1)
    t = lax.axis_index(TENSOR)
    order = jnp.arange(peers, dtype=jnp.int32) ^ t
    match = order[:, None] == jnp.arange(peers, dtype=jnp.int32)[None, :]
    pick = lambda v: jnp.sum(jnp.where(match[:, :, None], v[None], 0), axis=1)
    segment, position = pick(segment), pick(position)
    place = jnp.where(segment == 0, position // BLK, segment + (TRUNK - 1))
    seg, pos, own = segment[0], position[0], place[0]
    names = jnp.arange(parent_ids.shape[-1], dtype=jnp.int32)
    parent = jnp.sum(jnp.where(seg[:, None] == names[None, :], parent_ids[0][None], 0), axis=1)
    leaf = (seg > 0) & (parent > 0)
    parent_place = jnp.where(leaf, parent + (TRUNK - 1), own)
    base_own = jnp.where(seg > 0, pos, BIG)
    base_parent = jnp.where(leaf, TRUNK * BLK, BIG)
    mine = jnp.stack([pos, own, parent_place, base_own, base_parent], axis=1)
    return jnp.concatenate([place.reshape(-1), mine.reshape(-1)]).astype(jnp.int32)


def dispatch_plan(route, experts, capacity):
    count = route.shape[0]
    chosen = route[:, None] == jnp.arange(experts, dtype=jnp.int32)[None, :]
    index = jnp.arange(count, dtype=jnp.int32)
    before = (index[None, :] < index[:, None]).astype(BF16)
    ranks = dot(before, chosen.astype(BF16)).astype(jnp.int32)
    rank = jnp.sum(jnp.where(chosen, ranks, 0), axis=1)
    to = route ^ lax.axis_index(EXPERT) if experts == 4 else route
    slot = to * capacity + rank
    table = slot[None, :] == jnp.arange(experts * capacity, dtype=jnp.int32)[:, None]
    return chosen, (slot, table.astype(BF16))


def send_rows(table, rows, experts, capacity):
    chunks = [
        dot(table[k * capacity : (k + 1) * capacity], rows).astype(BF16) for k in range(experts)
    ]
    return jnp.concatenate(exchange(chunks), axis=0)


def return_rows(table, results, experts, capacity):
    chunks = exchange([results[k * capacity : (k + 1) * capacity] for k in range(experts)])
    return dot_tn(table, jnp.concatenate(chunks, axis=0))


def own_half(x):
    half = x.shape[0] // 2
    return lax.dynamic_slice_in_dim(x, lax.axis_index(DP) * half, half, 0)


def gather_all(x):
    out = lax.all_gather(x, (DP, TENSOR), axis=0)
    return out.reshape((lax.axis_size(DP), lax.axis_size(TENSOR)) + x.shape)


def scatter_all(x):
    flat = x.reshape((-1,) + x.shape[2:])
    return lax.psum_scatter(flat, (DP, TENSOR), scatter_dimension=0, tiled=True)[0]


def pack_attention(w_mix, w_proj):
    width = w_mix.shape[0]
    return jnp.concatenate([w_mix.transpose(1, 2, 0).reshape(-1, width), w_proj], axis=0)


def pack_experts(w_up, w_back):
    return jnp.stack([own_half(w_up), own_half(w_back)])


def swap_cores(half):
    return lax.all_gather(half, DP, axis=0)


def body(
    hidden_in, route_ids, segment_ids, path_pos, parent_ids, norm_att, w_qkv, w_out, norm_ffn, w_route, w_in, w_down, cotangent,
):
    depth_total = w_qkv.shape[0]
    tokens, width = hidden_in.shape
    experts = w_route.shape[-1]
    capacity = 3 * tokens // (2 * experts)
    peers = lax.axis_size(TENSOR)
    shard = width // peers
    table = path_table(segment_ids, path_pos, parent_ids, peers)
    plans = [dispatch_plan(route_ids[d, :, 0], experts, capacity) for d in range(depth_total)]
    routes = jnp.pad(w_route, ((0, 0), (0, 0), (0, BLK - experts)))
    cotangent = cotangent.astype(F32)

    stream = hidden_in.astype(F32)
    kept = []
    turned = (w_qkv.transpose(0, 2, 3, 1), w_out)
    own = (w_in, w_down)
    weights = None
    for depth in range(depth_total):
        gain_att, gain_ffn = norm_att[depth].astype(F32), norm_ffn[depth].astype(F32)
        chosen, plan = plans[depth]
        last = depth + 1 == depth_total
        inverse_att = inverse_rms(stream)
        normed = (stream * inverse_att * gain_att).astype(BF16)
        proj = project(normed, turned if depth == 0 else weights, depth == 0, peers)
        w_here = None if experts == CUTS else gather_all(pack_experts(w_in[depth, 0], w_down[depth, 0]))
        heads, lse = attend(table, proj.q, proj.k, proj.v)
        after_att = stream + dot(heads, proj.w_all[3])
        inverse_ffn = inverse_rms(after_att)
        token_rows = (after_att * inverse_ffn * gain_ffn).astype(BF16)
        router = jax.nn.softmax(dot(token_rows, w_route[depth]), axis=-1)
        gate = jnp.sum(jnp.where(chosen, router, 0.0), axis=1, keepdims=True)
        if last:
            d_low = (gate * cotangent).astype(BF16)
            held = experts_both(w_here, own, plan, token_rows, d_low, routes, experts, capacity, depth)
            if experts != CUTS:
                back = return_rows(plan[1], held.out, experts, capacity).astype(BF16)
        else:
            back, held = experts_forward(plan, token_rows, experts, capacity, w_here, own, turned, depth)
            if experts == CUTS:
                weights = held.next_all.reshape((2, peers, 1) + held.next_all.shape[1:])
            else:
                weights = gather_all(own_half(pack_attention(w_qkv[depth + 1], w_out[depth + 1])))[:, :, None]
        kept.append((stream, inverse_att, proj, heads, lse, after_att, inverse_ffn, gate, held))
        if not last:
            stream = after_att + gate * back.astype(F32)

    upstream = cotangent
    grads_e, grads_a, smalls = [None] * depth_total, [None] * depth_total, [None] * depth_total
    above = None
    for depth in reversed(range(depth_total)):
        stream, inverse_att, proj, heads, lse, after_att, inverse_ffn, gate, held = kept[depth]
        gain_att, gain_ffn = norm_att[depth].astype(F32), norm_ffn[depth].astype(F32)
        chosen, plan = plans[depth]
        last = depth + 1 == depth_total
        if not last:
            d_low = (gate * upstream).astype(BF16)
            held = experts_backward(plan, d_low, held, routes, experts, capacity, above, depth)
            above = held.summed
        dx1 = upstream + norm_backward(held.result.astype(F32), after_att, inverse_ffn, gain_ffn)
        d_att = dx1.astype(BF16)
        d_heads = dot(d_att, proj.out_turned).astype(BF16)
        dq, dk, dv = attend_back(table, proj.q, proj.k, proj.v, d_heads, heads, lse)
        args = (proj.w_all, dq, dk, dv, proj.n, heads, d_att)
        if depth == 0 and experts == CUTS:
            swaps = (held.grads, held.e_summed, xperm(held.to_x, TENSOR, 1), xperm(held.to_y, TENSOR, 2))
            part = jnp.concatenate([held.small, smalls[1]], axis=0)
            got = project_back(*args, above=above, small=part, swaps=swaps)
            grads_e = (got.e_up, got.e_down)
            grad_mix, grad_out = got.g_mix.astype(F32), got.g_out.astype(F32)
            small = got.small.reshape(depth_total, -1, width)
        else:
            if last and experts == CUTS:
                got = project_back(*args, out=held.out, slots=plan[0])
                back = got.result
            else:
                got = project_back(*args)
            if last:
                hidden_out = (after_att + gate * back.astype(F32)).astype(BF16)
            if above is not None:
                grads_a[depth + 1] = swap_cores(lax.psum(above, EXPERT))
            above = got.pack.reshape((2, peers) + got.pack.shape[1:])
            if experts == CUTS:
                above = (got.pack, held.grads)
            else:
                grads_e[depth] = scatter_all(after(held.grads, got.dn))
            line = lax.broadcasted_iota(jnp.int32, held.small.shape, 0)
            smalls[depth] = jnp.where(line == held.small.shape[0] - 1, got.att[:1], held.small)
            if depth == 0:
                grads_a[0] = swap_cores(lax.psum(scatter_all(above), EXPERT))
                small = sum_small(jnp.stack(smalls))
                grads_e = jnp.stack([swap_cores(g) for g in grads_e]).transpose(2, 0, 1, 3, 4)
                grads_a = jnp.stack(grads_a).reshape(depth_total, width, width).astype(F32)
                grad_mix, grad_out = grads_a[:, : 3 * shard], grads_a[:, 3 * shard :]
        upstream = dx1 + norm_backward(got.dn, stream, inverse_att, gain_att)
    grad_up, grad_down = [g.reshape(depth_total, 1, width, width).astype(F32) for g in grads_e]
    grad_mix = grad_mix.reshape(depth_total, 3, shard, width).transpose(0, 3, 1, 2)
    grad_route = small[:, :experts].transpose(0, 2, 1)
    grad_ffn = small[:, experts] / norm_ffn.astype(F32)
    grad_att = small[:, -1] / norm_att.astype(F32)
    return (hidden_out, upstream, grad_att, grad_mix, grad_out, grad_ffn, grad_route, grad_up, grad_down)


def solution(mesh):
    in_specs = (
        P((DP, EXPERT, TENSOR), None),
        P(None, (DP, EXPERT, TENSOR), None),
        P((DP, EXPERT)),
        P((DP, EXPERT)),
        P((DP, EXPERT), None),
        P(),
        P(None, None, None, TENSOR),
        P(None, TENSOR, None),
        P(),
        P(),
        P(None, EXPERT, None, TENSOR),
        P(None, EXPERT, TENSOR, None),
        P((DP, EXPERT, TENSOR), None),
    )
    out_specs = (
        P((DP, EXPERT, TENSOR), None),
        P((DP, EXPERT, TENSOR), None),
        P(),
        P(None, None, None, TENSOR),
        P(None, TENSOR, None),
        P(),
        P(),
        P(None, EXPERT, None, TENSOR),
        P(None, EXPERT, TENSOR, None),
    )
    return jax.shard_map(body, mesh=mesh, in_specs=in_specs, out_specs=out_specs, check_vma=False)
```

```python
from types import SimpleNamespace

import jax
import jax.numpy as jnp
from jax import lax
from jax.experimental import pallas as pl
from jax.experimental.pallas import tpu as pltpu
from jax.sharding import PartitionSpec as P

HEAD_DIM = 64
BLK = 128
TRUNK = 8
PAIR = 2 * HEAD_DIM
EPS = 1e-06
NEG = -1000000000.0
BIG = 1 << 20
F32 = jnp.float32
BF16 = jnp.bfloat16
VMEM_LIMIT = 58 * 1024 * 1024
DP, EXPERT, TENSOR = "dp", "expert", "tensor"

NT = (((1,), (1,)), ((), ()))
TN = (((0,), (0,)), ((), ()))


def dot(a, b):
    return jnp.dot(a, b, preferred_element_type=F32)


def dot_nt(a, b):
    return lax.dot_general(a, b, NT, preferred_element_type=F32)


def dot_tn(a, b):
    return lax.dot_general(a, b, TN, preferred_element_type=F32)


def cost(macs, moved, trans=0):
    return pl.CostEstimate(flops=macs // 64, bytes_accessed=moved // 64, transcendentals=0)


def xperm(x, axis, k):
    n = lax.axis_size(axis)
    return lax.ppermute(x, axis, [(i, i ^ k) for i in range(n)])


def after(x, dep):
    return lax.optimization_barrier((x, dep))[0]


def sum_small(x):
    for axis in (DP, TENSOR, EXPERT):
        n = lax.axis_size(axis)
        k = 1
        while k < n:
            x = x + xperm(x, axis, k)
            k *= 2
    return x


def exchange(chunks):
    n = len(chunks)
    if n == 4:
        return [chunks[0]] + [xperm(chunks[k], EXPERT, k) for k in range(1, n)]
    out = lax.all_to_all(jnp.stack(chunks), EXPERT, split_axis=0, concat_axis=0, tiled=True)
    return [out[k] for k in range(n)]


def masked_pair(x):
    lane = lax.broadcasted_iota(jnp.int32, x.shape, 1)
    zero = jnp.zeros_like(x)
    return jnp.concatenate([jnp.where(lane < HEAD_DIM, x, zero), jnp.where(lane < HEAD_DIM, zero, x)], axis=0)


def path_spans(table, at, trunk):
    own, parent, base_own, base_parent = [table[at + j] for j in range(1, 5)]
    block = lambda place: pl.ds(pl.multiple_of(place * BLK, BLK), BLK)
    return [(pl.ds(0, trunk), 0), (block(parent), base_parent), (block(own), base_own)]


def attend_kernel(table, q_ref, k_ref, v_ref, out_ref, lse_ref, keys, values_t):
    blocks = k_ref.shape[0] // BLK
    mine = q_ref.shape[0] // BLK
    trunk = TRUNK * BLK
    for b in range(blocks):
        place = pl.ds(pl.multiple_of(table[b] * BLK, BLK), BLK)
        rows = pl.ds(b * BLK, BLK)
        keys[place, :] = k_ref[rows, :]
        values_t[pl.ds(0, PAIR), place] = v_ref[rows, :].T
    values_t[pl.ds(PAIR, 16), :] = jnp.ones((16, blocks * BLK), BF16)
    lane = lax.broadcasted_iota(jnp.int32, (BLK, PAIR), 1)

    def scores_of(i):
        at = blocks + 5 * i
        q = masked_pair(q_ref[pl.ds(i * BLK, BLK), :] * jnp.asarray(HEAD_DIM ** -0.5, BF16))
        pos_q = table[at] + lax.broadcasted_iota(jnp.int32, (1, 2 * BLK), 1) % BLK
        parts = []
        for here, base in path_spans(table, at, trunk):
            scores = dot_nt(keys[here, :], q)
            key_pos = base + lax.broadcasted_iota(jnp.int32, (here.size, 1), 0)
            parts.append(jnp.where(key_pos <= pos_q, scores, NEG))
        top = parts[0].max(axis=0, keepdims=True)
        for part in parts[1:]:
            top = jnp.maximum(top, part.max(axis=0, keepdims=True))
        return parts, top

    coming = scores_of(0)
    for i in range(mine):
        parts, top = coming
        if i + 1 < mine:
            coming = scores_of(i + 1)
        rows = pl.ds(i * BLK, BLK)
        both = jnp.zeros((PAIR + 16, 2 * BLK), F32)
        for (here, _), part in zip(path_spans(table, blocks + 5 * i, trunk), parts):
            both = both + dot(values_t[:, here], jnp.exp(part - top).astype(BF16))
        total = both[PAIR : PAIR + 1]
        heads = (both[:PAIR] / total).T
        lse = top + jnp.log(total)
        out_ref[rows, :] = jnp.where(lane < HEAD_DIM, heads[:BLK], heads[BLK:]).astype(BF16)
        lse_ref[0, pl.ds(0, 1), rows] = lse[:, :BLK]
        lse_ref[0, pl.ds(1, 1), rows] = lse[:, BLK:]


def attend(table, q, k, v):
    mine, width = q.shape
    rows = k.shape[0]
    pairs = width // PAIR
    column = lambda n: pl.BlockSpec((n, PAIR), lambda p, table: (0, p))
    return pl.pallas_call(
        attend_kernel,
        grid_spec=pltpu.PrefetchScalarGridSpec(
            num_scalar_prefetch=1,
            grid=(pairs,),
            in_specs=[column(mine), column(rows), column(rows)],
            out_specs=[column(mine), pl.BlockSpec((1, 8, mine), lambda p, table: (p, 0, 0))],
            scratch_shapes=[pltpu.VMEM((rows, PAIR), BF16), pltpu.VMEM((PAIR + 16, rows), BF16)],
        ),
        out_shape=[jax.ShapeDtypeStruct((mine, width), BF16), jax.ShapeDtypeStruct((pairs, 8, mine), F32)],
        compiler_params=pltpu.CompilerParams(vmem_limit_bytes=VMEM_LIMIT),
        cost_estimate=cost(mine * 1280 * width * 8, 4 * rows * width, mine * 1280 * width // HEAD_DIM),
        name="attend",
    )(table, q, k, v)


def attend_back_kernel(
    table, q_ref, k_ref, v_ref, do_ref, o_ref, lse_ref, dq_ref, dk_ref, dv_ref, keys, values, keys_t, dk_acc, dv_acc,
):
    blocks = k_ref.shape[0] // BLK
    mine = q_ref.shape[0] // BLK
    trunk = TRUNK * BLK
    for b in range(blocks):
        place = pl.ds(pl.multiple_of(table[b] * BLK, BLK), BLK)
        rows = pl.ds(b * BLK, BLK)
        keys[place, :] = k_ref[rows, :]
        values[place, :] = v_ref[rows, :]
        keys_t[:, place] = k_ref[rows, :].T
    dk_acc[...] = jnp.zeros_like(dk_acc)
    dv_acc[...] = jnp.zeros_like(dv_acc)
    lane = lax.broadcasted_iota(jnp.int32, (BLK, PAIR), 1)

    def weights_of(i):
        at = blocks + 5 * i
        rows = pl.ds(i * BLK, BLK)
        q = masked_pair(q_ref[rows, :] * jnp.asarray(HEAD_DIM ** -0.5, BF16))
        do = do_ref[rows, :]
        product = (do.astype(F32) * o_ref[rows, :].astype(F32)).T
        inner = jnp.concatenate(
            [jnp.sum(product[:HEAD_DIM], axis=0, keepdims=True), jnp.sum(product[HEAD_DIM:], axis=0, keepdims=True)], axis=1
        )
        do = masked_pair(do)
        lse = jnp.concatenate([lse_ref[0, pl.ds(0, 1), rows], lse_ref[0, pl.ds(1, 1), rows]], axis=1)
        pos_q = table[at] + lax.broadcasted_iota(jnp.int32, (1, 2 * BLK), 1) % BLK
        parts = []
        for here, base in path_spans(table, at, trunk):
            scores = dot_nt(keys[here, :], q)
            key_pos = base + lax.broadcasted_iota(jnp.int32, (here.size, 1), 0)
            weights = jnp.exp(jnp.where(key_pos <= pos_q, scores - lse, NEG))
            d_weights = dot_nt(values[here, :], do)
            parts.append((weights.astype(BF16), (weights * (d_weights - inner)).astype(BF16)))
        return q, do, parts

    coming = weights_of(0)
    for i in range(mine):
        q, do, parts = coming
        if i + 1 < mine:
            coming = weights_of(i + 1)
        dq_t = jnp.zeros((PAIR, 2 * BLK), F32)
        for (here, _), (weights, d_scores) in zip(path_spans(table, blocks + 5 * i, trunk), parts):
            dv_acc[here, :] += dot(weights, do)
            dk_acc[here, :] += dot(d_scores, q)
            dq_t = dq_t + dot(keys_t[:, here], d_scores)
        dq = dq_t.T * (HEAD_DIM ** -0.5)
        dq_ref[pl.ds(i * BLK, BLK), :] = jnp.where(lane < HEAD_DIM, dq[:BLK], dq[BLK:]).astype(BF16)
    for b in range(blocks):
        place = pl.ds(pl.multiple_of(table[b] * BLK, BLK), BLK)
        rows = pl.ds(b * BLK, BLK)
        dk_ref[rows, :] = dk_acc[place, :].astype(BF16)
        dv_ref[rows, :] = dv_acc[place, :].astype(BF16)


def attend_back(table, q, k, v, d_heads, heads, lse):
    mine, width = q.shape
    rows = k.shape[0]
    pairs = width // PAIR
    column = lambda n: pl.BlockSpec((n, PAIR), lambda p, table: (0, p))
    return pl.pallas_call(
        attend_back_kernel,
        grid_spec=pltpu.PrefetchScalarGridSpec(
            num_scalar_prefetch=1,
            grid=(pairs,),
            in_specs=[
                column(mine), column(rows), column(rows), column(mine), column(mine),
                pl.BlockSpec((1, 8, mine), lambda p, table: (p, 0, 0)),
            ],
            out_specs=[column(mine), column(rows), column(rows)],
            scratch_shapes=[
                pltpu.VMEM((rows, PAIR), BF16),
                pltpu.VMEM((rows, PAIR), BF16),
                pltpu.VMEM((PAIR, rows), BF16),
                pltpu.VMEM((rows, PAIR), F32),
                pltpu.VMEM((rows, PAIR), F32),
            ],
        ),
        out_shape=[
            jax.ShapeDtypeStruct((mine, width), BF16),
            jax.ShapeDtypeStruct((rows, width), BF16),
            jax.ShapeDtypeStruct((rows, width), BF16),
        ],
        compiler_params=pltpu.CompilerParams(vmem_limit_bytes=VMEM_LIMIT),
        cost_estimate=cost(mine * 1280 * width * 20, 8 * rows * width, mine * 1280 * width // HEAD_DIM),
        name="attend_back",
    )(table, q, k, v, d_heads, heads, lse)


GELU_C = 0.7978845608028654
GELU_A = 0.044715
CUTS = 4
MESH = pl.DeviceIdType.MESH
ANY = pl.BlockSpec(memory_space=pl.ANY)
VMEM = pl.BlockSpec(memory_space=pltpu.VMEM)


def low_shape(*dims):
    return jax.ShapeDtypeStruct(dims, BF16)


def low_vmem(*dims):
    return pltpu.VMEM(dims, BF16)


def run_kernel(body, ins, outs, scratch, identity, macs, near, far, **flags):
    scratch = dict(scratch, near=pltpu.SemaphoreType.DMA((near,)))
    params = dict(vmem_limit_bytes=VMEM_LIMIT)
    if far:
        scratch.update(send=pltpu.SemaphoreType.DMA((far,)), recv=pltpu.SemaphoreType.DMA((far,)))
        params.update(collective_id=identity, has_side_effects=True)
    names = [*ins, *outs, *scratch]

    def kernel(*refs):
        body(Moves(SimpleNamespace(**dict(zip(names, refs)))), **flags)

    results = pl.pallas_call(
        kernel,
        in_specs=[spec for _, spec in ins.values()],
        out_specs=[spec for _, spec in outs.values()],
        out_shape=[shape for shape, _ in outs.values()],
        scratch_shapes=list(scratch.values()),
        compiler_params=pltpu.CompilerParams(**params),
        cost_estimate=cost(macs, 0),
        name=body.__name__,
    )(*[value for value, _ in ins.values()])
    return SimpleNamespace(**dict(zip(outs, results)))


def xor_peer(index, k):
    if k == 1:
        return index + 1 - 2 * lax.rem(index, 2)
    if k == 2:
        return index + 2 - 4 * lax.rem(lax.div(index, 2), 2)
    return index + 3 - 2 * lax.rem(index, 4)


class Moves:
    def __init__(self, refs):
        self.refs, self.near, self.far, self.seen, self.left, self.sent = refs, 0, 0, set(), set(), []
        self.c, self.t, self.z = [lax.axis_index(axis) for axis in (DP, TENSOR, EXPERT)]
        self.x_peer, self.y_peer = [{TENSOR: xor_peer(self.t, k)} for k in (1, 2)]
        self.sibling = {DP: 1 - self.c}
        self.z_peers = [{EXPERT: xor_peer(self.z, k)} for k in (1, 2, 3)]

    def local(self, src, dst):
        assert self.near < self.refs.near.shape[0]
        copy = pltpu.make_async_copy(src, dst, self.refs.near.at[self.near])
        self.near += 1
        copy.start()
        return copy

    def remote(self, src, dst, device):
        assert self.far < self.refs.send.shape[0]
        copy = pltpu.make_async_remote_copy(
            src_ref=src, dst_ref=dst, send_sem=self.refs.send.at[self.far], recv_sem=self.refs.recv.at[self.far],
            device_id=device, device_id_type=MESH,
        )
        self.far += 1
        copy.start()
        self.sent.append(copy)
        return copy

    def need(self, *copies):
        for copy in copies:
            if id(copy) not in self.seen:
                self.seen.add(id(copy))
                copy.wait()

    def arrived(self, *copies):
        for copy in copies:
            if id(copy) not in self.seen:
                self.seen.add(id(copy))
                copy.wait_recv()

    def finish(self):
        self.gone(*self.sent)

    def gone(self, *copies):
        for copy in copies:
            if id(copy) not in self.left:
                self.left.add(id(copy))
                copy.wait_send()

    def greet(self, devices):
        barrier = pltpu.get_barrier_semaphore()
        for device in devices:
            pl.semaphore_signal(barrier, inc=1, device_id=device, device_id_type=MESH)
        return lambda: pl.semaphore_wait(barrier, len(devices))


def add_low(ref, *more):
    total = ref[...].astype(F32)
    for other in more:
        total = total + other[...].astype(F32)
    return total


class Scatter:
    def __init__(self, moves, pack, core_in, g_in, piece):
        self.moves, self.pack, self.core_in, self.g_in, self.piece = moves, pack, core_in, g_in, piece
        self.peers = lax.axis_size(TENSOR)
        self.size = pack.shape[1] // 2
        c, t = moves.c, moves.t
        self.index = [t] + [xor_peer(t, k) for k in (1, 2, 3)]
        self.slots = self.index if core_in is None else [c * self.peers + i for i in self.index]
        self.flow = [dict(), dict()]

    def rows(self, h):
        return pl.ds(h * self.size, self.size)

    def sides(self, h):
        half = self.size // 2
        return pl.ds(h * self.size, half), pl.ds(h * self.size + half, half)

    def swap(self, h):
        m = self.moves
        there = pl.ds((1 - m.c) * self.peers, self.peers)
        self.flow[h][0] = m.remote(self.pack.at[there, self.rows(h)], self.core_in.at[:, self.rows(h)], m.sibling)

    def out(self, h):
        m, pack, slots, f = self.moves, self.pack, self.slots, self.flow[h]
        left, right = self.sides(h)
        if self.core_in is not None:
            m.arrived(f[0])
            for j in (3, 1, 2, 0):
                pack[slots[j], self.rows(h), :] = add_low(
                    pack.at[slots[j], self.rows(h)], self.core_in.at[self.index[j], self.rows(h)]
                ).astype(BF16)
        f[1] = m.remote(pack.at[slots[3], left], self.g_in.at[h, 0], m.x_peer)
        f[2] = m.remote(pack.at[slots[3], right], self.g_in.at[h, 1], m.y_peer)
        f[3] = m.remote(pack.at[slots[1], left], self.g_in.at[h, 2], m.x_peer)
        f[4] = m.remote(pack.at[slots[2], right], self.g_in.at[h, 3], m.y_peer)

    def turn(self, h):
        m, pack, slots, f = self.moves, self.pack, self.slots, self.flow[h]
        left, right = self.sides(h)
        m.arrived(f[1])
        pack[slots[2], left, :] = add_low(pack.at[slots[2], left], self.g_in.at[h, 0]).astype(BF16)
        f[5] = m.remote(pack.at[slots[2], left], self.g_in.at[h, 4], m.y_peer)
        m.arrived(f[2])
        pack[slots[1], right, :] = add_low(pack.at[slots[1], right], self.g_in.at[h, 1]).astype(BF16)
        f[6] = m.remote(pack.at[slots[1], right], self.g_in.at[h, 5], m.x_peer)

    def end(self, h):
        f = self.flow[h]
        self.moves.arrived(f[3], f[4], f[5], f[6])
        for cut, a, b in zip(self.sides(h), (2, 3), (4, 5)):
            total = add_low(self.pack.at[self.slots[0], cut], self.g_in.at[h, a], self.g_in.at[h, b])
            self.piece[cut, :] = total.astype(BF16)


class ExpertScatter:
    def __init__(self, moves, pack, own, keep, inbox):
        self.m, self.pack, self.own, self.keep, self.inbox = moves, pack, own, keep, inbox
        half = own.shape[1] // 2
        self.left, self.right = pl.ds(0, half), pl.ds(half, half)
        self.index = [moves.t] + [xor_peer(moves.t, k) for k in (1, 2, 3)]

    def load(self):
        p, i, m = self.pack, self.index, self.m
        return [
            m.local(p.at[i[0]], self.own),
            m.local(p.at[i[2], :, self.left], self.keep.at[0]),
            m.local(p.at[i[1], :, self.right], self.keep.at[1]),
        ]

    def out(self):
        p, i, m = self.pack, self.index, self.m
        self.flow = [
            m.remote(p.at[i[3], :, self.left], self.inbox.at[0], m.x_peer),
            m.remote(p.at[i[3], :, self.right], self.inbox.at[1], m.y_peer),
            m.remote(p.at[i[1], :, self.left], self.inbox.at[2], m.x_peer),
            m.remote(p.at[i[2], :, self.right], self.inbox.at[3], m.y_peer),
        ]

    def turn(self):
        m = self.m
        self.second = []
        for n, device in enumerate((m.y_peer, m.x_peer)):
            if self.flow:
                m.arrived(self.flow[n])
            self.keep[n] = add_low(self.keep.at[n], self.inbox.at[n]).astype(BF16)
            self.second.append(m.remote(self.keep.at[n], self.inbox.at[4 + n], device))

    def end(self):
        self.m.arrived(*self.flow, *self.second)
        for n, cut in enumerate((self.left, self.right)):
            self.own[:, cut, :] = add_low(self.own.at[:, cut], self.inbox.at[2 + n], self.inbox.at[4 + n]).astype(BF16)


def expert_scatter_scratch(half, width):
    return dict(e_own=low_vmem(2, half, width), e_keep=low_vmem(2, 2, half // 2, width), e_in=low_vmem(6, 2, half // 2, width))


class Gather:
    def __init__(self, moves, pack):
        self.moves, self.pack = moves, pack
        self.half = pack.shape[1] // 2
        self.slots = [moves.c * (pack.shape[0] // 2) + i for i in [moves.t] + [xor_peer(moves.t, k) for k in (1, 2, 3)]]

    def out(self):
        own = self.pack.at[self.slots[0]]
        self.first = [self.moves.remote(own, own, device) for device in (self.moves.x_peer, self.moves.y_peer)]

    def turn(self):
        m = self.moves
        self.swaps, self.second = [], []
        for k, device in ((1, m.y_peer), (2, m.x_peer)):
            m.arrived(self.first[k - 1])
            piece = self.pack.at[self.slots[k], pl.ds((k - 1) * self.half, self.half)]
            self.second.append(m.remote(piece, piece, device))
            self.swap(k)

    def swap(self, k):
        whole = self.pack.at[self.slots[k]]
        self.swaps.append(self.moves.remote(whole, whole, self.moves.sibling))

    def end(self):
        self.moves.arrived(*self.second)
        self.swap(3)
        self.moves.arrived(*self.swaps)


def attention_rows(r, depth, i):
    return r.w_qkv.at[depth, i] if i < 3 else r.w_out.at[depth]


def scatter_scratch(peers, half, width):
    return dict(
        pack_s=low_vmem(2 * peers, half, width), core_in=low_vmem(peers, half, width),
        g_in=low_vmem(2, 6, half // 4, width), piece=low_vmem(half, width),
    )


def one_hot(slot_row, k, size):
    index = lax.broadcasted_iota(jnp.int32, (size, slot_row.shape[1]), 0) + k * size
    return jnp.where(index == slot_row[...], 1.0, 0.0).astype(BF16)


def combine(m, slot_row, source, copies, back, size):
    total = dot_tn(one_hot(slot_row, 0, size), source[pl.ds(0, size), :])
    for k in (1, 2, 3):
        m.arrived(copies[k])
        total = total + dot_tn(one_hot(slot_row, k, size), back[k - 1])
    return total.astype(BF16)


def expert_part(m, forward, backward, remote, hosted, reduces, fetches, experts, depth):
    r = m.refs
    if hosted:
        own_up, own_down = r.w_in.at[depth, 0], r.w_down.at[depth, 0]
    up, down, hidden, slope, rows, outs = r.up, r.down, r.hidden_s, r.slope_s, r.rows_s, r.outs_s
    count, width = rows.shape
    inner = up.shape[1]
    half = width // 2
    peers = inner // width
    size = count // CUTS
    tile = 256
    cuts = [pl.ds(k * size, size) for k in range(CUTS)]
    met = []
    if remote:
        met += m.z_peers
    if hosted or reduces:
        met += [m.x_peer, m.y_peer]
    if remote:
        met += [m.sibling]
    ready = m.greet(met) if met else None

    def up_at(c, t, start=0, rows=half):
        return up.at[pl.ds(pl.multiple_of(c * half + start, half // 2), rows), pl.ds(pl.multiple_of(t * width, width), width)]

    def down_at(c, t, start=0, rows=half):
        return down.at[pl.ds(pl.multiple_of(t * width + c * half + start, half // 2), rows)]

    loads, weight_loads = [], []
    if not remote:
        if forward:
            loads.append(m.local(r.x, rows))
        if backward:
            loads.append(m.local(r.g, r.d_s))
    if hosted:
        weight_loads.append(m.local(own_up, up.at[:, pl.ds(pl.multiple_of(m.t * width, width), width)]))
        weight_loads.append(m.local(own_down, down.at[pl.ds(pl.multiple_of(m.t * width, width), width)]))
    else:
        for t in range(peers):
            for c in range(2):
                weight_loads += [m.local(r.w.at[c, t, 0], up_at(c, t)), m.local(r.w.at[c, t, 1], down_at(c, t))]
    if backward and not forward:
        loads += [m.local(a, b) for a, b in ((r.rows, rows), (r.out, outs), (r.slope, slope), (r.hidden, hidden))]
    if ready:
        ready()

    def dispatch(source, target, stage):
        copies = {}
        x = source[...]
        for k in (2, 1, 3):
            stage[k - 1] = dot(one_hot(r.slot_row, k, size), x).astype(BF16)
            copies[k] = m.remote(stage.at[k - 1], target.at[cuts[k]], m.z_peers[k - 1])
        target[cuts[0], :] = dot(one_hot(r.slot_row, 0, size), x).astype(BF16)
        return copies

    def give_back(source, k):
        return m.remote(source.at[cuts[k]], r.back.at[k - 1], m.z_peers[k - 1])

    def forward_block(cut, at):
        u = dot(rows[cut, :], up[:, at])
        square = u * u
        gate = 0.5 + 0.5 * jnp.tanh(u * (GELU_C + (GELU_C * GELU_A) * square))
        value = u * gate
        hidden[cut, at] = value.astype(BF16)
        grow = gate + value * (1.0 - gate) * (2 * GELU_C + (6 * GELU_C * GELU_A) * square)
        slope[cut, at] = grow.astype(BF16)

    def forward_peer(cut, t):
        for col in range(0, width, tile):
            forward_block(cut, pl.ds(pl.multiple_of(t * width + col, tile), tile))

    def forward_down(cut):
        outs[cut, :] = dot(hidden[cut, :], down[...]).astype(BF16)

    def backward_chunk(cut):
        d = r.d_s[cut, :]
        for col in range(0, inner, tile):
            at = pl.ds(col, tile)
            d_hidden = dot_nt(d, down[at, :])
            slope[cut, at] = (d_hidden * slope[cut, at].astype(F32)).astype(BF16)
        x = rows[cut, :]
        logits = dot(x, r.route[depth])
        lane = lax.broadcasted_iota(jnp.int32, logits.shape, 1)
        logits = jnp.where(lane < experts, logits, NEG)
        router = jnp.exp(logits - jnp.max(logits, axis=1, keepdims=True))
        router = router / jnp.sum(router, axis=1, keepdims=True)
        amount = jnp.sum(outs[cut, :].astype(F32) * d.astype(F32), axis=1, keepdims=True)
        d_log = (amount * (jnp.where(lane == m.z, 1.0, 0.0) - router)).astype(BF16)
        r.log_s[cut, :] = d_log
        d_rows = dot_nt(slope[cut, :], up[...]) + dot_nt(d_log, r.route[depth])
        r.back_s[cut, :] = d_rows.astype(BF16)
        return jnp.sum(d_rows * x.astype(F32), axis=0, keepdims=True)

    sent_x = sent_d = None
    saves, returns = [], {}
    scatter = None
    if fetches:
        shard = half // 2
        next_loads = [
            m.local(attention_rows(r, depth + 1, i), r.next_s.at[i // 2 * peers + m.t, pl.ds(i % 2 * shard, shard)]) for i in range(4)
        ]
        fetch = Gather(m, r.next_s)
    if hosted:
        first = {}
        mine = pl.ds(pl.multiple_of(m.c * half, half), half)
        for at, own in ((up_at, own_up), (down_at, own_down)):
            for k, device in ((1, m.x_peer), (2, m.y_peer)):
                first[at, k] = m.remote(own.at[mine], at(m.c, m.t), device)
    if reduces:
        scatter = Scatter(m, r.pack_s, r.core_in, r.g_in, r.piece)
        pack_load = m.local(r.pack, r.pack_s)
        e_scatter = ExpertScatter(m, r.e_pack, r.e_own, r.e_keep, r.e_in)
        e_scatter.out()
        e_loads = e_scatter.load()
    if remote and forward:
        sent_x = dispatch(r.x, rows, r.stage_x)
    if remote and backward:
        sent_d = dispatch(r.g, r.d_s, r.stage_d)
    if reduces:
        m.need(pack_load)
        scatter.swap(0)
        scatter.swap(1)
    m.need(*loads, *weight_loads)
    if hosted:
        tens = [m.t] + [xor_peer(m.t, k) for k in (1, 2, 3)]
        onward, swaps = {up_at: [], down_at: []}, {}

        def pass_on(at):
            for k, device in ((1, m.y_peer), (2, m.x_peer)):
                m.arrived(first[at, k])
                piece = at(m.c, tens[k], (k - 1) * (half // 2), half // 2)
                onward[at].append(m.remote(piece, piece, device))
                swap(at, k)

        def swap(at, k):
            swaps[at, k] = m.remote(at(m.c, tens[k]), at(m.c, tens[k]), m.sibling)

        forward_peer(cuts[0], tens[0])
        m.arrived(sent_x[1])
        forward_peer(cuts[1], tens[0])
        pass_on(up_at)
        pass_on(down_at)
        m.arrived(sent_x[2], sent_x[3])
        forward_peer(pl.ds(2 * size, 2 * size), tens[0])
        for k in (1, 2, 3):
            if k == 3:
                m.arrived(*onward[up_at])
                swap(up_at, 3)
            m.arrived(swaps[up_at, k])
            if k < 3:
                forward_peer(pl.ds(0, count), tens[k])
        m.arrived(*onward[down_at])
        swap(down_at, 3)
        if fetches:
            m.need(*next_loads)
            fetch.out()
        for first_k in (2, 0):
            pair = pl.ds(first_k * size, 2 * size)
            forward_peer(pair, tens[3])
            m.arrived(*[swaps[down_at, k] for k in (1, 2, 3)])
            forward_down(pair)
            for k in (first_k, first_k + 1):
                if k and not backward:
                    returns[k] = give_back(outs, k)
        if not backward:
            for c in range(2):
                for t in range(peers):
                    saves += [m.local(up_at(c, t), r.w.at[c, t, 0]), m.local(down_at(c, t), r.w.at[c, t, 1])]
        if fetches:
            fetch.turn()
            fetch.end()
            saves.append(m.local(r.next_s, r.next_all))
    elif forward:
        for k in range(CUTS):
            if remote and k:
                m.arrived(sent_x[k])
            for t in range(peers):
                forward_peer(cuts[k], t)
            forward_down(cuts[k])
            if remote and k and not backward:
                returns[k] = give_back(outs, k)
    if forward:
        if not backward:
            saves += [m.local(hidden, r.hidden), m.local(slope, r.slope), m.local(rows, r.rows)]
        saves.append(m.local(outs, r.out))
    if backward:
        gain = jnp.zeros((1, width), F32)
        for k in range(CUTS):
            if remote and k:
                m.arrived(sent_d[k])
            gain = gain + backward_chunk(cuts[k])
            if remote and k:
                returns[k] = give_back(r.back_s, k)
            if reduces and k == 0:
                scatter.out(0)
                scatter.out(1)
            if reduces and k == 2:
                scatter.turn(0)
                scatter.turn(1)
        if not remote:
            saves.append(m.local(r.back_s, r.result))
        if reduces:
            m.need(*e_loads)
            e_scatter.turn()
        r.turned[...] = rows[...].T
        route = dot_tn(r.log_s[...], rows[...])
        pad = r.small.shape[0] - experts - 1
        r.small[...] = jnp.concatenate([route[:experts], gain, jnp.zeros((pad, width), F32)], axis=0)
        swapped = []
        if hosted:
            m.gone(*onward[up_at], *onward[down_at], *swaps.values())
        for t in range(peers):
            at = pl.ds(t * width, width)
            up[:, at] = dot(r.turned[...], slope[:, at]).astype(BF16)
            down[at, :] = dot_tn(hidden[:, at], r.d_s[...]).astype(BF16)
            if remote:
                swapped.append([m.remote(at(1 - m.c, t), r.grads_in.at[t, i], m.sibling) for i, at in enumerate((up_at, down_at))])
            else:
                for c in range(2):
                    saves += [m.local(up_at(c, t), r.grads.at[c, t, 0]), m.local(down_at(c, t), r.grads.at[c, t, 1])]
    if reduces:
        for h in range(2):
            scatter.end(h)
        e_scatter.end()
        saves += [m.local(r.piece, r.summed), m.local(r.e_own, r.e_summed)]
    if remote:
        if backward:
            for t in range(peers):
                for i, at in enumerate((up_at, down_at)):
                    m.arrived(swapped[t][i])
                    here = at(m.c, t)
                    here[...] = add_low(here, r.grads_in.at[t, i]).astype(BF16)
                    saves.append(m.local(here, r.grads.at[t, i]))
            if reduces:
                for i, at in enumerate((up_at, down_at)):
                    for box, k, start in ((r.to_x.at[0], 3, 0), (r.to_x.at[1], 1, 0), (r.to_y.at[0], 3, 1), (r.to_y.at[1], 2, 1)):
                        saves.append(m.local(at(m.c, xor_peer(m.t, k), start * (half // 2), half // 2), box.at[i]))
        r.result[...] = combine(m, r.slot_row, r.back_s if backward else outs, returns, r.back, size)
    m.finish()
    m.need(*saves)


def expert_call(plan, experts, count, w=None, own=None, x=None, g=None, kept=None, route=None, pack=None, fetch=None, depth=0):
    slots = plan[0]
    forward, backward, remote, hosted, reduces = x is not None, g is not None, experts == CUTS, own is not None, pack is not None
    tokens, width = (x if forward else g).shape
    peers = lax.axis_size(TENSOR)
    half, inner = width // 2, peers * width
    w_shape = low_shape(2, peers, 2, half, width)
    data = VMEM if remote else ANY
    rows_shape, inner_shape = low_shape(count, width), low_shape(count, inner)
    ins, outs = {}, {}
    if hosted:
        ins.update(w_in=(own[0], ANY), w_down=(own[1], ANY))
        if not backward:
            outs.update(w=(w_shape, ANY))
    else:
        ins.update(w=(w, ANY))
    if remote:
        ins.update(slot_row=(slots[None, :], VMEM))
    if forward:
        ins.update(x=(x, data))
    if backward:
        ins.update(g=(g, data), route=(route, VMEM))
        if not forward:
            ins.update(rows=(kept.rows, ANY), out=(kept.out, ANY), hidden=(kept.hidden, ANY), slope=(kept.slope, ANY))
    if remote or backward:
        outs.update(result=(low_shape(tokens if remote else count, width), data))
    if forward:
        outs.update(out=(rows_shape, ANY))
        if not backward:
            outs.update(rows=(rows_shape, ANY), hidden=(inner_shape, ANY), slope=(inner_shape, ANY))
    if backward:
        outs.update(grads=(low_shape(peers, 2, half, width) if remote else w_shape, ANY))
        outs.update(small=(jax.ShapeDtypeStruct((-(-(experts + 2) // 8) * 8, width), F32), VMEM))
    scratch = dict(
        up=low_vmem(width, inner), down=low_vmem(inner, width), hidden_s=low_vmem(count, inner), slope_s=low_vmem(count, inner),
        rows_s=low_vmem(count, width), outs_s=low_vmem(count, width),
    )
    if backward:
        scratch.update(
            d_s=low_vmem(count, width), back_s=low_vmem(count, width), log_s=low_vmem(count, BLK), turned=low_vmem(width, count)
        )
    if backward and remote:
        scratch.update(grads_in=low_vmem(peers, 2, half, width))
    if fetch is not None:
        ins.update(w_qkv=(fetch[0], ANY), w_out=(fetch[1], ANY))
        outs.update(next_all=(low_shape(2 * peers, half, width), ANY))
        scratch.update(next_s=low_vmem(2 * peers, half, width))
    if reduces:
        ins.update(pack=(pack[0], ANY), e_pack=(pack[1], ANY))
        box = (low_shape(2, 2, half // 2, width), ANY)
        outs.update(summed=(low_shape(half, width), ANY), e_summed=(low_shape(2, half, width), ANY), to_x=box, to_y=box)
        scratch.update(scatter_scratch(peers, half, width), **expert_scatter_scratch(half, width))
    if remote:
        part = low_vmem(3, count // CUTS, width)
        scratch.update(back=part)
        if forward:
            scratch.update(stage_x=part)
        if backward:
            scratch.update(stage_d=part)
    return run_kernel(
        expert_part, ins, outs, scratch, forward + 2 * backward, count * width * inner, 64, 48 if remote else 0,
        forward=forward, backward=backward, remote=remote, hosted=hosted, reduces=reduces,
        fetches=fetch is not None, experts=experts, depth=depth,
    )


def experts_forward(plan, token_rows, experts, capacity, w, own, fetch, depth):
    count = experts * capacity
    if experts == CUTS:
        got = expert_call(plan, experts, count, own=own, x=token_rows, fetch=fetch, depth=depth)
        return got.result, got
    got = expert_call(plan, experts, count, w=w, x=send_rows(plan[1], token_rows, experts, capacity))
    got.w = w
    return return_rows(plan[1], got.out, experts, capacity).astype(BF16), got


def experts_backward(plan, d_low, kept, route, experts, capacity, pack, depth):
    count = experts * capacity
    if experts == CUTS:
        return expert_call(plan, experts, count, w=kept.w, g=d_low, kept=kept, route=route, pack=pack, depth=depth)
    d_sent = send_rows(plan[1], d_low, experts, capacity)
    got = expert_call(plan, experts, count, w=kept.w, g=d_sent, kept=kept, route=route, depth=depth)
    got.result = return_rows(plan[1], got.result, experts, capacity).astype(BF16)
    got.summed = scatter_all(pack)
    return got


def experts_both(w, own, plan, token_rows, d_low, route, experts, capacity, depth):
    count = experts * capacity
    if experts == CUTS:
        return expert_call(plan, experts, count, own=own, x=token_rows, g=d_low, route=route, depth=depth)
    rows = send_rows(plan[1], token_rows, experts, capacity)
    d_sent = send_rows(plan[1], d_low, experts, capacity)
    got = expert_call(plan, experts, count, w=w, x=rows, g=d_sent, route=route, depth=depth)
    got.result = return_rows(plan[1], got.result, experts, capacity).astype(BF16)
    return got


def project_part(m, hosted):
    r = m.refs
    rows, w = r.n_s, r.w_s
    tokens = r.x.shape[0]
    peers = rows.shape[0] // tokens
    shard = w.shape[1] // peers
    c, t = m.c, m.t
    ready = m.greet([m.x_peer, m.y_peer] + ([m.sibling] if hosted else []))
    at = lambda index: pl.ds(pl.multiple_of(index * shard, shard), shard)
    first_load = m.local(r.x, rows.at[pl.ds(0, tokens)])
    loads = []
    if hosted:
        for i in range(4):
            loads.append(m.local(attention_rows(r, 0, i), w.at[i, at(t)]))
    else:
        for i in range(4):
            for j in range(peers):
                piece = r.w.at[i // 2, j, r.w.shape[2] - 1, pl.ds(i % 2 * shard, shard)]
                loads.append(m.local(piece, w.at[i, pl.ds(j * shard, shard)]))
    ready()
    half = tokens // 2
    m.need(first_load)
    cut = lambda j, part: pl.ds(j * tokens + part * half, half)

    def send(j, part, to, device):
        return m.remote(rows.at[cut(j, part)], rows.at[cut(to, part)], device)

    first, second, swaps, kept = {}, [], [], []
    if hosted:
        m.need(*loads)
        for h in range(2):
            mine = w.at[2 * c + h, at(t)]
            first[1, h] = m.remote(mine, mine, m.x_peer)
            first[2, h] = m.remote(mine, mine, m.y_peer)
    a_low, b_high = send(0, 0, 1, m.x_peer), send(0, 1, 2, m.y_peer)
    if hosted:
        for h in range(2):
            for k, onward, part in ((1, m.y_peer, 0), (2, m.x_peer, 1)):
                m.arrived(first[k, h])
                start = pl.multiple_of(xor_peer(t, k) * shard + part * (shard // 2), shard // 2)
                piece = w.at[2 * c + h, pl.ds(start, shard // 2)]
                second.append(m.remote(piece, piece, onward))
                whole = w.at[2 * c + h, at(xor_peer(t, k))]
                swaps.append(m.remote(whole, whole, m.sibling))
    a_high, b_low = send(0, 1, 1, m.x_peer), send(0, 0, 2, m.y_peer)
    m.arrived(a_low)
    c_low = send(1, 0, 3, m.y_peer)
    m.arrived(b_high)
    c_high = send(2, 1, 3, m.x_peer)
    if hosted:
        m.arrived(*second)
        for h in range(2):
            whole = w.at[2 * c + h, at(xor_peer(t, 3))]
            swaps.append(m.remote(whole, whole, m.sibling))
        m.arrived(*swaps)
    else:
        m.need(*loads)
    for i in range(4):
        kept.append(m.local(w.at[i], r.w_all.at[i]))

    def keys_values(start, size):
        here = pl.ds(start, size)
        x = rows[here, :]
        for i, near, far in ((1, r.k_s, r.k), (2, r.v_s, r.v)):
            near[here, :] = dot_nt(x, w[i]).astype(BF16)
            kept.append(m.local(near.at[here], far.at[here]))

    r.q_s[...] = dot_nt(rows[pl.ds(0, tokens), :], w[0]).astype(BF16)
    kept.append(m.local(r.q_s, r.q))
    keys_values(0, tokens)
    m.arrived(a_high)
    keys_values(tokens, tokens)
    m.arrived(b_low)
    keys_values(2 * tokens, tokens)
    r.turned_s[...] = w[3].T
    kept.append(m.local(r.turned_s, r.out_turned))
    m.arrived(c_low)
    keys_values(3 * tokens, half)
    m.arrived(c_high)
    keys_values(3 * tokens + half, half)
    kept.append(m.local(rows, r.n))
    m.finish()
    m.need(*kept)


def project(x, w, hosted, peers):
    tokens, width = x.shape
    every = peers * tokens
    outs = dict(
        q=(low_shape(tokens, width), ANY), k=(low_shape(every, width), ANY), v=(low_shape(every, width), ANY),
        n=(low_shape(every, width), ANY), w_all=(low_shape(4, width, width), ANY),
        out_turned=(low_shape(width, width), ANY),
    )
    scratch = dict(
        n_s=low_vmem(every, width), w_s=low_vmem(4, width, width), q_s=low_vmem(tokens, width),
        k_s=low_vmem(every, width), v_s=low_vmem(every, width), turned_s=low_vmem(width, width),
    )
    given = dict(w_qkv=(w[0], ANY), w_out=(w[1], ANY)) if hosted else dict(w=(w, ANY))
    return run_kernel(
        project_part, dict(x=(x, ANY), **given), outs, scratch, 6 + hosted, 9 * tokens * width * width, 40, 24, hosted=hosted
    )


def project_back_part(m, full, returns):
    r = m.refs
    tokens, width = r.dq_s.shape
    peers = r.dk_s.shape[0] // tokens
    shard = width // peers
    c, z = m.c, m.z
    local, remote, need, arrived = m.local, m.remote, m.need, m.arrived
    ready = m.greet([m.x_peer, m.y_peer] + ([m.sibling] if full else []) + (m.z_peers if full or returns else []))
    rows_of = lambda j: pl.ds(j * tokens, tokens)
    w = r.w_s
    weights_in = {i: local(r.w.at[i], w.at[i]) for i in (1, 2)}
    parts_in = {}
    for j in (3, 1, 2, 0):
        parts_in[j] = [local(a.at[rows_of(j)], b.at[rows_of(j)]) for a, b in ((r.dk, r.dk_s), (r.dv, r.dv_s))]
    above_in = local(r.above, r.above_s) if full else None
    rest_in = [local(a, b) for a, b in ((r.n, r.n_s), (r.dq, r.dq_s), (r.heads, r.heads_s), (r.d_att, r.d_att_s))]
    weights_in[0] = local(r.w.at[0], w.at[0])
    swaps_in = []
    if full:
        e_scatter = ExpertScatter(m, r.e0, r.e_own, r.e_keep, r.e_in)
        e_scatter.flow = []
        e_loads = [local(a.at[n], r.e_in.at[2 * n + i]) for n in range(2) for i, a in enumerate((r.from_x, r.from_y))]
        e_loads += e_scatter.load()
        swaps_in = [local(r.e1.at[i], r.e_s.at[i, 1, c]) for i in range(2)]
    ready()
    tops, ends = pl.ds(0, tokens // 2), pl.ds(tokens // 2, tokens // 2)

    def partial(j):
        at = rows_of(j)
        return dot(r.dk_s[at, :], w[1]) + dot(r.dv_s[at, :], w[2])

    over_x, over_y = {}, {}

    stages = {1: r.p1, 2: r.p2, 3: r.p3}

    def rows_part(*which):
        need(weights_in[1], weights_in[2])
        for j in which:
            need(*parts_in[j])
            stages[j][...] = partial(j).astype(BF16)

    def rows_send(*which):
        for j in which:
            if j != 2:
                over_x[j] = remote(stages[j].at[tops], r.row_in.at[j // 2], m.x_peer)
            if j != 1:
                over_y[j] = remote(stages[j].at[ends], r.row_in.at[2 + j // 3], m.y_peer)

    def rows_turn():
        arrived(over_x[3])
        r.p2[tops, :] = add_low(r.p2.at[tops], r.row_in.at[1]).astype(BF16)
        over_y[1] = remote(r.p2.at[tops], r.row_in.at[4], m.y_peer)
        arrived(over_y[3])
        r.p1[ends, :] = add_low(r.p1.at[ends], r.row_in.at[3]).astype(BF16)
        over_x[2] = remote(r.p1.at[ends], r.row_in.at[5], m.x_peer)

    def rows_own():
        need(*parts_in[0], weights_in[0], rest_in[1])
        r.dn[...] = partial(0) + dot(r.dq_s[...], w[0])

    def rows_end():
        for copy, slot, cut in ((over_x[1], 0, tops), (over_y[2], 2, ends), (over_y[1], 4, tops), (over_x[2], 5, ends)):
            arrived(copy)
            r.dn[cut, :] += r.row_in[slot].astype(F32)

    pack = r.pack_s
    part = lambda i: pl.ds(i % 2 * shard, shard)

    def weight_grad(i):
        need(*rest_in, weights_in[0], *[p for j in (3, 1, 2, 0) for p in parts_in[j]])
        if i == 0:
            g = dot_tn(r.dq_s[...], r.n_s[rows_of(0), :])
        elif i == 3:
            g = dot_tn(r.heads_s[...], r.d_att_s[...])
        else:
            g = dot_tn((r.dk_s if i == 1 else r.dv_s)[...], r.n_s[...])
        low = g.astype(BF16)
        for j in range(peers):
            pack[i // 2 * peers + j, part(i), :] = low[j * shard : (j + 1) * shard]
        return jnp.sum(g * w[i].astype(F32), axis=0, keepdims=True) if i < 3 else 0.0

    if not full:
        copies = {}
        if returns:
            size = r.out.shape[0] // CUTS
            out_in = local(r.out.at[pl.ds(0, size)], r.out_s)
            for k in (2, 3, 1):
                copies[k] = remote(r.out.at[pl.ds(k * size, size)], r.back.at[k - 1], m.z_peers[k - 1])
        for j in (3, 1, 2):
            rows_part(j)
            rows_send(j)
        total = weight_grad(1)
        rows_turn()
        rows_own()
        total = total + weight_grad(2) + weight_grad(0) + weight_grad(3)
        r.att[...] = jnp.broadcast_to(total, r.att.shape)
        saved = local(pack, r.pack)
        if returns:
            need(out_in)
            r.result[...] = combine(m, r.slot_row, r.out_s, copies, r.back, size)
        rows_end()
        m.finish()
        need(saved)
        return

    mini = shard // 4
    at_z = lambda h, index: pl.ds(pl.multiple_of(h * shard + index * mini, mini), mini)
    both, z_in = r.both, r.z_in

    def z_out(source, layer, h):
        return [remote(source.at[at_z(h, xor_peer(z, k))], z_in.at[layer * 2 + h, k - 1], m.z_peers[k - 1]) for k in (1, 2, 3)]

    def z_sum(source, copies, layer, h):
        arrived(*copies)
        here = both.at[layer, c, at_z(h, z)]
        both[layer, c, at_z(h, z), :] = add_low(
            source.at[at_z(h, z)], *[z_in.at[layer * 2 + h, k] for k in range(3)]
        ).astype(BF16)
        return [remote(here, here, device) for device in m.z_peers]

    def core_out(copies, layer, h):
        arrived(*copies)
        here = both.at[layer, c, pl.ds(h * shard, shard)]
        return remote(here, here, m.sibling)

    scatter = Scatter(m, pack, r.core_in, r.g_in, r.piece)
    need(above_in)
    above = [z_out(r.above_s, 1, h) for h in range(2)]
    rows_part(3)
    rows_send(3)
    total = weight_grad(3) + weight_grad(1)
    scatter.swap(1)
    need(*e_loads)
    e_scatter.turn()
    total = total + weight_grad(0) + weight_grad(2)
    scatter.swap(0)
    small_s, small_r = r.small_s, r.small_r
    row = lax.broadcasted_iota(jnp.int32, r.small.shape, 0)
    att_row = r.small_in.shape[0] // 2 - 1
    small_s[0] = jnp.where(row == att_row, total, r.small_in[...])
    small_1 = remote(small_s.at[0], small_r.at[0], m.sibling)
    above = [z_sum(r.above_s, above[h], 1, h) for h in range(2)]
    arrived(small_1)
    small_s[1] = small_s[0] + small_r[0]
    small_2 = [remote(small_s.at[1], small_r.at[k], m.z_peers[k - 1]) for k in (1, 2, 3)]
    scatter.out(1)
    scatter.out(0)
    rows_part(1)
    rows_part(2)
    arrived(*small_2)
    small_s[2] = small_s[1] + small_r[1] + small_r[2] + small_r[3]
    scatter.turn(1)
    small_3 = remote(small_s.at[2], small_r.at[4], m.x_peer)
    scatter.turn(0)
    rows_send(1, 2)
    above = [core_out(above[h], 1, h) for h in range(2)]
    need(*swaps_in)
    e_copies = [remote(r.e_s.at[i, 1, c], r.e_s.at[i, 1, c], m.sibling) for i in range(2)]
    rows_own()
    scatter.end(1)
    piece_1 = z_out(r.piece, 0, 1)
    scatter.end(0)
    piece_0 = z_out(r.piece, 0, 0)
    arrived(small_3)
    small_s[3] = small_s[2] + small_r[4]
    rows_turn()
    small_4 = remote(small_s.at[3], small_r.at[5], m.y_peer)
    piece_1 = z_sum(r.piece, piece_1, 0, 1)
    piece_0 = z_sum(r.piece, piece_0, 0, 0)
    e_scatter.end()
    for i in range(2):
        r.e_s[i, 0, c] = r.e_own[i]
        e_copies.append(remote(r.e_s.at[i, 0, c], r.e_s.at[i, 0, c], m.sibling))
    arrived(*e_copies)
    saved = [local(r.e_s.at[0], r.e_up), local(r.e_s.at[1], r.e_down)]
    piece_1 = core_out(piece_1, 0, 1)
    piece_0 = core_out(piece_0, 0, 0)
    rows_end()
    arrived(*above, piece_1, piece_0)
    for l in range(2):
        saved += [
            local(both.at[l, 0], r.g_mix.at[l, pl.ds(0, 2 * shard)]),
            local(both.at[l, 1, pl.ds(0, shard)], r.g_mix.at[l, pl.ds(2 * shard, shard)]),
            local(both.at[l, 1, pl.ds(shard, shard)], r.g_out.at[l]),
        ]
    arrived(small_4)
    r.small[...] = small_s[3] + small_r[5]
    m.finish()
    need(*saved)


def project_back(w, dq, dk, dv, normed_all, heads, d_att, above=None, small=None, swaps=None, out=None, slots=None):
    full, returns = above is not None, out is not None
    tokens, width = dq.shape
    rows = dk.shape[0]
    half = width // 2
    peers = rows // tokens
    shape = jax.ShapeDtypeStruct
    ins = dict(
        w=(w, ANY), dq=(dq, ANY), dk=(dk, ANY), dv=(dv, ANY), n=(normed_all, ANY), heads=(heads, ANY), d_att=(d_att, ANY),
    )
    outs = dict(dn=(shape((tokens, width), F32), VMEM))
    some, every = low_vmem(tokens, width), low_vmem(rows, width)
    scratch = dict(
        w_s=low_vmem(3, width, width), dq_s=some, dk_s=every, dv_s=every, n_s=every, heads_s=some, d_att_s=some,
        p1=some, p2=some, p3=some, row_in=low_vmem(6, tokens // 2, width),
    )
    if full:
        ins.update(above=(above, ANY), small_in=(small, VMEM), e0=(swaps[0], ANY), e1=(swaps[1], ANY), from_x=(swaps[2], ANY), from_y=(swaps[3], ANY))
        twice = (low_shape(2, 2, half, width), ANY)
        outs.update(
            g_mix=(low_shape(2, 3 * width // 4, width), ANY), g_out=(low_shape(2, width // 4, width), ANY), e_up=twice, e_down=twice,
            small=(shape(small.shape, F32), VMEM),
        )
        scratch.update(
            scatter_scratch(peers, half, width), **expert_scatter_scratch(half, width), above_s=low_vmem(half, width), e_s=low_vmem(2, 2, 2, half, width),
            small_s=pltpu.VMEM((4,) + small.shape, F32), small_r=pltpu.VMEM((6,) + small.shape, F32),
            z_in=low_vmem(4, 3, half // 8, width), both=low_vmem(2, 2, half, width),
        )
    else:
        outs.update(pack=(low_shape(2 * peers, half, width), ANY), att=(shape((8, width), F32), VMEM))
        scratch.update(pack_s=low_vmem(2 * peers, half, width))
        if returns:
            ins.update(out=(out, ANY), slot_row=(slots[None, :], VMEM))
            outs.update(result=(low_shape(tokens, width), VMEM))
            size = out.shape[0] // CUTS
            scratch.update(out_s=low_vmem(size, width), back=low_vmem(3, size, width))
    return run_kernel(
        project_back_part, ins, outs, scratch, 4 + full, 4 * rows * width * width, 40, 96, full=full, returns=returns
    )


def inverse_rms(stream):
    return lax.rsqrt(jnp.mean(stream * stream, axis=-1, keepdims=True) + EPS)


def norm_backward(upstream, stream, inverse, gain):
    weighted = upstream * gain
    inner = jnp.mean(weighted * stream, axis=-1, keepdims=True)
    return inverse * weighted - stream * (inverse * inverse * inverse) * inner


def path_table(segment_ids, path_pos, parent_ids, peers):
    front = jnp.arange(BLK, dtype=jnp.int32) == 0
    head = lambda v: jnp.sum(jnp.where(front, v.reshape(-1, BLK), 0), axis=1).reshape(peers, -1)
    segment, position = head(segment_ids), head(path_pos)
    t = lax.axis_index(TENSOR)
    order = jnp.arange(peers, dtype=jnp.int32) ^ t
    match = order[:, None] == jnp.arange(peers, dtype=jnp.int32)[None, :]
    pick = lambda v: jnp.sum(jnp.where(match[:, :, None], v[None], 0), axis=1)
    segment, position = pick(segment), pick(position)
    place = jnp.where(segment == 0, position // BLK, segment + (TRUNK - 1))
    seg, pos, own = segment[0], position[0], place[0]
    names = jnp.arange(parent_ids.shape[-1], dtype=jnp.int32)
    parent = jnp.sum(jnp.where(seg[:, None] == names[None, :], parent_ids[0][None], 0), axis=1)
    leaf = (seg > 0) & (parent > 0)
    parent_place = jnp.where(leaf, parent + (TRUNK - 1), own)
    base_own = jnp.where(seg > 0, pos, BIG)
    base_parent = jnp.where(leaf, TRUNK * BLK, BIG)
    mine = jnp.stack([pos, own, parent_place, base_own, base_parent], axis=1)
    return jnp.concatenate([place.reshape(-1), mine.reshape(-1)]).astype(jnp.int32)


def dispatch_plans(routes, experts, capacity):
    layers, count = routes.shape
    names = jnp.arange(experts, dtype=jnp.int32)
    chosen = routes[:, :, None] == names[None, None, :]
    index = jnp.arange(count, dtype=jnp.int32)
    before = (index[None, :] < index[:, None]).astype(BF16)
    every = jnp.concatenate([chosen[d] for d in range(layers)], axis=1)
    ranks = jnp.where(every, dot(before, every.astype(BF16)), 0.0)
    plans = []
    for d in range(layers):
        rank = jnp.sum(ranks[:, d * experts : (d + 1) * experts], axis=1).astype(jnp.int32)
        to = routes[d] ^ lax.axis_index(EXPERT) if experts == CUTS else routes[d]
        slot = to * capacity + rank
        table = slot[None, :] == jnp.arange(experts * capacity, dtype=jnp.int32)[:, None]
        plans.append((chosen[d], (slot, table.astype(BF16))))
    return plans


def send_rows(table, rows, experts, capacity):
    chunks = [
        dot(table[k * capacity : (k + 1) * capacity], rows).astype(BF16) for k in range(experts)
    ]
    return jnp.concatenate(exchange(chunks), axis=0)


def return_rows(table, results, experts, capacity):
    chunks = exchange([results[k * capacity : (k + 1) * capacity] for k in range(experts)])
    return dot_tn(table, jnp.concatenate(chunks, axis=0))


def own_half(x):
    half = x.shape[0] // 2
    return lax.dynamic_slice_in_dim(x, lax.axis_index(DP) * half, half, 0)


def gather_all(x):
    out = lax.all_gather(x, (DP, TENSOR), axis=0)
    return out.reshape((lax.axis_size(DP), lax.axis_size(TENSOR)) + x.shape)


def scatter_all(x):
    flat = x.reshape((-1,) + x.shape[2:])
    return lax.psum_scatter(flat, (DP, TENSOR), scatter_dimension=0, tiled=True)[0]


def pack_attention(w_mix, w_proj):
    width = w_mix.shape[0]
    return jnp.concatenate([w_mix.transpose(1, 2, 0).reshape(-1, width), w_proj], axis=0)


def pack_experts(w_up, w_back):
    return jnp.stack([own_half(w_up), own_half(w_back)])


def swap_cores(half):
    return lax.all_gather(half, DP, axis=0)


def body(
    hidden_in, route_ids, segment_ids, path_pos, parent_ids, norm_att, w_qkv, w_out, norm_ffn, w_route, w_in, w_down, cotangent,
):
    depth_total = w_qkv.shape[0]
    tokens, width = hidden_in.shape
    experts = w_route.shape[-1]
    capacity = 3 * tokens // (2 * experts)
    peers = lax.axis_size(TENSOR)
    shard = width // peers
    table = path_table(segment_ids, path_pos, parent_ids, peers)
    plans = dispatch_plans(route_ids[:, :, 0], experts, capacity)
    routes = jnp.pad(w_route, ((0, 0), (0, 0), (0, BLK - experts)))
    cotangent = cotangent.astype(F32)

    stream = hidden_in.astype(F32)
    kept = []
    turned = (w_qkv.transpose(0, 2, 3, 1), w_out)
    own = (w_in, w_down)
    weights = None
    for depth in range(depth_total):
        gain_att, gain_ffn = norm_att[depth].astype(F32), norm_ffn[depth].astype(F32)
        chosen, plan = plans[depth]
        last = depth + 1 == depth_total
        inverse_att = inverse_rms(stream)
        normed = (stream * inverse_att * gain_att).astype(BF16)
        proj = project(normed, turned if depth == 0 else weights, depth == 0, peers)
        w_here = None if experts == CUTS else gather_all(pack_experts(w_in[depth, 0], w_down[depth, 0]))
        heads, lse = attend(table, proj.q, proj.k, proj.v)
        after_att = stream + dot(heads, proj.w_all[3])
        inverse_ffn = inverse_rms(after_att)
        token_rows = (after_att * inverse_ffn * gain_ffn).astype(BF16)
        router = jax.nn.softmax(dot(token_rows, w_route[depth]), axis=-1)
        gate = jnp.sum(jnp.where(chosen, router, 0.0), axis=1, keepdims=True)
        if last:
            d_low = (gate * cotangent).astype(BF16)
            held = experts_both(w_here, own, plan, token_rows, d_low, routes, experts, capacity, depth)
            if experts != CUTS:
                back = return_rows(plan[1], held.out, experts, capacity).astype(BF16)
        else:
            back, held = experts_forward(plan, token_rows, experts, capacity, w_here, own, turned, depth)
            if experts == CUTS:
                weights = held.next_all.reshape((2, peers, 1) + held.next_all.shape[1:])
            else:
                weights = gather_all(own_half(pack_attention(w_qkv[depth + 1], w_out[depth + 1])))[:, :, None]
        kept.append((stream, inverse_att, proj, heads, lse, after_att, inverse_ffn, gate, held))
        if not last:
            stream = after_att + gate * back.astype(F32)

    upstream = cotangent
    grads_e, grads_a, smalls = [None] * depth_total, [None] * depth_total, [None] * depth_total
    above = None
    for depth in reversed(range(depth_total)):
        stream, inverse_att, proj, heads, lse, after_att, inverse_ffn, gate, held = kept[depth]
        gain_att, gain_ffn = norm_att[depth].astype(F32), norm_ffn[depth].astype(F32)
        chosen, plan = plans[depth]
        last = depth + 1 == depth_total
        if not last:
            d_low = (gate * upstream).astype(BF16)
            held = experts_backward(plan, d_low, held, routes, experts, capacity, above, depth)
            above = held.summed
        dx1 = upstream + norm_backward(held.result.astype(F32), after_att, inverse_ffn, gain_ffn)
        d_att = dx1.astype(BF16)
        d_heads = dot(d_att, proj.out_turned).astype(BF16)
        dq, dk, dv = attend_back(table, proj.q, proj.k, proj.v, d_heads, heads, lse)
        args = (proj.w_all, dq, dk, dv, proj.n, heads, d_att)
        if depth == 0 and experts == CUTS:
            swaps = (held.grads, held.e_summed, xperm(held.to_x, TENSOR, 1), xperm(held.to_y, TENSOR, 2))
            part = jnp.concatenate([held.small, smalls[1]], axis=0)
            got = project_back(*args, above=above, small=part, swaps=swaps)
            grads_e = (got.e_up, got.e_down)
            grad_mix, grad_out = got.g_mix.astype(F32), got.g_out.astype(F32)
            small = got.small.reshape(depth_total, -1, width)
        else:
            if last and experts == CUTS:
                got = project_back(*args, out=held.out, slots=plan[0])
                back = got.result
            else:
                got = project_back(*args)
            if last:
                hidden_out = (after_att + gate * back.astype(F32)).astype(BF16)
            if above is not None:
                grads_a[depth + 1] = swap_cores(lax.psum(above, EXPERT))
            above = got.pack.reshape((2, peers) + got.pack.shape[1:])
            if experts == CUTS:
                above = (got.pack, held.grads)
            else:
                grads_e[depth] = scatter_all(after(held.grads, got.dn))
            line = lax.broadcasted_iota(jnp.int32, held.small.shape, 0)
            smalls[depth] = jnp.where(line == held.small.shape[0] - 1, got.att[:1], held.small)
            if depth == 0:
                grads_a[0] = swap_cores(lax.psum(scatter_all(above), EXPERT))
                small = sum_small(jnp.stack(smalls))
                grads_e = jnp.stack([swap_cores(g) for g in grads_e]).transpose(2, 0, 1, 3, 4)
                grads_a = jnp.stack(grads_a).reshape(depth_total, width, width).astype(F32)
                grad_mix, grad_out = grads_a[:, : 3 * shard], grads_a[:, 3 * shard :]
        upstream = dx1 + norm_backward(got.dn, stream, inverse_att, gain_att)
    grad_up, grad_down = [g.reshape(depth_total, 1, width, width).astype(F32) for g in grads_e]
    grad_mix = grad_mix.reshape(depth_total, 3, shard, width).transpose(0, 3, 1, 2)
    grad_route = small[:, :experts].transpose(0, 2, 1)
    grad_ffn = small[:, experts] / norm_ffn.astype(F32)
    grad_att = small[:, -1] / norm_att.astype(F32)
    return (hidden_out, upstream, grad_att, grad_mix, grad_out, grad_ffn, grad_route, grad_up, grad_down)


def solution(mesh):
    in_specs = (
        P((DP, EXPERT, TENSOR), None),
        P(None, (DP, EXPERT, TENSOR), None),
        P((DP, EXPERT)),
        P((DP, EXPERT)),
        P((DP, EXPERT), None),
        P(),
        P(None, None, None, TENSOR),
        P(None, TENSOR, None),
        P(),
        P(),
        P(None, EXPERT, None, TENSOR),
        P(None, EXPERT, TENSOR, None),
        P((DP, EXPERT, TENSOR), None),
    )
    out_specs = (
        P((DP, EXPERT, TENSOR), None),
        P((DP, EXPERT, TENSOR), None),
        P(),
        P(None, None, None, TENSOR),
        P(None, TENSOR, None),
        P(),
        P(),
        P(None, EXPERT, None, TENSOR),
        P(None, EXPERT, TENSOR, None),
    )
    return jax.shard_map(body, mesh=mesh, in_specs=in_specs, out_specs=out_specs, check_vma=False)
```
